128 devices in a mesh: group: 4 (over y_lo, core), span: 32 (over x, z, y_hi).
Axes of the slice: x: 4, y: 4 (y_hi: 2, y_lo: 2; y = y_hi * 2 + y_lo), z: 4, core: 2. Of those that a mesh axis runs over, the one named last changes fastest.
Arguments:
- tokens: bfloat16 [16384, 1024], P(('group', 'span')), may hold values from -32 to 32
- query_weight: bfloat16 [1024, 1024], replicated, may hold values from -0.1875 to 0.1875
- key_weight: bfloat16 [1024, 1024], replicated, may hold values from -0.1875 to 0.1875
- value_weight: bfloat16 [1024, 1024], replicated, may hold values from -0.1875 to 0.1875
- log_decay: float32 [16, 16384], P(None, ('group', 'span')), may hold values from -0.6 to 0
- neighbour_blocks: int32 [128, 4], P(('group', 'span')), may hold values from 0 to 127, as said below
- cotangent: bfloat16 [16384, 1024], P(('group', 'span')), may hold values from -6 to 6
Outputs:
- layer_out: bfloat16 [16384, 1024], P(('group', 'span'))
- tokens_grad: bfloat16 [16384, 1024], P(('group', 'span'))
- query_grad: bfloat16 [1024, 1024], replicated
- key_grad: bfloat16 [1024, 1024], replicated
- value_grad: bfloat16 [1024, 1024], replicated
The draws below stay inside these ranges and needn't reach their ends.
Inputs may be any that keep to these rules, and one draw needn't show every extreme that they name: `neighbour_blocks`: row b is [b, b - 1, b - 1, b - 1]; any entry that would fall before block 0 is block 0.
All inputs are finite; a program needn't handle non-finite values.
Results may differ from the reference program's by a relative error of at most 0.0077.
Values may be sent and summed in bfloat16 or wider, within the bound.
No kernel may reach another device: no remote copies, remote signals or barrier semaphores. Data moves between devices by JAX's collectives and lax.ppermute only.
A program may use at most 192 MiB of HBM per device.

```python
import math
import jax
import jax.numpy as jnp
from jax import lax

D = 1024
ATTENDER_NUMBER = 16
DH = 64
TOK_DEV = 128
BLK = 128
NB = 4
FRAME_ELEMENTS = 16384


def draw_tokens(key, part):
    base_vals = jnp.clip(jax.random.normal(jax.random.fold_in(key, 1), (FRAME_ELEMENTS, D), jnp.float32), -4.5, 4.5)
    return base_vals.astype(jnp.bfloat16)


def attention_pair(key):
    first_matrix = jnp.clip(jax.random.normal(jax.random.fold_in(key, 11), (D, D), jnp.float32), -6.0, 6.0) / math.sqrt(D)
    other_matrix = jnp.clip(jax.random.normal(jax.random.fold_in(key, 12), (D, D), jnp.float32), -6.0, 6.0) / math.sqrt(D)
    second_matrix = other_matrix
    return (first_matrix, second_matrix)


def draw_query_weight(key, part):
    return attention_pair(key)[0].astype(jnp.bfloat16)


def draw_key_weight(key, part):
    return attention_pair(key)[1].astype(jnp.bfloat16)


def draw_log_decay(key, part):
    lookup_fragments = jax.random.split(key, 6)
    fast_share = 0.5
    seg_count = FRAME_ELEMENTS // TOK_DEV
    is_fast = jax.random.uniform(lookup_fragments[0], (ATTENDER_NUMBER, 1, 1), jnp.float32) < fast_share
    fast_rate = jnp.exp(jax.random.uniform(lookup_fragments[1], (ATTENDER_NUMBER, 1, 1), jnp.float32, math.log(1.0 / 50.0), math.log(1.0 / 30.0)))
    slow_rate = jnp.exp(jax.random.uniform(lookup_fragments[2], (ATTENDER_NUMBER, 1, 1), jnp.float32, math.log(0.1), math.log(0.4))) / FRAME_ELEMENTS
    device_factor = jnp.exp(jax.random.uniform(lookup_fragments[3], (ATTENDER_NUMBER, seg_count, 1), jnp.float32, math.log(0.5), math.log(2.0)))
    default_forget_factors = -jnp.broadcast_to(jnp.where(is_fast, fast_rate, slow_rate) * device_factor, (ATTENDER_NUMBER, seg_count, TOK_DEV)).reshape(ATTENDER_NUMBER, FRAME_ELEMENTS)
    pulse_volley_locations = jax.random.randint(lookup_fragments[4], (2,), 0, FRAME_ELEMENTS)
    pulse_volley_extent = jax.random.uniform(lookup_fragments[5], (ATTENDER_NUMBER, 2), jnp.float32, 0.22, 0.5)
    pairing_tallies = (jnp.arange(FRAME_ELEMENTS)[None, :, None] == pulse_volley_locations[None, None, :]).astype(jnp.float32)
    return default_forget_factors - jnp.sum(pairing_tallies * pulse_volley_extent[:, None, :], axis=2)


def draw_neighbour_blocks(key, part):
    block_total = FRAME_ELEMENTS // BLK
    per_dev = TOK_DEV // BLK
    own_block = jnp.arange(block_total, dtype=jnp.int32)[:, None]
    reach_back = jax.random.randint(key, (block_total, NB - 2), 1, per_dev + 1)
    far_block = jnp.maximum(own_block - per_dev, 0)
    near_block = jnp.maximum(own_block - reach_back, 0)
    return jnp.concatenate([own_block, far_block, near_block], axis=1).astype(jnp.int32)


def steps_of(stream_key, shape, cuts, least, largest):
    level, own = 1.0, jax.random.fold_in(stream_key, 6)
    for axis_at, shards_of in cuts:
        heights = jnp.exp(jax.random.uniform(jax.random.fold_in(own, axis_at), (shards_of,), jnp.float32, least / len(cuts), largest / len(cuts)))
        level = level * jnp.repeat(heights, shape[axis_at] // shards_of).reshape([-1 if axis == axis_at else 1 for axis in range(len(shape))])
    return level


def scatter_about(own_key, shape, width, most, pieces=(), kind=jnp.bfloat16):
    level = steps_of(own_key, shape, pieces, -0.22, 0.18) if pieces else 1.0
    drawn = jax.random.normal(own_key, shape, jnp.float32) * width * level
    return jnp.minimum(jnp.maximum(drawn, -most), most).astype(kind)


def setup_inputs(seed: int = 0) -> dict:
    arg_keys = jax.random.split(jax.random.key(seed), 8)
    tokens = draw_tokens(jax.random.fold_in(arg_keys[7], 71), 0)
    query_weight = draw_query_weight(jax.random.fold_in(arg_keys[7], 71), 0)
    key_weight = draw_key_weight(jax.random.fold_in(arg_keys[7], 71), 0)
    value_weight = scatter_about(arg_keys[3], (D, D), D ** -0.5, 0.1875)
    log_decay = draw_log_decay(jax.random.fold_in(arg_keys[7], 71), 0)
    neighbour_blocks = draw_neighbour_blocks(jax.random.fold_in(arg_keys[7], 71), 0)
    cotangent = scatter_about(arg_keys[6], (FRAME_ELEMENTS, D), 1.0, 6.0, ((0, 128),))
    return {"tokens": tokens, "query_weight": query_weight, "key_weight": key_weight, "value_weight": value_weight, "log_decay": log_decay, "neighbour_blocks": neighbour_blocks, "cotangent": cotangent}


def rounded(values):
    return lax.optimization_barrier(values.astype(jnp.bfloat16)).astype(jnp.float32)

def summarize(rate_seg, query, key, value, grad_out):
    row_count, feat_width = query.shape
    head_count = rate_seg.shape[0]
    head_size = feat_width // head_count
    lin_scale = 1.0 / (head_size * math.sqrt(row_count))
    running = jnp.cumsum(rate_seg, axis=1)
    seg_total = running[:, -1]
    fading = jnp.exp(seg_total[:, None] - running).T[:, :, None]
    growth = jnp.exp(running).T[:, :, None]
    q_heads = query.reshape(row_count, head_count, head_size).astype(jnp.float32)
    k_heads = key.reshape(row_count, head_count, head_size).astype(jnp.float32)
    v_heads = value.reshape(row_count, head_count, head_size).astype(jnp.float32)
    g_heads = grad_out.reshape(row_count, head_count, head_size).astype(jnp.float32)
    weighted = rounded(v_heads * fading)
    local_state = jnp.einsum('shd,she->hde', k_heads, weighted)
    scaled_grad = rounded(g_heads * growth)
    head_grad = lin_scale * jnp.einsum('thd,the->hde', q_heads, scaled_grad)
    return (seg_total, local_state, head_grad)

def segment_work(rate_seg, query, keyval, prev_keyval, grad_out, local_ids, state_in, later):
    row_count, feat_width = query.shape
    head_count = rate_seg.shape[0]
    head_size = feat_width // head_count
    blocks = row_count // BLK
    lin_scale = 1.0 / (head_size * math.sqrt(row_count))
    soft_scale = 1.0 / math.sqrt(head_size)
    running = jnp.cumsum(rate_seg, axis=1)
    seg_total = running[:, -1]
    growth = jnp.exp(running).T[:, :, None]
    fading = jnp.exp(seg_total[:, None] - running).T[:, :, None]
    places = jnp.arange(row_count, dtype=jnp.int32)
    is_lower = places[:, None] >= places[None, :]
    decay_mat = jnp.where(is_lower[None], jnp.exp(jnp.minimum(running[:, :, None] - running[:, None, :], 0.0)), 0.0)
    q_heads = query.reshape(row_count, head_count, head_size).astype(jnp.float32)
    k_heads = keyval[:, :feat_width].reshape(row_count, head_count, head_size).astype(jnp.float32)
    v_heads = keyval[:, feat_width:].reshape(row_count, head_count, head_size).astype(jnp.float32)
    g_heads = grad_out.reshape(row_count, head_count, head_size).astype(jnp.float32)
    intra_mat = rounded(jnp.einsum('thd,shd->hts', q_heads, k_heads) * decay_mat)
    state_bf = rounded(state_in)
    linear_out = jnp.einsum('hts,she->the', intra_mat, v_heads) + growth * jnp.einsum('thd,hde->the', q_heads, state_bf)
    extended = jnp.concatenate([prev_keyval, keyval], axis=0).reshape(2 * blocks, BLK, 2 * feat_width)
    picked = jnp.take(extended, local_ids, axis=0).reshape(blocks, NB * BLK, 2 * feat_width).astype(jnp.float32)
    near_key = picked[:, :, :feat_width].reshape(blocks, NB * BLK, head_count, head_size)
    near_val = picked[:, :, feat_width:].reshape(blocks, NB * BLK, head_count, head_size)
    q_blocks = q_heads.reshape(blocks, BLK, head_count, head_size)
    g_blocks = g_heads.reshape(blocks, BLK, head_count, head_size)
    logits = jnp.einsum('bthd,bshd->bhts', q_blocks, near_key) * soft_scale
    row_peak = lax.optimization_barrier(jnp.max(logits, axis=-1, keepdims=True))
    exp_terms = jnp.exp(logits - row_peak)
    soft_probs = exp_terms / lax.optimization_barrier(jnp.sum(exp_terms, axis=-1, keepdims=True))
    probs_bf = rounded(soft_probs)
    near_out = jnp.einsum('bhts,bshd->bthd', probs_bf, near_val).reshape(row_count, head_count, head_size)
    layer_out = (lin_scale * linear_out + near_out).reshape(row_count, feat_width).astype(jnp.bfloat16)
    prob_grad = jnp.einsum('bthd,bshd->bhts', g_blocks, near_val)
    inner_sum = lax.optimization_barrier(jnp.sum(soft_probs * prob_grad, axis=-1, keepdims=True))
    dlogit = rounded(soft_probs * (prob_grad - inner_sum) * soft_scale)
    dq_near = jnp.einsum('bhts,bshd->bthd', dlogit, near_key).reshape(row_count, head_count, head_size)
    dk_near = jnp.einsum('bhts,bthd->bshd', dlogit, q_blocks).reshape(blocks * NB, BLK, feat_width)
    dv_near = jnp.einsum('bhts,bthd->bshd', probs_bf, g_blocks).reshape(blocks * NB, BLK, feat_width)
    dpicked = jnp.concatenate([dk_near, dv_near], axis=-1)
    onehot = (local_ids.reshape(-1)[:, None] == jnp.arange(2 * blocks, dtype=jnp.int32)[None, :]).astype(jnp.float32)
    ext_grad = jnp.einsum('nm,ntc->mtc', onehot, dpicked, precision=lax.Precision.HIGHEST).reshape(2 * row_count, 2 * feat_width)
    back_mat = rounded(jnp.einsum('thd,shd->hts', g_heads, v_heads) * decay_mat)
    later_bf = rounded(later)
    dq_lin = lin_scale * (jnp.einsum('hts,shd->thd', back_mat, k_heads) + growth * jnp.einsum('the,hde->thd', g_heads, state_bf))
    dk_lin = lin_scale * jnp.einsum('hts,thd->shd', back_mat, q_heads) + fading * jnp.einsum('she,hde->shd', v_heads, later_bf)
    dv_lin = lin_scale * jnp.einsum('hts,the->she', intra_mat, g_heads) + fading * jnp.einsum('shd,hde->she', k_heads, later_bf)
    query_delta = (dq_lin + dq_near).reshape(row_count, feat_width).astype(jnp.bfloat16)
    lin_kv = jnp.concatenate([dk_lin.reshape(row_count, feat_width), dv_lin.reshape(row_count, feat_width)], axis=1)
    own_grad = (lin_kv + ext_grad[row_count:]).astype(jnp.bfloat16)
    prev_grad = ext_grad[:row_count].astype(jnp.bfloat16)
    return (layer_out, query_delta, own_grad, prev_grad)

def reference(tokens, query_weight, key_weight, value_weight, log_decay, neighbour_blocks, cotangent):
    query = jnp.dot(tokens, query_weight, preferred_element_type=jnp.float32).astype(jnp.bfloat16)
    key = jnp.dot(tokens, key_weight, preferred_element_type=jnp.float32).astype(jnp.bfloat16)
    value = jnp.dot(tokens, value_weight, preferred_element_type=jnp.float32).astype(jnp.bfloat16)
    keyval = jnp.concatenate([key, value], axis=1)
    seg_count = FRAME_ELEMENTS // TOK_DEV
    per_dev = TOK_DEV // BLK
    rate_segs = log_decay.reshape(ATTENDER_NUMBER, seg_count, TOK_DEV).transpose(1, 0, 2)
    q_segs = query.reshape(seg_count, TOK_DEV, D)
    k_segs = key.reshape(seg_count, TOK_DEV, D)
    v_segs = value.reshape(seg_count, TOK_DEV, D)
    kv_segs = keyval.reshape(seg_count, TOK_DEV, 2 * D)
    g_segs = cotangent.reshape(seg_count, TOK_DEV, D)

    def summary_entry(entry):
        return summarize(entry[0], entry[1], entry[2], entry[3], entry[4])
    totals, states, head_grads = lax.map(summary_entry, (rate_segs, q_segs, k_segs, v_segs, g_segs))

    def advance(running_state, entry):
        return (jnp.exp(entry[0])[:, None, None] * running_state + entry[1], running_state)
    zero_state = jnp.zeros((ATTENDER_NUMBER, DH, DH), jnp.float32)
    _, state_in = lax.scan(advance, zero_state, (totals, states))
    _, later = lax.scan(advance, zero_state, (totals, head_grads), reverse=True)
    padded = jnp.concatenate([jnp.zeros((TOK_DEV, 2 * D), jnp.bfloat16), keyval], axis=0)
    block_ids = neighbour_blocks.reshape(seg_count, per_dev, NB)

    def work_entry(entry):
        seg_index = entry[0]
        prev_keyval = lax.dynamic_slice_in_dim(padded, (seg_index * TOK_DEV).astype(jnp.int32), TOK_DEV, 0)
        local_ids = (entry[5] - (seg_index - 1) * per_dev).astype(jnp.int32)
        return segment_work(entry[1], entry[2], entry[3], prev_keyval, entry[4], local_ids, entry[6], entry[7])
    outs_seg, delta_seg, own_seg, prev_seg = lax.map(work_entry, (jnp.arange(seg_count, dtype=jnp.int32), rate_segs, q_segs, kv_segs, g_segs, block_ids, state_in, later))
    layer_out = outs_seg.reshape(FRAME_ELEMENTS, D)
    query_delta = delta_seg.reshape(FRAME_ELEMENTS, D)
    own_grad = own_seg.reshape(FRAME_ELEMENTS, 2 * D)
    next_grad = jnp.concatenate([prev_seg[1:], jnp.zeros_like(prev_seg[:1])], axis=0).reshape(FRAME_ELEMENTS, 2 * D)
    tokens_grad = jnp.dot(query_delta, query_weight.T, preferred_element_type=jnp.float32)
    tokens_grad = tokens_grad + jnp.dot(own_grad[:, :D], key_weight.T, preferred_element_type=jnp.float32)
    tokens_grad = tokens_grad + jnp.dot(own_grad[:, D:], value_weight.T, preferred_element_type=jnp.float32)
    tokens_grad = tokens_grad + jnp.dot(next_grad[:, :D], key_weight.T, preferred_element_type=jnp.float32)
    tokens_grad = tokens_grad + jnp.dot(next_grad[:, D:], value_weight.T, preferred_element_type=jnp.float32)
    grad_norm = 1.0 / math.sqrt(FRAME_ELEMENTS)
    query_grad = jnp.dot(tokens.T, query_delta, preferred_element_type=jnp.float32) * grad_norm
    key_grad = (jnp.dot(tokens.T, own_grad[:, :D], preferred_element_type=jnp.float32) + jnp.dot(tokens.T, next_grad[:, :D], preferred_element_type=jnp.float32)) * grad_norm
    value_grad = (jnp.dot(tokens.T, own_grad[:, D:], preferred_element_type=jnp.float32) + jnp.dot(tokens.T, next_grad[:, D:], preferred_element_type=jnp.float32)) * grad_norm
    return (layer_out, tokens_grad.astype(jnp.bfloat16), query_grad.astype(jnp.bfloat16), key_grad.astype(jnp.bfloat16), value_grad.astype(jnp.bfloat16))
```

```python
import functools
import math

import jax
import jax.numpy as jnp
from jax import lax
from jax.experimental import pallas as pl
from jax.experimental.pallas import tpu as pltpu
from jax.sharding import Mesh
from jax.sharding import PartitionSpec as P

BF = jnp.bfloat16
F32 = jnp.float32
AX = ("yl", "c", "x", "z", "yh")
NEAR8 = ("z", "yh")
FAR16 = ("yl", "c", "x")
PLANE = ("yl", "x", "z", "yh")
SEG = 128
PAIR = 128
DH = 64
DEVS = 128
VMEM = pltpu.VMEM
HIGH = lax.Precision.HIGHEST


def dot(a, b, ca, cb, precision=None):
    return lax.dot_general(
        a, b, (((ca,), (cb,)), ((), ())), precision=precision, preferred_element_type=F32
    )


def iota(shape, axis):
    return lax.broadcasted_iota(jnp.int32, shape, axis)


def params(mib):
    return pltpu.CompilerParams(vmem_limit_bytes=mib << 20)


def cost(flops, moved, trans=0):
    return pl.CostEstimate(flops=flops, bytes_accessed=moved, transcendentals=trans)


def project_kernel(lin_scale, tok, tok_col, wq, wk, wv, decay, cot, q_out, kv_out, run_out, runt_out, tokt_out, msg):
    step = pl.program_id(0)
    x = tok[...]
    q = dot(x, wq[...], 1, 0).astype(BF)
    k = dot(x, wk[...], 1, 0).astype(BF)
    v = dot(x, wv[...], 1, 0).astype(BF)
    q_out[...] = q
    kv_out[0] = k
    kv_out[1] = v
    tokt_out[...] = tok_col[...].T
    ld = decay[...]
    heads = ld.shape[0]
    lower = (iota((SEG, SEG), 0) >= iota((SEG, SEG), 1)).astype(F32)
    runt = dot(lower, ld, 1, 1, HIGH)
    runt_out[...] = runt

    @pl.when(step == 0)
    def _():
        run_out[...] = dot(ld, lower, 1, 1, HIGH)

    head_of = iota((SEG, PAIR), 1) // DH
    head_id = iota((SEG, heads), 1)
    rows = iota((8, PAIR), 0)
    for half in range(2):
        cols = slice(half * PAIR, (half + 1) * PAIR)
        first = (step * 2 + half) * 2
        c0 = jnp.sum(jnp.where(head_id == first, runt, 0.0), axis=1, keepdims=True)
        c1 = jnp.sum(jnp.where(head_id == first + 1, runt, 0.0), axis=1, keepdims=True)
        run = jnp.where(head_of == 0, c0, c1)
        total = run[SEG - 1 : SEG, :]
        weighted = (v[:, cols].astype(F32) * jnp.exp(total - run)).astype(BF)
        scaled = (cot[:, cols].astype(F32) * jnp.exp(run)).astype(BF)
        full_s = dot(k[:, cols], weighted, 0, 0)
        full_g = dot(q[:, cols], scaled, 0, 0) * lin_scale
        high = total.astype(BF).astype(F32)
        mid = (total - high).astype(BF).astype(F32)
        low = total - high - mid
        tail = jnp.where(rows == 0, high, jnp.where(rows == 1, mid, jnp.where(rows == 2, low, 0.0)))
        tail = jnp.broadcast_to(tail[None], (8, 8, PAIR))
        lanes = iota((DH, PAIR), 1) < DH
        for part, full in ((0, full_s), (1, full_g)):
            own = jnp.where(lanes, full[:DH], full[DH:]).reshape(8, 8, PAIR)
            both = jnp.concatenate([own, tail], axis=1).reshape(PAIR, PAIR)
            msg[part, half * PAIR : (half + 1) * PAIR, :] = both.astype(BF)


def project(tokens, wq, wk, wv, log_decay, cot, lin_scale):
    rows, width = tokens.shape
    heads = log_decay.shape[0]
    steps = width // 256
    col = pl.BlockSpec((rows, 256), lambda i: (0, i))
    weight = pl.BlockSpec((width, 256), lambda i: (0, i))
    return pl.pallas_call(
        functools.partial(project_kernel, lin_scale),
        grid=(steps,),
        in_specs=[
            pl.BlockSpec((rows, width), lambda i: (0, 0)),
            col,
            weight,
            weight,
            weight,
            pl.BlockSpec((heads, rows), lambda i: (0, 0)),
            col,
        ],
        out_specs=[
            col,
            pl.BlockSpec((2, rows, 256), lambda i: (0, 0, i)),
            pl.BlockSpec((heads, rows), lambda i: (0, 0)),
            pl.BlockSpec((rows, heads), lambda i: (0, 0)),
            pl.BlockSpec((256, rows), lambda i: (i, 0)),
            pl.BlockSpec((2, 2 * PAIR, PAIR), lambda i: (0, i, 0)),
        ],
        out_shape=[
            jax.ShapeDtypeStruct((rows, width), BF),
            jax.ShapeDtypeStruct((2, rows, width), BF),
            jax.ShapeDtypeStruct((heads, rows), F32),
            jax.ShapeDtypeStruct((rows, heads), F32),
            jax.ShapeDtypeStruct((width, rows), BF),
            jax.ShapeDtypeStruct((2, width, PAIR), BF),
        ],
        compiler_params=params(40),
        cost_estimate=cost(6 * rows * width * width, 6 * width * width + 12 * rows * width),
        name="project",
    )(tokens, tokens, wq, wk, wv, log_decay, cot)


def scan_kernel(place, got, out, xs, decays, states):
    both = got[...].astype(F32)
    xs[...] = both[:, :8, :]
    total = both[:, 8:9, :] + both[:, 9:10, :] + both[:, 10:11, :]
    decays[...] = jnp.broadcast_to(jnp.exp(total), decays.shape)
    backward = place[0] >= DEVS // 2

    def one(i, state):
        at = jnp.where(backward, DEVS - 1 - i, i)
        states[at] = state
        return decays[at] * state + xs[at]

    lax.fori_loop(0, DEVS, one, jnp.zeros((8, PAIR), F32), unroll=8)
    out[...] = states[...].reshape(DEVS * 8, PAIR).astype(BF)


def scan(place, got):
    whole = pl.BlockSpec(memory_space=VMEM)
    return pl.pallas_call(
        scan_kernel,
        in_specs=[pl.BlockSpec(memory_space=pltpu.SMEM), whole],
        out_specs=whole,
        out_shape=jax.ShapeDtypeStruct((DEVS * 8, PAIR), BF),
        scratch_shapes=[VMEM((DEVS, 8, PAIR), F32)] * 3,
        compiler_params=params(24),
        cost_estimate=cost(2 * DEVS * 8 * PAIR, 4 * DEVS * 16 * PAIR),
        name="scan",
    )(place, got)


def near_kernel(lin_scale, place, blocks, q_ref, kv, pkv, cot, run_rows, runt, out, dq_out, own, prev):
    pair = pl.program_id(0)
    soft_scale = 1.0 / math.sqrt(DH)
    n_own = jnp.int32(0)
    n_prev = jnp.int32(0)
    for j in range(blocks.shape[1]):
        n_own += (blocks[0, j] == place[0]).astype(jnp.int32)
        n_prev += (blocks[0, j] == place[0] - 1).astype(jnp.int32)
    is_own = iota((1, 2 * SEG), 1) < SEG
    times = jnp.where(is_own, n_own, n_prev)
    bias = jnp.where(times > 0, 0.0, -1e30)
    times = times.astype(F32)
    q = q_ref[...]
    g = cot[...]
    kk = jnp.concatenate([kv[0], pkv[0]], axis=0)
    vv = jnp.concatenate([kv[1], pkv[1]], axis=0)
    head_of = iota((SEG, PAIR), 1) // DH
    head_of2 = iota((2 * SEG, PAIR), 1) // DH
    lower = iota((SEG, SEG), 0) >= iota((SEG, SEG), 1)
    head_id = iota(runt.shape, 1)
    zero = jnp.zeros((), BF)
    res = []
    for i in range(2):
        mine = head_of == i
        col = jnp.sum(jnp.where(head_id == pair * 2 + i, runt[...], 0.0), axis=1, keepdims=True)
        row = run_rows[0, i : i + 1, :]
        dec = jnp.where(lower, jnp.exp(jnp.minimum(col - row, 0.0)), 0.0) * lin_scale
        scores = dot(jnp.where(mine, q, zero), kk, 1, 1)
        pgrad = dot(jnp.where(mine, g, zero), vv, 1, 1)
        logits = scores * soft_scale + bias
        peak = jnp.max(logits, axis=1, keepdims=True)
        terms = jnp.exp(logits - peak) * times
        probs = terms * (1.0 / jnp.sum(terms, axis=1, keepdims=True))
        inner = jnp.sum(probs * pgrad, axis=1, keepdims=True)
        dlog = probs * (pgrad - inner) * soft_scale
        a = jnp.concatenate(
            [probs[:, :SEG] + scores[:, :SEG] * dec, probs[:, SEG:]], axis=1
        ).astype(BF)
        b = jnp.concatenate([dlog[:, :SEG] + pgrad[:, :SEG] * dec, dlog[:, SEG:]], axis=1).astype(BF)
        res.append((dot(a, vv, 1, 0), dot(b, kk, 1, 0), dot(b, q, 0, 0), dot(a, g, 0, 0)))
    out[...] = jnp.where(head_of == 0, res[0][0], res[1][0])
    dq_out[...] = jnp.where(head_of == 0, res[0][1], res[1][1])
    for part in range(2):
        both = jnp.where(head_of2 == 0, res[0][2 + part], res[1][2 + part])
        own[part] = both[:SEG]
        prev[part] = both[SEG:].astype(BF)


def near(place, blocks, q, kv, pkv, cot, run, runt, lin_scale):
    rows, width = q.shape
    heads = run.shape[0]
    smem = pl.BlockSpec(memory_space=pltpu.SMEM)
    col = pl.BlockSpec((rows, PAIR), lambda i: (0, i))
    two = pl.BlockSpec((2, rows, PAIR), lambda i: (0, 0, i))
    return pl.pallas_call(
        functools.partial(near_kernel, lin_scale),
        grid=(width // PAIR,),
        in_specs=[
            smem,
            smem,
            col,
            two,
            two,
            col,
            pl.BlockSpec((1, 2, rows), lambda i: (i, 0, 0)),
            pl.BlockSpec((rows, heads), lambda i: (0, 0)),
        ],
        out_specs=[col, col, two, two],
        out_shape=[
            jax.ShapeDtypeStruct((rows, width), F32),
            jax.ShapeDtypeStruct((rows, width), F32),
            jax.ShapeDtypeStruct((2, rows, width), F32),
            jax.ShapeDtypeStruct((2, rows, width), BF),
        ],
        compiler_params=params(32),
        cost_estimate=cost(4000 * 1000 * 1000, 16 * 1000 * 1000, heads * 3 * SEG * SEG),
        name="near",
    )(place, blocks, q, kv, pkv, cot, run.reshape(heads // 2, 2, rows), runt)


def join_kernel(lin_scale, near_out, dq_in, own, nxt, q, kv, cot, runt, states, layer, delta):
    pair = pl.program_id(0)
    head_of = iota((SEG, PAIR), 1) // DH
    head_id = iota(runt.shape, 1)
    c0 = jnp.sum(jnp.where(head_id == pair * 2, runt[...], 0.0), axis=1, keepdims=True)
    c1 = jnp.sum(jnp.where(head_id == pair * 2 + 1, runt[...], 0.0), axis=1, keepdims=True)
    run = jnp.where(head_of == 0, c0, c1)
    growth = jnp.exp(run) * lin_scale
    fading = jnp.exp(run[SEG - 1 : SEG, :] - run)
    diag = iota((PAIR, PAIR), 0) // DH == iota((PAIR, PAIR), 1) // DH
    zero = jnp.zeros((), BF)

    def blocks(part):
        one = states[part, 0]
        return jnp.where(diag, jnp.concatenate([one, one], axis=0), zero)

    before, after = blocks(0), blocks(1)
    layer[...] = (near_out[...] + growth * dot(q[...], before, 1, 0)).astype(BF)
    delta[0, :, :PAIR] = (dq_in[...] + growth * dot(cot[...], before, 1, 1)).astype(BF)
    dk = own[0] + fading * dot(kv[1], after, 1, 1)
    dv = own[1] + fading * dot(kv[0], after, 1, 0)
    delta[0, :, PAIR : 2 * PAIR] = (dk + nxt[0].astype(F32)).astype(BF)
    delta[0, :, 2 * PAIR :] = (dv + nxt[1].astype(F32)).astype(BF)


def join(near_out, dq, own, nxt, q, kv, cot, runt, states, lin_scale):
    rows, width = q.shape
    heads = runt.shape[1]
    pairs = width // PAIR
    col = pl.BlockSpec((rows, PAIR), lambda i: (0, i))
    two = pl.BlockSpec((2, rows, PAIR), lambda i: (0, 0, i))
    return pl.pallas_call(
        functools.partial(join_kernel, lin_scale),
        grid=(pairs,),
        in_specs=[
            col,
            col,
            two,
            two,
            col,
            two,
            col,
            pl.BlockSpec((rows, heads), lambda i: (0, 0)),
            pl.BlockSpec((2, 1, DH, PAIR), lambda i: (0, i, 0, 0)),
        ],
        out_specs=[col, pl.BlockSpec((1, rows, 3 * PAIR), lambda i: (i, 0, 0))],
        out_shape=[
            jax.ShapeDtypeStruct((rows, width), BF),
            jax.ShapeDtypeStruct((pairs, rows, 3 * PAIR), BF),
        ],
        compiler_params=params(32),
        cost_estimate=cost(8 * rows * PAIR * PAIR * pairs, 24 * rows * width),
        name="join",
    )(near_out, dq, own, nxt, q, kv, cot, runt, states)


def back_kernel(delta, wq, wk, wv, out, total):
    step = pl.program_id(0)

    @pl.when(step == 0)
    def _():
        total[...] = jnp.zeros_like(total)

    acc = total[...]
    for part, w in enumerate((wq, wk, wv)):
        for half in range(2):
            acc += dot(
                delta[half, :, part * PAIR : (part + 1) * PAIR],
                w[:, half * PAIR : (half + 1) * PAIR],
                1,
                1,
            )
    total[...] = acc

    @pl.when(step == pl.num_programs(0) - 1)
    def _():
        out[...] = acc.astype(BF)


def back(delta, wq, wk, wv):
    pairs, rows, _ = delta.shape
    width = wq.shape[0]
    weight = pl.BlockSpec((width, 2 * PAIR), lambda i: (0, i))
    return pl.pallas_call(
        back_kernel,
        grid=(pairs // 2,),
        in_specs=[pl.BlockSpec((2, rows, 3 * PAIR), lambda i: (i, 0, 0)), weight, weight, weight],
        out_specs=pl.BlockSpec((rows, width), lambda i: (0, 0)),
        out_shape=jax.ShapeDtypeStruct((rows, width), BF),
        scratch_shapes=[VMEM((rows, width), F32)],
        compiler_params=params(32),
        cost_estimate=cost(6 * rows * width * width, 6 * width * width + 8 * rows * width),
        name="back",
    )(delta, wq, wk, wv)


def outer_kernel(tokt, delta, out):
    acc = dot(tokt[0], delta[0], 1, 0)
    for i in range(1, delta.shape[0]):
        acc += dot(tokt[i], delta[i], 1, 0)
    out[...] = acc.astype(BF)


def outer(tokt, delta):
    near_count, rows, cols = delta.shape
    width = tokt.shape[1]
    return pl.pallas_call(
        outer_kernel,
        grid=(4,),
        in_specs=[
            pl.BlockSpec((near_count, width // 4, rows), lambda i: (0, i, 0)),
            pl.BlockSpec((near_count, rows, cols), lambda i: (0, 0, 0)),
        ],
        out_specs=pl.BlockSpec((width // 4, cols), lambda i: (i, 0)),
        out_shape=jax.ShapeDtypeStruct((width, cols), BF),
        compiler_params=params(32),
        cost_estimate=cost(
            2 * near_count * rows * cols * width, 2 * near_count * rows * (width + cols)
        ),
        name="outer",
    )(tokt, delta)


def place_kernel(core, mine, other, gq, gk, gv):
    del core
    step = pl.program_id(0)

    def put(src):
        for j in range(8):
            for part, o in enumerate((gq, gk, gv)):
                o[:, j * PAIR : (j + 1) * PAIR] = src[0, j, :, part * PAIR : (part + 1) * PAIR]

    @pl.when(step < 8)
    def _():
        put(mine)

    @pl.when(step >= 8)
    def _():
        put(other)


def place_all(core, mine, other):
    blocks, near_count, rows, cols = mine.shape
    width = 2 * blocks * rows

    def where(i, core):
        half = i // 8
        piece = i % 8
        c = jnp.where(half == 0, core[0], 1 - core[0])
        return ((piece // 4) * 8 + c * 4 + piece % 4, 0)

    grad = pl.BlockSpec((rows, width), where)
    return pl.pallas_call(
        place_kernel,
        grid_spec=pltpu.PrefetchScalarGridSpec(
            num_scalar_prefetch=1,
            grid=(16,),
            in_specs=[
                pl.BlockSpec(
                    (1, near_count, rows, cols), lambda i, core: (jnp.minimum(i, 7), 0, 0, 0)
                ),
                pl.BlockSpec(
                    (1, near_count, rows, cols), lambda i, core: (jnp.maximum(i - 8, 0), 0, 0, 0)
                ),
            ],
            out_specs=[grad, grad, grad],
        ),
        out_shape=[jax.ShapeDtypeStruct((width, width), BF)] * 3,
        compiler_params=params(32),
        cost_estimate=cost(0, 12 * width * width),
        name="place",
    )(core, mine, other)


def shards(tokens, wq, wk, wv, log_decay, neighbour_blocks, cot):
    rows, width = tokens.shape
    lin_scale = 1.0 / (DH * math.sqrt(rows))
    place = lax.axis_index(AX).astype(jnp.int32).reshape(1)
    core = lax.axis_index("c").astype(jnp.int32).reshape(1)

    q, kv, run, runt, tokt, msg = project(tokens, wq, wk, wv, log_decay, cot, lin_scale)
    got = lax.all_to_all(msg.reshape(DEVS, 16, PAIR), AX, 0, 0)
    pkv = lax.ppermute(kv, AX, [(i, i + 1) for i in range(DEVS - 1)])
    tokt8 = lax.all_gather(tokt, NEAR8)
    near_out, dq, own, prev = near(
        place, neighbour_blocks, q, kv, pkv, cot, run, runt, lin_scale
    )
    states = scan(place, got)
    nxt = lax.ppermute(prev, AX, [(i + 1, i) for i in range(DEVS - 1)])
    states = lax.all_to_all(states.reshape(DEVS, 8, PAIR), AX, 0, 0)
    states = states.reshape(2, width // PAIR, DH, PAIR)
    layer, delta = join(near_out, dq, own, nxt, q, kv, cot, runt, states, lin_scale)

    delta8 = lax.all_to_all(delta, NEAR8, 0, 0)
    partial = outer(tokt8, delta8)
    parts = lax.all_to_all(partial.reshape(16, width // 16, 3 * PAIR), FAR16, 0, 0)
    grad_norm = 1.0 / math.sqrt(rows * DEVS)
    piece = (jnp.sum(parts.astype(F32), axis=0) * grad_norm).astype(BF)
    plane = lax.all_to_all(jnp.broadcast_to(piece[None], (DEVS // 2, *piece.shape)), PLANE, 0, 0)
    other = lax.ppermute(plane, "c", [(0, 1), (1, 0)])
    tokens_grad = back(delta, wq, wk, wv)
    shape = (8, 8, *piece.shape)
    gq, gk, gv = place_all(core, plane.reshape(shape), other.reshape(shape))
    return layer, tokens_grad, gq, gk, gv


def solution(mesh):
    chips = Mesh(mesh.devices.reshape(2, 2, 4, 4, 2), AX)
    tok = P(AX, None)
    return jax.shard_map(
        shards,
        mesh=chips,
        in_specs=(tok, P(), P(), P(), P(None, AX), tok, tok),
        out_specs=(tok, tok, P(), P(), P()),
        check_vma=False,
    )
```

```python
import functools
import math

import jax
import jax.numpy as jnp
from jax import lax
from jax.experimental import pallas as pl
from jax.experimental.pallas import tpu as pltpu
from jax.sharding import Mesh
from jax.sharding import PartitionSpec as P

BF = jnp.bfloat16
F32 = jnp.float32
AX = ("yl", "c", "x", "z", "yh")
NEAR8 = ("c", "x")
FAR16 = ("yl", "z", "yh")
PLANE = ("x", "yl", "z", "yh")
SEG = 128
PAIR = 128
DH = 64
DEVS = 128
VMEM = pltpu.VMEM
HIGH = lax.Precision.HIGHEST


def dot(a, b, ca, cb, precision=None):
    return lax.dot_general(
        a, b, (((ca,), (cb,)), ((), ())), precision=precision, preferred_element_type=F32
    )


def iota(shape, axis):
    return lax.broadcasted_iota(jnp.int32, shape, axis)


def params(mib):
    return pltpu.CompilerParams(vmem_limit_bytes=mib << 20)


def cost(flops, moved, trans=0):
    return pl.CostEstimate(flops=flops, bytes_accessed=moved, transcendentals=trans)


def project_kernel(lin_scale, tok, ptok, wq, wk, wv, decay, cot, q_out, kv_out, pkv_out, run_out, runt_out, msg):
    step = pl.program_id(0)
    x = tok[...]
    both = jnp.concatenate([x, ptok[...]], axis=0)
    q = dot(x, wq[...], 1, 0).astype(BF)
    kk = dot(both, wk[...], 1, 0).astype(BF)
    vv = dot(both, wv[...], 1, 0).astype(BF)
    k, v = kk[:SEG], vv[:SEG]
    q_out[...] = q
    kv_out[0] = k
    kv_out[1] = v
    pkv_out[0] = kk[SEG:]
    pkv_out[1] = vv[SEG:]
    ld = decay[...]
    heads = ld.shape[0]
    lower = (iota((SEG, SEG), 0) >= iota((SEG, SEG), 1)).astype(F32)
    runt = dot(lower, ld, 1, 1, HIGH)
    runt_out[...] = runt

    @pl.when(step == 0)
    def _():
        run_out[...] = dot(ld, lower, 1, 1, HIGH)

    head_of = iota((SEG, PAIR), 1) // DH
    head_id = iota((SEG, heads), 1)
    rows = iota((8, PAIR), 0)
    for half in range(2):
        cols = slice(half * PAIR, (half + 1) * PAIR)
        first = (step * 2 + half) * 2
        c0 = jnp.sum(jnp.where(head_id == first, runt, 0.0), axis=1, keepdims=True)
        c1 = jnp.sum(jnp.where(head_id == first + 1, runt, 0.0), axis=1, keepdims=True)
        run = jnp.where(head_of == 0, c0, c1)
        total = run[SEG - 1 : SEG, :]
        weighted = (v[:, cols].astype(F32) * jnp.exp(total - run)).astype(BF)
        scaled = (cot[:, cols].astype(F32) * jnp.exp(run)).astype(BF)
        full_s = dot(k[:, cols], weighted, 0, 0)
        full_g = dot(q[:, cols], scaled, 0, 0) * lin_scale
        high = total.astype(BF).astype(F32)
        mid = (total - high).astype(BF).astype(F32)
        low = total - high - mid
        tail = jnp.where(rows == 0, high, jnp.where(rows == 1, mid, jnp.where(rows == 2, low, 0.0)))
        tail = jnp.broadcast_to(tail[None], (8, 8, PAIR))
        lanes = iota((DH, PAIR), 1) < DH
        for part, full in ((0, full_s), (1, full_g)):
            own = jnp.where(lanes, full[:DH], full[DH:]).reshape(8, 8, PAIR)
            both = jnp.concatenate([own, tail], axis=1).reshape(PAIR, PAIR)
            msg[part, half * PAIR : (half + 1) * PAIR, :] = both.astype(BF)


def project(tokens, prev_tokens, wq, wk, wv, log_decay, cot, lin_scale):
    rows, width = tokens.shape
    heads = log_decay.shape[0]
    steps = width // 256
    col = pl.BlockSpec((rows, 256), lambda i: (0, i))
    weight = pl.BlockSpec((width, 256), lambda i: (0, i))
    return pl.pallas_call(
        functools.partial(project_kernel, lin_scale),
        grid=(steps,),
        in_specs=[
            pl.BlockSpec((rows, width), lambda i: (0, 0)),
            pl.BlockSpec((rows, width), lambda i: (0, 0)),
            weight,
            weight,
            weight,
            pl.BlockSpec((heads, rows), lambda i: (0, 0)),
            col,
        ],
        out_specs=[
            col,
            pl.BlockSpec((2, rows, 256), lambda i: (0, 0, i)),
            pl.BlockSpec((2, rows, 256), lambda i: (0, 0, i)),
            pl.BlockSpec((heads, rows), lambda i: (0, 0)),
            pl.BlockSpec((rows, heads), lambda i: (0, 0)),
            pl.BlockSpec((2, 2 * PAIR, PAIR), lambda i: (0, i, 0)),
        ],
        out_shape=[
            jax.ShapeDtypeStruct((rows, width), BF),
            jax.ShapeDtypeStruct((2, rows, width), BF),
            jax.ShapeDtypeStruct((2, rows, width), BF),
            jax.ShapeDtypeStruct((heads, rows), F32),
            jax.ShapeDtypeStruct((rows, heads), F32),
            jax.ShapeDtypeStruct((2, width, PAIR), BF),
        ],
        compiler_params=params(58),
        cost_estimate=cost(10 * rows * width * width, 6 * width * width + 12 * rows * width),
        name="project",
    )(tokens, prev_tokens, wq, wk, wv, log_decay, cot)


def flip_kernel(tok, out):
    out[...] = tok[...].T


def flip(tokens):
    rows, width = tokens.shape
    return pl.pallas_call(
        flip_kernel,
        in_specs=[pl.BlockSpec(memory_space=VMEM)],
        out_specs=pl.BlockSpec(memory_space=VMEM),
        out_shape=jax.ShapeDtypeStruct((width, rows), BF),
        compiler_params=params(16),
        cost_estimate=cost(0, 4 * rows * width),
        name="flip",
    )(tokens)


def scan_kernel(place, got, out, xs, decays, states):
    both = got[...].astype(F32)
    xs[...] = both[:, :8, :]
    total = both[:, 8:9, :] + both[:, 9:10, :] + both[:, 10:11, :]
    decays[...] = jnp.broadcast_to(jnp.exp(total), decays.shape)
    backward = place[0] >= DEVS // 2

    def one(i, state):
        at = jnp.where(backward, DEVS - 1 - i, i)
        states[at] = state
        return decays[at] * state + xs[at]

    lax.fori_loop(0, DEVS, one, jnp.zeros((8, PAIR), F32), unroll=8)
    out[...] = states[...].reshape(DEVS * 8, PAIR).astype(BF)


def scan(place, got):
    whole = pl.BlockSpec(memory_space=VMEM)
    return pl.pallas_call(
        scan_kernel,
        in_specs=[pl.BlockSpec(memory_space=pltpu.SMEM), whole],
        out_specs=whole,
        out_shape=jax.ShapeDtypeStruct((DEVS * 8, PAIR), BF),
        scratch_shapes=[VMEM((DEVS, 8, PAIR), F32)] * 3,
        compiler_params=params(24),
        cost_estimate=cost(2 * DEVS * 8 * PAIR, 4 * DEVS * 16 * PAIR),
        name="scan",
    )(place, got)


def near_kernel(lin_scale, place, blocks, q_ref, kv, pkv, cot, run_rows, runt, out, dq_out, own, prev):
    pair = pl.program_id(0)
    soft_scale = 1.0 / math.sqrt(DH)
    n_own = jnp.int32(0)
    n_prev = jnp.int32(0)
    for j in range(blocks.shape[1]):
        n_own += (blocks[0, j] == place[0]).astype(jnp.int32)
        n_prev += (blocks[0, j] == place[0] - 1).astype(jnp.int32)
    is_own = iota((1, 2 * SEG), 1) < SEG
    times = jnp.where(is_own, n_own, n_prev)
    bias = jnp.where(times > 0, 0.0, -1e30)
    times = times.astype(F32)
    q = q_ref[...]
    g = cot[...]
    kk = jnp.concatenate([kv[0], pkv[0]], axis=0)
    vv = jnp.concatenate([kv[1], pkv[1]], axis=0)
    head_of = iota((SEG, PAIR), 1) // DH
    head_of2 = iota((2 * SEG, PAIR), 1) // DH
    lower = iota((SEG, SEG), 0) >= iota((SEG, SEG), 1)
    head_id = iota(runt.shape, 1)
    zero = jnp.zeros((), BF)
    res = []
    for i in range(2):
        mine = head_of == i
        col = jnp.sum(jnp.where(head_id == pair * 2 + i, runt[...], 0.0), axis=1, keepdims=True)
        row = run_rows[0, i : i + 1, :]
        dec = jnp.where(lower, jnp.exp(jnp.minimum(col - row, 0.0)), 0.0) * lin_scale
        scores = dot(jnp.where(mine, q, zero), kk, 1, 1)
        pgrad = dot(jnp.where(mine, g, zero), vv, 1, 1)
        logits = scores * soft_scale + bias
        peak = jnp.max(logits, axis=1, keepdims=True)
        terms = jnp.exp(logits - peak) * times
        probs = terms * (1.0 / jnp.sum(terms, axis=1, keepdims=True))
        inner = jnp.sum(probs * pgrad, axis=1, keepdims=True)
        dlog = probs * (pgrad - inner) * soft_scale
        a = jnp.concatenate(
            [probs[:, :SEG] + scores[:, :SEG] * dec, probs[:, SEG:]], axis=1
        ).astype(BF)
        b = jnp.concatenate([dlog[:, :SEG] + pgrad[:, :SEG] * dec, dlog[:, SEG:]], axis=1).astype(BF)
        res.append((dot(a, vv, 1, 0), dot(b, kk, 1, 0), dot(b, q, 0, 0), dot(a, g, 0, 0)))
    out[...] = jnp.where(head_of == 0, res[0][0], res[1][0])
    dq_out[...] = jnp.where(head_of == 0, res[0][1], res[1][1])
    for part in range(2):
        both = jnp.where(head_of2 == 0, res[0][2 + part], res[1][2 + part])
        own[part] = both[:SEG]
        prev[part] = both[SEG:].astype(BF)


def near(place, blocks, q, kv, pkv, cot, run, runt, lin_scale):
    rows, width = q.shape
    heads = run.shape[0]
    smem = pl.BlockSpec(memory_space=pltpu.SMEM)
    col = pl.BlockSpec((rows, PAIR), lambda i: (0, i))
    two = pl.BlockSpec((2, rows, PAIR), lambda i: (0, 0, i))
    return pl.pallas_call(
        functools.partial(near_kernel, lin_scale),
        grid=(width // PAIR,),
        in_specs=[
            smem,
            smem,
            col,
            two,
            two,
            col,
            pl.BlockSpec((1, 2, rows), lambda i: (i, 0, 0)),
            pl.BlockSpec((rows, heads), lambda i: (0, 0)),
        ],
        out_specs=[col, col, two, two],
        out_shape=[
            jax.ShapeDtypeStruct((rows, width), F32),
            jax.ShapeDtypeStruct((rows, width), F32),
            jax.ShapeDtypeStruct((2, rows, width), F32),
            jax.ShapeDtypeStruct((2, rows, width), BF),
        ],
        compiler_params=params(32),
        cost_estimate=cost(4000 * 1000 * 1000, 16 * 1000 * 1000, heads * 3 * SEG * SEG),
        name="near",
    )(place, blocks, q, kv, pkv, cot, run.reshape(heads // 2, 2, rows), runt)


def join_kernel(lin_scale, near_out, dq_in, own, nxt, q, kv, cot, runt, states, layer, delta):
    pair = pl.program_id(0)
    head_of = iota((SEG, PAIR), 1) // DH
    head_id = iota(runt.shape, 1)
    c0 = jnp.sum(jnp.where(head_id == pair * 2, runt[...], 0.0), axis=1, keepdims=True)
    c1 = jnp.sum(jnp.where(head_id == pair * 2 + 1, runt[...], 0.0), axis=1, keepdims=True)
    run = jnp.where(head_of == 0, c0, c1)
    growth = jnp.exp(run) * lin_scale
    fading = jnp.exp(run[SEG - 1 : SEG, :] - run)
    diag = iota((PAIR, PAIR), 0) // DH == iota((PAIR, PAIR), 1) // DH
    zero = jnp.zeros((), BF)

    def blocks(part):
        one = states[part, 0]
        return jnp.where(diag, jnp.concatenate([one, one], axis=0), zero)

    before, after = blocks(0), blocks(1)
    layer[...] = (near_out[...] + growth * dot(q[...], before, 1, 0)).astype(BF)
    delta[0, :, :PAIR] = (dq_in[...] + growth * dot(cot[...], before, 1, 1)).astype(BF)
    dk = own[0] + fading * dot(kv[1], after, 1, 1)
    dv = own[1] + fading * dot(kv[0], after, 1, 0)
    delta[0, :, PAIR : 2 * PAIR] = (dk + nxt[0].astype(F32)).astype(BF)
    delta[0, :, 2 * PAIR :] = (dv + nxt[1].astype(F32)).astype(BF)


def join(near_out, dq, own, nxt, q, kv, cot, runt, states, lin_scale):
    rows, width = q.shape
    heads = runt.shape[1]
    pairs = width // PAIR
    col = pl.BlockSpec((rows, PAIR), lambda i: (0, i))
    two = pl.BlockSpec((2, rows, PAIR), lambda i: (0, 0, i))
    return pl.pallas_call(
        functools.partial(join_kernel, lin_scale),
        grid=(pairs,),
        in_specs=[
            col,
            col,
            two,
            two,
            col,
            two,
            col,
            pl.BlockSpec((rows, heads), lambda i: (0, 0)),
            pl.BlockSpec((2, 1, DH, PAIR), lambda i: (0, i, 0, 0)),
        ],
        out_specs=[col, pl.BlockSpec((1, rows, 3 * PAIR), lambda i: (i, 0, 0))],
        out_shape=[
            jax.ShapeDtypeStruct((rows, width), BF),
            jax.ShapeDtypeStruct((pairs, rows, 3 * PAIR), BF),
        ],
        compiler_params=params(32),
        cost_estimate=cost(8 * rows * PAIR * PAIR * pairs, 24 * rows * width),
        name="join",
    )(near_out, dq, own, nxt, q, kv, cot, runt, states)


def back_kernel(delta, wq, wk, wv, out, total):
    step = pl.program_id(0)

    @pl.when(step == 0)
    def _():
        total[...] = jnp.zeros_like(total)

    acc = total[...]
    for part, w in enumerate((wq, wk, wv)):
        for half in range(2):
            acc += dot(
                delta[half, :, part * PAIR : (part + 1) * PAIR],
                w[:, half * PAIR : (half + 1) * PAIR],
                1,
                1,
            )
    total[...] = acc

    @pl.when(step == pl.num_programs(0) - 1)
    def _():
        out[...] = acc.astype(BF)


def back(delta, wq, wk, wv):
    pairs, rows, _ = delta.shape
    width = wq.shape[0]
    weight = pl.BlockSpec((width, 2 * PAIR), lambda i: (0, i))
    return pl.pallas_call(
        back_kernel,
        grid=(pairs // 2,),
        in_specs=[pl.BlockSpec((2, rows, 3 * PAIR), lambda i: (i, 0, 0)), weight, weight, weight],
        out_specs=pl.BlockSpec((rows, width), lambda i: (0, 0)),
        out_shape=jax.ShapeDtypeStruct((rows, width), BF),
        scratch_shapes=[VMEM((rows, width), F32)],
        compiler_params=params(32),
        cost_estimate=cost(6 * rows * width * width, 6 * width * width + 8 * rows * width),
        name="back",
    )(delta, wq, wk, wv)


def outer_kernel(tokt, delta, out):
    acc = dot(tokt[0], delta[0], 1, 0)
    for i in range(1, delta.shape[0]):
        acc += dot(tokt[i], delta[i], 1, 0)
    out[...] = acc.astype(BF)


def outer(tokt, delta):
    near_count, rows, cols = delta.shape
    width = tokt.shape[1]
    return pl.pallas_call(
        outer_kernel,
        grid=(4,),
        in_specs=[
            pl.BlockSpec((near_count, width // 4, rows), lambda i: (0, i, 0)),
            pl.BlockSpec((near_count, rows, cols), lambda i: (0, 0, 0)),
        ],
        out_specs=pl.BlockSpec((width // 4, cols), lambda i: (i, 0)),
        out_shape=jax.ShapeDtypeStruct((width, cols), BF),
        compiler_params=params(58),
        cost_estimate=cost(
            2 * near_count * rows * cols * width, 2 * near_count * rows * (width + cols)
        ),
        name="outer",
    )(tokt, delta)


def place_kernel(side, pieces, *rest):
    del side
    for x in range(pieces.shape[0]):
        for r in range(pieces.shape[1]):
            rows = slice(r * pieces.shape[2], (r + 1) * pieces.shape[2])
            for part, o in enumerate(rest[-3:]):
                o[rows, x * PAIR : (x + 1) * PAIR] = pieces[x, r, :, part * PAIR : (part + 1) * PAIR]


def place_half(side, pieces, grads=()):
    near_count, blocks, rows, cols = pieces.shape
    width = blocks * rows
    out = jax.ShapeDtypeStruct((width, width), BF)
    return pl.pallas_call(
        place_kernel,
        grid_spec=pltpu.PrefetchScalarGridSpec(
            num_scalar_prefetch=1,
            grid=(blocks // 2,),
            in_specs=[pl.BlockSpec((near_count, 2, rows, cols), lambda i, side: (0, i, 0, 0))]
            + [pl.BlockSpec(memory_space=pl.ANY)] * len(grads),
            out_specs=[
                pl.BlockSpec((2 * rows, near_count * PAIR), lambda i, side: (i, side[0]))
            ]
            * 3,
        ),
        out_shape=[out] * 3,
        input_output_aliases={2 + i: i for i in range(len(grads))},
        compiler_params=params(24),
        cost_estimate=cost(0, 6 * width * width),
        name="place",
    )(side, pieces, *grads)


def shards(tokens, wq, wk, wv, log_decay, neighbour_blocks, cot):
    rows, width = tokens.shape
    lin_scale = 1.0 / (DH * math.sqrt(rows))
    place = lax.axis_index(AX).astype(jnp.int32).reshape(1)
    core = lax.axis_index("c").astype(jnp.int32).reshape(1)

    prev_tokens = lax.ppermute(tokens, AX, [(i, i + 1) for i in range(DEVS - 1)])
    tokt8 = lax.all_gather(flip(tokens), NEAR8)
    q, kv, pkv, run, runt, msg = project(
        tokens, prev_tokens, wq, wk, wv, log_decay, cot, lin_scale
    )
    got = lax.all_to_all(msg.reshape(DEVS, 16, PAIR), AX, 0, 0)
    near_out, dq, own, prev = near(
        place, neighbour_blocks, q, kv, pkv, cot, run, runt, lin_scale
    )
    states = scan(place, got)
    nxt = lax.ppermute(prev, AX, [(i + 1, i) for i in range(DEVS - 1)])
    states = lax.all_to_all(states.reshape(DEVS, 8, PAIR), AX, 0, 0)
    states = states.reshape(2, width // PAIR, DH, PAIR)
    layer, delta = join(near_out, dq, own, nxt, q, kv, cot, runt, states, lin_scale)

    delta8 = lax.all_to_all(delta, NEAR8, 0, 0)
    partial = outer(tokt8, delta8)
    parts = lax.all_to_all(partial.reshape(16, width // 16, 3 * PAIR), FAR16, 0, 0)
    grad_norm = 1.0 / math.sqrt(rows * DEVS)
    piece = (jnp.sum(parts.astype(F32), axis=0) * grad_norm).astype(BF)
    plane = lax.all_to_all(jnp.broadcast_to(piece[None], (DEVS // 2, *piece.shape)), PLANE, 0, 0)
    other = lax.ppermute(plane, "c", [(0, 1), (1, 0)])
    tokens_grad = back(delta, wq, wk, wv)
    shape = (4, 16, *piece.shape)
    grads = place_half(core, plane.reshape(shape))
    gq, gk, gv = place_half(1 - core, other.reshape(shape), grads)
    return layer, tokens_grad, gq, gk, gv


def solution(mesh):
    chips = Mesh(mesh.devices.reshape(2, 2, 4, 4, 2), AX)
    tok = P(AX, None)
    return jax.shard_map(
        shards,
        mesh=chips,
        in_specs=(tok, P(), P(), P(), P(None, AX), tok, tok),
        out_specs=(tok, tok, P(), P(), P()),
        check_vma=False,
    )
```

```python
import functools
import math

import jax
import jax.numpy as jnp
from jax import lax
from jax.experimental import pallas as pl
from jax.experimental.pallas import tpu as pltpu
from jax.sharding import Mesh
from jax.sharding import PartitionSpec as P

BF = jnp.bfloat16
F32 = jnp.float32
AX = ("yl", "c", "x", "z", "yh")
NEAR8 = ("c", "x")
FAR16 = ("yl", "z", "yh")
PLANE = ("x", "yl", "z", "yh")
SEG = 128
PAIR = 128
DH = 64
DEVS = 128
VMEM = pltpu.VMEM
HIGH = lax.Precision.HIGHEST


def dot(a, b, ca, cb, precision=None):
    return lax.dot_general(
        a, b, (((ca,), (cb,)), ((), ())), precision=precision, preferred_element_type=F32
    )


def iota(shape, axis):
    return lax.broadcasted_iota(jnp.int32, shape, axis)


def params(mib):
    return pltpu.CompilerParams(vmem_limit_bytes=mib << 20)


def cost(flops, moved, trans=0):
    return pl.CostEstimate(flops=flops, bytes_accessed=moved, transcendentals=trans)


CHUNK = 256


def project_kernel(lin_scale, tok, ptok, wq, wk, wv, decay, cot, q_out, kv_out, pkv_out, run_out, runt_out, msg, held, sems):
    width = tok.shape[1]
    chunks = width // CHUNK
    copies = []
    for step in range(chunks):
        for part, w in enumerate((wq, wk, wv)):
            copy = pltpu.make_async_copy(
                w.at[:, pl.ds(step * CHUNK, CHUNK)], held.at[part, step], sems.at[part, step]
            )
            copy.start()
            copies.append(copy)
    x = tok[...]
    both = jnp.concatenate([x, ptok[...]], axis=0)
    ld = decay[...]
    heads = ld.shape[0]
    lower = (iota((SEG, SEG), 0) >= iota((SEG, SEG), 1)).astype(F32)
    runt = dot(lower, ld, 1, 1, HIGH)
    run = dot(ld, lower, 1, 1, HIGH)
    group = heads // chunks
    for step in range(chunks):
        runt_out[step] = runt[:, step * group : (step + 1) * group]
        run_out[step] = run[step * group : (step + 1) * group, :]
    head_of = iota((SEG, PAIR), 1) // DH
    rows = iota((8, PAIR), 0)
    lanes = iota((DH, PAIR), 1) < DH
    for step in range(chunks):
        for part in range(3):
            copies[step * 3 + part].wait()
        at = slice(step * CHUNK, (step + 1) * CHUNK)
        q = dot(x, held[0, step], 1, 0).astype(BF)
        kk = dot(both, held[1, step], 1, 0).astype(BF)
        vv = dot(both, held[2, step], 1, 0).astype(BF)
        k, v = kk[:SEG], vv[:SEG]
        q_out[:, at] = q
        kv_out[0, :, at] = k
        kv_out[1, :, at] = v
        pkv_out[0, :, at] = kk[SEG:]
        pkv_out[1, :, at] = vv[SEG:]
        for half in range(CHUNK // PAIR):
            cols = slice(half * PAIR, (half + 1) * PAIR)
            pair = step * (CHUNK // PAIR) + half
            run = jnp.where(
                head_of == 0, runt[:, 2 * pair : 2 * pair + 1], runt[:, 2 * pair + 1 : 2 * pair + 2]
            )
            total = run[SEG - 1 : SEG, :]
            grads = cot[:, pair * PAIR : (pair + 1) * PAIR].astype(F32)
            weighted = (v[:, cols].astype(F32) * jnp.exp(total - run)).astype(BF)
            scaled = (grads * jnp.exp(run)).astype(BF)
            full_s = dot(k[:, cols], weighted, 0, 0)
            full_g = dot(q[:, cols], scaled, 0, 0) * lin_scale
            high = total.astype(BF).astype(F32)
            mid = (total - high).astype(BF).astype(F32)
            low = total - high - mid
            tail = jnp.where(
                rows == 0, high, jnp.where(rows == 1, mid, jnp.where(rows == 2, low, 0.0))
            )
            tail = jnp.broadcast_to(tail[None], (8, 8, PAIR))
            for part, full in ((0, full_s), (1, full_g)):
                own = jnp.where(lanes, full[:DH], full[DH:]).reshape(8, 8, PAIR)
                sent = jnp.concatenate([own, tail], axis=1).reshape(PAIR, PAIR)
                msg[part, pair * PAIR : (pair + 1) * PAIR, :] = sent.astype(BF)


def project(tokens, prev_tokens, wq, wk, wv, log_decay, cot, lin_scale):
    rows, width = tokens.shape
    heads = log_decay.shape[0]
    vmem = pl.BlockSpec(memory_space=VMEM)
    hbm = pl.BlockSpec(memory_space=pltpu.HBM)
    return pl.pallas_call(
        functools.partial(project_kernel, lin_scale),
        in_specs=[vmem, vmem, hbm, hbm, hbm, vmem, vmem],
        out_specs=[vmem] * 6,
        out_shape=[
            jax.ShapeDtypeStruct((rows, width), BF),
            jax.ShapeDtypeStruct((2, rows, width), BF),
            jax.ShapeDtypeStruct((2, rows, width), BF),
            jax.ShapeDtypeStruct((width // CHUNK, heads * CHUNK // width, rows), F32),
            jax.ShapeDtypeStruct((width // CHUNK, rows, heads * CHUNK // width), F32),
            jax.ShapeDtypeStruct((2, width, PAIR), BF),
        ],
        scratch_shapes=[
            VMEM((3, width // CHUNK, width, CHUNK), BF),
            pltpu.SemaphoreType.DMA((3, width // CHUNK)),
        ],
        compiler_params=params(58),
        cost_estimate=cost(10 * rows * width * width, 6 * width * width + 12 * rows * width),
        name="project",
    )(tokens, prev_tokens, wq, wk, wv, log_decay, cot)


def flip_kernel(tok, after, out):
    del after
    out[...] = tok[...].T


def flip(tokens, after):
    rows, width = tokens.shape
    return pl.pallas_call(
        flip_kernel,
        in_specs=[pl.BlockSpec(memory_space=VMEM), pl.BlockSpec(memory_space=pl.ANY)],
        out_specs=pl.BlockSpec(memory_space=VMEM),
        out_shape=jax.ShapeDtypeStruct((width, rows), BF),
        compiler_params=params(16),
        cost_estimate=cost(0, 4 * rows * width),
        name="flip",
    )(tokens, after)


def scan_kernel(place, got, after, out, xs, decays, states):
    del after
    both = got[...].astype(F32)
    xs[...] = both[:, :8, :]
    total = both[:, 8:9, :] + both[:, 9:10, :] + both[:, 10:11, :]
    decays[...] = jnp.broadcast_to(jnp.exp(total), decays.shape)
    backward = place[0] >= DEVS // 2

    def one(i, state):
        at = jnp.where(backward, DEVS - 1 - i, i)
        states[at] = state
        return decays[at] * state + xs[at]

    lax.fori_loop(0, DEVS, one, jnp.zeros((8, PAIR), F32), unroll=8)
    out[...] = states[...].reshape(DEVS * 8, PAIR).astype(BF)


def scan(place, got, after):
    whole = pl.BlockSpec(memory_space=VMEM)
    return pl.pallas_call(
        scan_kernel,
        in_specs=[
            pl.BlockSpec(memory_space=pltpu.SMEM),
            whole,
            pl.BlockSpec(memory_space=pl.ANY),
        ],
        out_specs=whole,
        out_shape=jax.ShapeDtypeStruct((DEVS * 8, PAIR), BF),
        scratch_shapes=[VMEM((DEVS, 8, PAIR), F32)] * 3,
        compiler_params=params(24),
        cost_estimate=cost(2 * DEVS * 8 * PAIR, 4 * DEVS * 16 * PAIR),
        name="scan",
    )(place, got, after)


def near_kernel(lin_scale, place, blocks, q_ref, kv, pkv, cot, run, runt, out, dq_out, own, prev):
    soft_scale = 1.0 / math.sqrt(DH)
    n_own = jnp.int32(0)
    n_prev = jnp.int32(0)
    for j in range(blocks.shape[1]):
        n_own += (blocks[0, j] == place[0]).astype(jnp.int32)
        n_prev += (blocks[0, j] == place[0] - 1).astype(jnp.int32)
    is_own = iota((1, 2 * SEG), 1) < SEG
    times = jnp.where(is_own, n_own, n_prev)
    bias = jnp.where(times > 0, 0.0, -1e30)
    times = times.astype(F32)
    head_of = iota((SEG, PAIR), 1) // DH
    head_of2 = iota((2 * SEG, PAIR), 1) // DH
    lower = iota((SEG, SEG), 0) >= iota((SEG, SEG), 1)
    zero = jnp.zeros((), BF)
    for pair in range(q_ref.shape[1] // PAIR):
        at = slice(pair * PAIR, (pair + 1) * PAIR)
        q = q_ref[:, at]
        g = cot[:, at]
        kk = jnp.concatenate([kv[0, :, at], pkv[0, :, at]], axis=0)
        vv = jnp.concatenate([kv[1, :, at], pkv[1, :, at]], axis=0)
        res = []
        for i in range(2):
            head = pair * 2 + i
            mine = head_of == i
            col = runt[0, :, head : head + 1]
            row = run[0, head : head + 1, :]
            dec = jnp.where(lower, jnp.exp(jnp.minimum(col - row, 0.0)), 0.0) * lin_scale
            scores = dot(jnp.where(mine, q, zero), kk, 1, 1)
            pgrad = dot(jnp.where(mine, g, zero), vv, 1, 1)
            logits = scores * soft_scale + bias
            peak = jnp.max(logits, axis=1, keepdims=True)
            terms = jnp.exp(logits - peak) * times
            probs = terms * (1.0 / jnp.sum(terms, axis=1, keepdims=True))
            inner = jnp.sum(probs * pgrad, axis=1, keepdims=True)
            dlog = probs * (pgrad - inner) * soft_scale
            a = jnp.concatenate(
                [probs[:, :SEG] + scores[:, :SEG] * dec, probs[:, SEG:]], axis=1
            ).astype(BF)
            b = jnp.concatenate(
                [dlog[:, :SEG] + pgrad[:, :SEG] * dec, dlog[:, SEG:]], axis=1
            ).astype(BF)
            res.append((dot(a, vv, 1, 0), dot(b, kk, 1, 0), dot(b, q, 0, 0), dot(a, g, 0, 0)))
        out[:, at] = jnp.where(head_of == 0, res[0][0], res[1][0])
        dq_out[:, at] = jnp.where(head_of == 0, res[0][1], res[1][1])
        for part in range(2):
            sums = jnp.where(head_of2 == 0, res[0][2 + part], res[1][2 + part])
            own[part, :, at] = sums[:SEG]
            prev[part, :, at] = sums[SEG:].astype(BF)


def near(place, blocks, q, kv, pkv, cot, run, runt, lin_scale):
    rows, width = q.shape
    heads = run.shape[1]
    smem = pl.BlockSpec(memory_space=pltpu.SMEM)
    col = pl.BlockSpec((rows, CHUNK), lambda i: (0, i))
    two = pl.BlockSpec((2, rows, CHUNK), lambda i: (0, 0, i))
    return pl.pallas_call(
        functools.partial(near_kernel, lin_scale),
        grid=(width // CHUNK,),
        in_specs=[
            smem,
            smem,
            col,
            two,
            two,
            col,
            pl.BlockSpec((1, heads, rows), lambda i: (i, 0, 0)),
            pl.BlockSpec((1, rows, heads), lambda i: (i, 0, 0)),
        ],
        out_specs=[col, col, two, two],
        out_shape=[
            jax.ShapeDtypeStruct((rows, width), F32),
            jax.ShapeDtypeStruct((rows, width), F32),
            jax.ShapeDtypeStruct((2, rows, width), F32),
            jax.ShapeDtypeStruct((2, rows, width), BF),
        ],
        compiler_params=params(58),
        cost_estimate=cost(4000 * 1000 * 1000, 16 * 1000 * 1000, 1000 * 1000),
        name="near",
    )(place, blocks, q, kv, pkv, cot, run, runt)


def join_kernel(lin_scale, near_out, dq_in, own, nxt, q, kv, cot, runt, states, after, layer, delta):
    del after
    head_of = iota((SEG, PAIR), 1) // DH
    diag = iota((PAIR, PAIR), 0) // DH == iota((PAIR, PAIR), 1) // DH
    zero = jnp.zeros((), BF)
    for pair in range(q.shape[1] // PAIR):
        at = slice(pair * PAIR, (pair + 1) * PAIR)
        run = jnp.where(
            head_of == 0,
            runt[0, :, 2 * pair : 2 * pair + 1],
            runt[0, :, 2 * pair + 1 : 2 * pair + 2],
        )
        growth = jnp.exp(run) * lin_scale
        fading = jnp.exp(run[SEG - 1 : SEG, :] - run)
        before, after = (
            jnp.where(diag, jnp.concatenate([states[part, pair]] * 2, axis=0), zero)
            for part in range(2)
        )
        layer[:, at] = (near_out[:, at] + growth * dot(q[:, at], before, 1, 0)).astype(BF)
        dq = dq_in[:, at] + growth * dot(cot[:, at], before, 1, 1)
        dk = own[0, :, at] + fading * dot(kv[1, :, at], after, 1, 1) + nxt[0, :, at].astype(F32)
        dv = own[1, :, at] + fading * dot(kv[0, :, at], after, 1, 0) + nxt[1, :, at].astype(F32)
        delta[pair, :, :PAIR] = dq.astype(BF)
        delta[pair, :, PAIR : 2 * PAIR] = dk.astype(BF)
        delta[pair, :, 2 * PAIR :] = dv.astype(BF)


def join(near_out, dq, own, nxt, q, kv, cot, runt, states, after, lin_scale):
    rows, width = q.shape
    pairs = width // PAIR
    col = pl.BlockSpec((rows, CHUNK), lambda i: (0, i))
    two = pl.BlockSpec((2, rows, CHUNK), lambda i: (0, 0, i))
    return pl.pallas_call(
        functools.partial(join_kernel, lin_scale),
        grid=(width // CHUNK,),
        in_specs=[
            col,
            col,
            two,
            two,
            col,
            two,
            col,
            pl.BlockSpec((1, rows, runt.shape[2]), lambda i: (i, 0, 0)),
            pl.BlockSpec((2, CHUNK // PAIR, DH, PAIR), lambda i: (0, i, 0, 0)),
            pl.BlockSpec(memory_space=pl.ANY),
        ],
        out_specs=[col, pl.BlockSpec((CHUNK // PAIR, rows, 3 * PAIR), lambda i: (i, 0, 0))],
        out_shape=[
            jax.ShapeDtypeStruct((rows, width), BF),
            jax.ShapeDtypeStruct((pairs, rows, 3 * PAIR), BF),
        ],
        compiler_params=params(58),
        cost_estimate=cost(8 * rows * PAIR * PAIR * pairs, 24 * rows * width),
        name="join",
    )(near_out, dq, own, nxt, q, kv, cot, runt, states, after)


def back_kernel(delta, wq, wk, wv, out, total):
    step = pl.program_id(0)

    @pl.when(step == 0)
    def _():
        total[...] = jnp.zeros_like(total)

    acc = total[...]
    for part, w in enumerate((wq, wk, wv)):
        for half in range(2):
            acc += dot(
                delta[half, :, part * PAIR : (part + 1) * PAIR],
                w[:, half * PAIR : (half + 1) * PAIR],
                1,
                1,
            )
    total[...] = acc

    @pl.when(step == pl.num_programs(0) - 1)
    def _():
        out[...] = acc.astype(BF)


def back(delta, wq, wk, wv):
    pairs, rows, _ = delta.shape
    width = wq.shape[0]
    weight = pl.BlockSpec((width, 2 * PAIR), lambda i: (0, i))
    return pl.pallas_call(
        back_kernel,
        grid=(pairs // 2,),
        in_specs=[pl.BlockSpec((2, rows, 3 * PAIR), lambda i: (i, 0, 0)), weight, weight, weight],
        out_specs=pl.BlockSpec((rows, width), lambda i: (0, 0)),
        out_shape=jax.ShapeDtypeStruct((rows, width), BF),
        scratch_shapes=[VMEM((rows, width), F32)],
        compiler_params=params(58),
        cost_estimate=cost(6 * rows * width * width, 6 * width * width + 8 * rows * width),
        name="back",
    )(delta, wq, wk, wv)


def outer_kernel(tokt, delta, after, out):
    del after
    near_count, rows, cols = delta.shape
    left = jnp.concatenate([tokt[i] for i in range(near_count)], axis=1)
    out[...] = dot(left, delta[...].reshape(near_count * rows, cols), 1, 0).astype(BF)


def outer(tokt, delta, after):
    near_count, rows, cols = delta.shape
    width = tokt.shape[1]
    return pl.pallas_call(
        outer_kernel,
        grid=(4,),
        in_specs=[
            pl.BlockSpec((near_count, width // 4, rows), lambda i: (0, i, 0)),
            pl.BlockSpec((near_count, rows, cols), lambda i: (0, 0, 0)),
            pl.BlockSpec(memory_space=pl.ANY),
        ],
        out_specs=pl.BlockSpec((width // 4, cols), lambda i: (i, 0)),
        out_shape=jax.ShapeDtypeStruct((width, cols), BF),
        compiler_params=params(58),
        cost_estimate=cost(
            2 * near_count * rows * cols * width, 2 * near_count * rows * (width + cols)
        ),
        name="outer",
    )(tokt, delta, after)


def place_kernel(side, pieces, *rest):
    del side
    for x in range(pieces.shape[0]):
        for r in range(pieces.shape[1]):
            rows = slice(r * pieces.shape[2], (r + 1) * pieces.shape[2])
            for part, o in enumerate(rest[-3:]):
                o[rows, x * PAIR : (x + 1) * PAIR] = pieces[x, r, :, part * PAIR : (part + 1) * PAIR]


def place_half(side, pieces, grads=()):
    near_count, blocks, rows, cols = pieces.shape
    width = blocks * rows
    out = jax.ShapeDtypeStruct((width, width), BF)
    return pl.pallas_call(
        place_kernel,
        grid_spec=pltpu.PrefetchScalarGridSpec(
            num_scalar_prefetch=1,
            grid=(blocks // 4,),
            in_specs=[pl.BlockSpec((near_count, 4, rows, cols), lambda i, side: (0, i, 0, 0))]
            + [pl.BlockSpec(memory_space=pl.ANY)] * len(grads),
            out_specs=[
                pl.BlockSpec((4 * rows, near_count * PAIR), lambda i, side: (i, side[0]))
            ]
            * 3,
        ),
        out_shape=[out] * 3,
        input_output_aliases={2 + i: i for i in range(len(grads))},
        compiler_params=params(24),
        cost_estimate=cost(0, 6 * width * width),
        name="place",
    )(side, pieces, *grads)


def shards(tokens, wq, wk, wv, log_decay, neighbour_blocks, cot):
    rows, width = tokens.shape
    lin_scale = 1.0 / (DH * math.sqrt(rows))
    place = lax.axis_index(AX).astype(jnp.int32).reshape(1)
    core = lax.axis_index("c").astype(jnp.int32).reshape(1)

    prev_tokens = lax.ppermute(tokens, AX, [(i, i + 1) for i in range(DEVS - 1)])
    q, kv, pkv, run, runt, msg = project(
        tokens, prev_tokens, wq, wk, wv, log_decay, cot, lin_scale
    )
    got = lax.all_to_all(msg.reshape(DEVS, 16, PAIR), AX, 0, 0)
    near_out, dq, own, prev = near(
        place, neighbour_blocks, q, kv, pkv, cot, run, runt, lin_scale
    )
    states = scan(place, got, prev)
    tokt = flip(tokens, states)
    tokt8 = lax.all_to_all(jnp.broadcast_to(tokt[None], (8, *tokt.shape)), NEAR8, 0, 0)
    nxt = lax.ppermute(prev, AX, [(i + 1, i) for i in range(DEVS - 1)])
    states = lax.all_to_all(states.reshape(DEVS, 8, PAIR), AX, 0, 0)
    states = states.reshape(2, width // PAIR, DH, PAIR)
    layer, delta = join(near_out, dq, own, nxt, q, kv, cot, runt, states, tokt8, lin_scale)

    delta8 = lax.all_to_all(delta, NEAR8, 0, 0)
    tokens_grad = back(delta, wq, wk, wv)
    partial = outer(tokt8, delta8, tokens_grad)
    parts = lax.all_to_all(partial.reshape(16, width // 16, 3 * PAIR), FAR16, 0, 0)
    grad_norm = 1.0 / math.sqrt(rows * DEVS)
    piece = (jnp.sum(parts.astype(F32), axis=0) * grad_norm).astype(BF)
    plane = lax.all_to_all(jnp.broadcast_to(piece[None], (DEVS // 2, *piece.shape)), PLANE, 0, 0)
    other = lax.ppermute(plane, "c", [(0, 1), (1, 0)])
    shape = (4, 16, *piece.shape)
    grads = place_half(core, plane.reshape(shape))
    gq, gk, gv = place_half(1 - core, other.reshape(shape), grads)
    return layer, tokens_grad, gq, gk, gv


def solution(mesh):
    chips = Mesh(mesh.devices.reshape(2, 2, 4, 4, 2), AX)
    tok = P(AX, None)
    return jax.shard_map(
        shards,
        mesh=chips,
        in_specs=(tok, P(), P(), P(), P(None, AX), tok, tok),
        out_specs=(tok, tok, P(), P(), P()),
        check_vma=False,
    )
```

```python
import functools
import math

import jax
import jax.numpy as jnp
from jax import lax
from jax.experimental import pallas as pl
from jax.experimental.pallas import tpu as pltpu
from jax.sharding import Mesh
from jax.sharding import PartitionSpec as P

BF = jnp.bfloat16
F32 = jnp.float32
AX = ("yl", "c", "x", "z", "yh")
NEAR8 = ("c", "x")
FAR16 = ("yl", "z", "yh")
PLANE = ("x", "yl", "z", "yh")
SEG = 128
PAIR = 128
DH = 64
DEVS = 128
VMEM = pltpu.VMEM
HIGH = lax.Precision.HIGHEST


def dot(a, b, ca, cb, precision=None):
    return lax.dot_general(
        a, b, (((ca,), (cb,)), ((), ())), precision=precision, preferred_element_type=F32
    )


def iota(shape, axis):
    return lax.broadcasted_iota(jnp.int32, shape, axis)


def params(mib):
    return pltpu.CompilerParams(vmem_limit_bytes=mib << 20)


def cost(flops, moved, trans=0):
    return pl.CostEstimate(flops=flops, bytes_accessed=moved, transcendentals=trans)


CHUNK = 256


def project_kernel(lin_scale, tok, wq, wk, wv, decay, cot, q_out, kv_out, run_out, runt_out, msg, held, sems):
    width = tok.shape[1]
    chunks = width // CHUNK
    copies = []
    for step in range(chunks):
        for part, w in enumerate((wq, wk, wv)):
            copy = pltpu.make_async_copy(
                w.at[:, pl.ds(step * CHUNK, CHUNK)], held.at[part, step], sems.at[part, step]
            )
            copy.start()
            copies.append(copy)
    x = tok[...]
    ld = decay[...]
    heads = ld.shape[0]
    lower = (iota((SEG, SEG), 0) >= iota((SEG, SEG), 1)).astype(F32)
    runt = dot(lower, ld, 1, 1, HIGH)
    run = dot(ld, lower, 1, 1, HIGH)
    group = heads // chunks
    for step in range(chunks):
        runt_out[step] = runt[:, step * group : (step + 1) * group]
        run_out[step] = run[step * group : (step + 1) * group, :]
    head_of = iota((SEG, PAIR), 1) // DH
    rows = iota((8, PAIR), 0)
    lanes = iota((DH, PAIR), 1) < DH
    for step in range(chunks):
        for part in range(3):
            copies[step * 3 + part].wait()
        at = slice(step * CHUNK, (step + 1) * CHUNK)
        q = dot(x, held[0, step], 1, 0).astype(BF)
        k = dot(x, held[1, step], 1, 0).astype(BF)
        v = dot(x, held[2, step], 1, 0).astype(BF)
        q_out[:, at] = q
        kv_out[0, :, at] = k
        kv_out[1, :, at] = v
        for half in range(CHUNK // PAIR):
            cols = slice(half * PAIR, (half + 1) * PAIR)
            pair = step * (CHUNK // PAIR) + half
            run = jnp.where(
                head_of == 0, runt[:, 2 * pair : 2 * pair + 1], runt[:, 2 * pair + 1 : 2 * pair + 2]
            )
            total = run[SEG - 1 : SEG, :]
            grads = cot[:, pair * PAIR : (pair + 1) * PAIR].astype(F32)
            weighted = (v[:, cols].astype(F32) * jnp.exp(total - run)).astype(BF)
            scaled = (grads * jnp.exp(run)).astype(BF)
            full_s = dot(k[:, cols], weighted, 0, 0)
            full_g = dot(q[:, cols], scaled, 0, 0) * lin_scale
            high = total.astype(BF).astype(F32)
            mid = (total - high).astype(BF).astype(F32)
            low = total - high - mid
            tail = jnp.where(
                rows == 0, high, jnp.where(rows == 1, mid, jnp.where(rows == 2, low, 0.0))
            )
            tail = jnp.broadcast_to(tail[None], (8, 8, PAIR))
            for part, full in ((0, full_s), (1, full_g)):
                own = jnp.where(lanes, full[:DH], full[DH:]).reshape(8, 8, PAIR)
                sent = jnp.concatenate([own, tail], axis=1).reshape(PAIR, PAIR)
                msg[part, pair * PAIR : (pair + 1) * PAIR, :] = sent.astype(BF)


def project(tokens, wq, wk, wv, log_decay, cot, lin_scale):
    rows, width = tokens.shape
    heads = log_decay.shape[0]
    vmem = pl.BlockSpec(memory_space=VMEM)
    hbm = pl.BlockSpec(memory_space=pltpu.HBM)
    return pl.pallas_call(
        functools.partial(project_kernel, lin_scale),
        in_specs=[vmem, hbm, hbm, hbm, vmem, vmem],
        out_specs=[vmem] * 5,
        out_shape=[
            jax.ShapeDtypeStruct((rows, width), BF),
            jax.ShapeDtypeStruct((2, rows, width), BF),
            jax.ShapeDtypeStruct((width // CHUNK, heads * CHUNK // width, rows), F32),
            jax.ShapeDtypeStruct((width // CHUNK, rows, heads * CHUNK // width), F32),
            jax.ShapeDtypeStruct((2, width, PAIR), BF),
        ],
        scratch_shapes=[
            VMEM((3, width // CHUNK, width, CHUNK), BF),
            pltpu.SemaphoreType.DMA((3, width // CHUNK)),
        ],
        compiler_params=params(58),
        cost_estimate=cost(6 * rows * width * width, 6 * width * width + 12 * rows * width),
        name="project",
    )(tokens, wq, wk, wv, log_decay, cot)


def flip_kernel(tok, after, out):
    del after
    out[...] = tok[...].T


def flip(tokens, after):
    rows, width = tokens.shape
    return pl.pallas_call(
        flip_kernel,
        in_specs=[pl.BlockSpec(memory_space=VMEM), pl.BlockSpec(memory_space=pl.ANY)],
        out_specs=pl.BlockSpec(memory_space=VMEM),
        out_shape=jax.ShapeDtypeStruct((width, rows), BF),
        compiler_params=params(16),
        cost_estimate=cost(0, 4 * rows * width),
        name="flip",
    )(tokens, after)


def stack_kernel(*refs):
    out = refs[-1]
    for i in range(out.shape[0]):
        out[i] = refs[i][...]


def stack(parts, after):
    shape = parts[0].shape
    whole = pl.BlockSpec(memory_space=VMEM)
    return pl.pallas_call(
        stack_kernel,
        in_specs=[whole] * len(parts) + [pl.BlockSpec(memory_space=pl.ANY)],
        out_specs=whole,
        out_shape=jax.ShapeDtypeStruct((len(parts), *shape), BF),
        compiler_params=params(16),
        cost_estimate=cost(0, 4 * len(parts) * shape[0] * shape[1]),
        name="stack",
    )(*parts, after)


def scan_kernel(place, got, after, out, xs, decays, states):
    del after
    both = got[...].astype(F32)
    xs[...] = both[:, :8, :]
    total = both[:, 8:9, :] + both[:, 9:10, :] + both[:, 10:11, :]
    decays[...] = jnp.broadcast_to(jnp.exp(total), decays.shape)
    backward = place[0] >= DEVS // 2

    def one(i, state):
        at = jnp.where(backward, DEVS - 1 - i, i)
        states[at] = state
        return decays[at] * state + xs[at]

    lax.fori_loop(0, DEVS, one, jnp.zeros((8, PAIR), F32), unroll=8)
    out[...] = states[...].reshape(DEVS * 8, PAIR).astype(BF)


def scan(place, got, after):
    whole = pl.BlockSpec(memory_space=VMEM)
    return pl.pallas_call(
        scan_kernel,
        in_specs=[
            pl.BlockSpec(memory_space=pltpu.SMEM),
            whole,
            pl.BlockSpec(memory_space=pl.ANY),
        ],
        out_specs=whole,
        out_shape=jax.ShapeDtypeStruct((DEVS * 8, PAIR), BF),
        scratch_shapes=[VMEM((DEVS, 8, PAIR), F32)] * 3,
        compiler_params=params(24),
        cost_estimate=cost(2 * DEVS * 8 * PAIR, 4 * DEVS * 16 * PAIR),
        name="scan",
    )(place, got, after)


def near_kernel(lin_scale, place, blocks, q_ref, kv, pkv, cot, run, runt, out, dq_out, own, prev):
    soft_scale = 1.0 / math.sqrt(DH)
    n_own = jnp.int32(0)
    n_prev = jnp.int32(0)
    for j in range(blocks.shape[1]):
        n_own += (blocks[0, j] == place[0]).astype(jnp.int32)
        n_prev += (blocks[0, j] == place[0] - 1).astype(jnp.int32)
    is_own = iota((1, 2 * SEG), 1) < SEG
    times = jnp.where(is_own, n_own, n_prev)
    bias = jnp.where(times > 0, 0.0, -1e30)
    times = times.astype(F32)
    head_of = iota((SEG, PAIR), 1) // DH
    head_of2 = iota((2 * SEG, PAIR), 1) // DH
    lower = iota((SEG, SEG), 0) >= iota((SEG, SEG), 1)
    zero = jnp.zeros((), BF)
    for pair in range(q_ref.shape[1] // PAIR):
        at = slice(pair * PAIR, (pair + 1) * PAIR)
        q = q_ref[:, at]
        g = cot[:, at]
        kk = jnp.concatenate([kv[0, :, at], pkv[0, :, at]], axis=0)
        vv = jnp.concatenate([kv[1, :, at], pkv[1, :, at]], axis=0)
        res = []
        for i in range(2):
            head = pair * 2 + i
            mine = head_of == i
            col = runt[0, :, head : head + 1]
            row = run[0, head : head + 1, :]
            dec = jnp.where(lower, jnp.exp(jnp.minimum(col - row, 0.0)), 0.0) * lin_scale
            scores = dot(jnp.where(mine, q, zero), kk, 1, 1)
            pgrad = dot(jnp.where(mine, g, zero), vv, 1, 1)
            logits = scores * soft_scale + bias
            peak = jnp.max(logits, axis=1, keepdims=True)
            terms = jnp.exp(logits - peak) * times
            probs = terms * (1.0 / jnp.sum(terms, axis=1, keepdims=True))
            inner = jnp.sum(probs * pgrad, axis=1, keepdims=True)
            dlog = probs * (pgrad - inner) * soft_scale
            a = jnp.concatenate(
                [probs[:, :SEG] + scores[:, :SEG] * dec, probs[:, SEG:]], axis=1
            ).astype(BF)
            b = jnp.concatenate(
                [dlog[:, :SEG] + pgrad[:, :SEG] * dec, dlog[:, SEG:]], axis=1
            ).astype(BF)
            res.append((dot(a, vv, 1, 0), dot(b, kk, 1, 0), dot(b, q, 0, 0), dot(a, g, 0, 0)))
        out[:, at] = jnp.where(head_of == 0, res[0][0], res[1][0])
        dq_out[:, at] = jnp.where(head_of == 0, res[0][1], res[1][1])
        for part in range(2):
            sums = jnp.where(head_of2 == 0, res[0][2 + part], res[1][2 + part])
            own[part, :, at] = sums[:SEG]
            prev[part, :, at] = sums[SEG:].astype(BF)


def near(place, blocks, q, kv, pkv, cot, run, runt, lin_scale):
    rows, width = q.shape
    heads = run.shape[1]
    smem = pl.BlockSpec(memory_space=pltpu.SMEM)
    col = pl.BlockSpec((rows, CHUNK), lambda i: (0, i))
    two = pl.BlockSpec((2, rows, CHUNK), lambda i: (0, 0, i))
    return pl.pallas_call(
        functools.partial(near_kernel, lin_scale),
        grid=(width // CHUNK,),
        in_specs=[
            smem,
            smem,
            col,
            two,
            two,
            col,
            pl.BlockSpec((1, heads, rows), lambda i: (i, 0, 0)),
            pl.BlockSpec((1, rows, heads), lambda i: (i, 0, 0)),
        ],
        out_specs=[col, col, two, two],
        out_shape=[
            jax.ShapeDtypeStruct((rows, width), F32),
            jax.ShapeDtypeStruct((rows, width), F32),
            jax.ShapeDtypeStruct((2, rows, width), F32),
            jax.ShapeDtypeStruct((2, rows, width), BF),
        ],
        compiler_params=params(58),
        cost_estimate=cost(4000 * 1000 * 1000, 16 * 1000 * 1000, 1000 * 1000),
        name="near",
    )(place, blocks, q, kv, pkv, cot, run, runt)


def join_kernel(lin_scale, near_out, dq_in, own, nxt, q, kv, cot, runt, states, *rest):
    layer, delta = rest[-2:]
    head_of = iota((SEG, PAIR), 1) // DH
    diag = iota((PAIR, PAIR), 0) // DH == iota((PAIR, PAIR), 1) // DH
    zero = jnp.zeros((), BF)
    for pair in range(q.shape[1] // PAIR):
        at = slice(pair * PAIR, (pair + 1) * PAIR)
        run = jnp.where(
            head_of == 0,
            runt[0, :, 2 * pair : 2 * pair + 1],
            runt[0, :, 2 * pair + 1 : 2 * pair + 2],
        )
        growth = jnp.exp(run) * lin_scale
        fading = jnp.exp(run[SEG - 1 : SEG, :] - run)
        before, after = (
            jnp.where(diag, jnp.concatenate([states[part, pair]] * 2, axis=0), zero)
            for part in range(2)
        )
        layer[:, at] = (near_out[:, at] + growth * dot(q[:, at], before, 1, 0)).astype(BF)
        dq = dq_in[:, at] + growth * dot(cot[:, at], before, 1, 1)
        dk = own[0, :, at] + fading * dot(kv[1, :, at], after, 1, 1) + nxt[0, :, at].astype(F32)
        dv = own[1, :, at] + fading * dot(kv[0, :, at], after, 1, 0) + nxt[1, :, at].astype(F32)
        delta[pair, :, :PAIR] = dq.astype(BF)
        delta[pair, :, PAIR : 2 * PAIR] = dk.astype(BF)
        delta[pair, :, 2 * PAIR :] = dv.astype(BF)


def join(near_out, dq, own, nxt, q, kv, cot, runt, states, after, lin_scale):
    rows, width = q.shape
    pairs = width // PAIR
    col = pl.BlockSpec((rows, CHUNK), lambda i: (0, i))
    two = pl.BlockSpec((2, rows, CHUNK), lambda i: (0, 0, i))
    return pl.pallas_call(
        functools.partial(join_kernel, lin_scale),
        grid=(width // CHUNK,),
        in_specs=[
            col,
            col,
            two,
            two,
            col,
            two,
            col,
            pl.BlockSpec((1, rows, runt.shape[2]), lambda i: (i, 0, 0)),
            pl.BlockSpec((2, CHUNK // PAIR, DH, PAIR), lambda i: (0, i, 0, 0)),
        ]
        + [pl.BlockSpec(memory_space=pl.ANY)] * len(after),
        out_specs=[col, pl.BlockSpec((CHUNK // PAIR, rows, 3 * PAIR), lambda i: (i, 0, 0))],
        out_shape=[
            jax.ShapeDtypeStruct((rows, width), BF),
            jax.ShapeDtypeStruct((pairs, rows, 3 * PAIR), BF),
        ],
        compiler_params=params(58),
        cost_estimate=cost(8 * rows * PAIR * PAIR * pairs, 24 * rows * width),
        name="join",
    )(near_out, dq, own, nxt, q, kv, cot, runt, states, *after)


def back_kernel(delta, wq, wk, wv, out, total):
    step = pl.program_id(0)

    @pl.when(step == 0)
    def _():
        total[...] = jnp.zeros_like(total)

    acc = total[...]
    for part, w in enumerate((wq, wk, wv)):
        for half in range(2):
            acc += dot(
                delta[half, :, part * PAIR : (part + 1) * PAIR],
                w[:, half * PAIR : (half + 1) * PAIR],
                1,
                1,
            )
    total[...] = acc

    @pl.when(step == pl.num_programs(0) - 1)
    def _():
        out[...] = acc.astype(BF)


def back(delta, wq, wk, wv):
    pairs, rows, _ = delta.shape
    width = wq.shape[0]
    weight = pl.BlockSpec((width, 2 * PAIR), lambda i: (0, i))
    return pl.pallas_call(
        back_kernel,
        grid=(pairs // 2,),
        in_specs=[pl.BlockSpec((2, rows, 3 * PAIR), lambda i: (i, 0, 0)), weight, weight, weight],
        out_specs=pl.BlockSpec((rows, width), lambda i: (0, 0)),
        out_shape=jax.ShapeDtypeStruct((rows, width), BF),
        scratch_shapes=[VMEM((rows, width), F32)],
        compiler_params=params(58),
        cost_estimate=cost(6 * rows * width * width, 6 * width * width + 8 * rows * width),
        name="back",
    )(delta, wq, wk, wv)


def outer_kernel(core, at_x, mine, theirs, delta, after, out):
    del after
    near_x = mine.shape[0]
    left, right = [], []
    for tokt, c in ((mine, core[0]), (theirs, 1 - core[0])):
        for i in range(near_x):
            left.append(tokt[i])
            right.append(delta[c * near_x + lax.rem(at_x[0] + near_x - i, near_x)])
    left = jnp.concatenate(left, axis=1)
    out[...] = dot(left, jnp.concatenate(right, axis=0), 1, 0).astype(BF)


def outer(core, at_x, mine, theirs, delta, after):
    near_count, rows, cols = delta.shape
    width = mine.shape[1]
    smem = pl.BlockSpec(memory_space=pltpu.SMEM)
    tok = pl.BlockSpec((near_count // 2, width // 4, rows), lambda i: (0, i, 0))
    return pl.pallas_call(
        outer_kernel,
        grid=(4,),
        in_specs=[
            smem,
            smem,
            tok,
            tok,
            pl.BlockSpec((near_count, rows, cols), lambda i: (0, 0, 0)),
            pl.BlockSpec(memory_space=pl.ANY),
        ],
        out_specs=pl.BlockSpec((width // 4, cols), lambda i: (i, 0)),
        out_shape=jax.ShapeDtypeStruct((width, cols), BF),
        compiler_params=params(58),
        cost_estimate=cost(
            2 * near_count * rows * cols * width, 2 * near_count * rows * (width + cols)
        ),
        name="outer",
    )(core, at_x, mine, theirs, delta, after)


def place_kernel(side, pieces, *rest):
    del side
    for x in range(pieces.shape[0]):
        for r in range(pieces.shape[1]):
            rows = slice(r * pieces.shape[2], (r + 1) * pieces.shape[2])
            for part, o in enumerate(rest[-3:]):
                o[rows, x * PAIR : (x + 1) * PAIR] = pieces[x, r, :, part * PAIR : (part + 1) * PAIR]


def place_half(side, pieces, grads=()):
    near_count, blocks, rows, cols = pieces.shape
    width = blocks * rows
    out = jax.ShapeDtypeStruct((width, width), BF)
    return pl.pallas_call(
        place_kernel,
        grid_spec=pltpu.PrefetchScalarGridSpec(
            num_scalar_prefetch=1,
            grid=(blocks // 4,),
            in_specs=[pl.BlockSpec((near_count, 4, rows, cols), lambda i, side: (0, i, 0, 0))]
            + [pl.BlockSpec(memory_space=pl.ANY)] * len(grads),
            out_specs=[
                pl.BlockSpec((4 * rows, near_count * PAIR), lambda i, side: (i, side[0]))
            ]
            * 3,
        ),
        out_shape=[out] * 3,
        input_output_aliases={2 + i: i for i in range(len(grads))},
        compiler_params=params(24),
        cost_estimate=cost(0, 6 * width * width),
        name="place",
    )(side, pieces, *grads)


def shards(tokens, wq, wk, wv, log_decay, neighbour_blocks, cot):
    rows, width = tokens.shape
    lin_scale = 1.0 / (DH * math.sqrt(rows))
    place = lax.axis_index(AX).astype(jnp.int32).reshape(1)
    core = lax.axis_index("c").astype(jnp.int32).reshape(1)

    at_x = lax.axis_index("x").astype(jnp.int32).reshape(1)
    swap = [(0, 1), (1, 0)]
    q, kv, run, runt, msg = project(tokens, wq, wk, wv, log_decay, cot, lin_scale)
    pkv = lax.ppermute(kv, AX, [(i, i + 1) for i in range(DEVS - 1)])
    got = lax.all_to_all(msg.reshape(DEVS, 16, PAIR), AX, 0, 0)
    near_out, dq, own, prev = near(
        place, neighbour_blocks, q, kv, pkv, cot, run, runt, lin_scale
    )
    nxt = lax.ppermute(prev, AX, [(i + 1, i) for i in range(DEVS - 1)])
    states = scan(place, got, prev)
    tokt = flip(tokens, prev)
    around = [lax.ppermute(tokt, "x", [(i, (i + d) % 4) for i in range(4)]) for d in (1, 2, 3)]
    states = lax.all_to_all(states.reshape(DEVS, 8, PAIR), AX, 0, 0)
    states = states.reshape(2, width // PAIR, DH, PAIR)
    layer, delta = join(near_out, dq, own, nxt, q, kv, cot, runt, states, [], lin_scale)

    delta8 = lax.all_to_all(delta, NEAR8, 0, 0)
    mine = stack([tokt, *around], delta)
    theirs = lax.ppermute(mine, "c", swap)
    tokens_grad = back(delta, wq, wk, wv)
    partial = outer(core, at_x, mine, theirs, delta8, tokens_grad)
    parts = lax.all_to_all(partial.reshape(16, width // 16, 3 * PAIR), FAR16, 0, 0)
    grad_norm = 1.0 / math.sqrt(rows * DEVS)
    piece = (jnp.sum(parts.astype(F32), axis=0) * grad_norm).astype(BF)
    plane = lax.all_to_all(jnp.broadcast_to(piece[None], (DEVS // 2, *piece.shape)), PLANE, 0, 0)
    other = lax.ppermute(plane, "c", swap)
    shape = (4, 16, *piece.shape)
    grads = place_half(core, plane.reshape(shape))
    gq, gk, gv = place_half(1 - core, other.reshape(shape), grads)
    return layer, tokens_grad, gq, gk, gv


def solution(mesh):
    chips = Mesh(mesh.devices.reshape(2, 2, 4, 4, 2), AX)
    tok = P(AX, None)
    return jax.shard_map(
        shards,
        mesh=chips,
        in_specs=(tok, P(), P(), P(), P(None, AX), tok, tok),
        out_specs=(tok, tok, P(), P(), P()),
        check_vma=False,
    )
```

```python
import functools
import math

import jax
import jax.numpy as jnp
from jax import lax
from jax.experimental import pallas as pl
from jax.experimental.pallas import tpu as pltpu
from jax.sharding import Mesh
from jax.sharding import PartitionSpec as P

BF = jnp.bfloat16
F32 = jnp.float32
AX = ("yl", "c", "x", "z", "yh")
NEAR8 = ("c", "x")
FAR16 = ("yl", "z", "yh")
PLANE = ("x", "yl", "z", "yh")
SEG = 128
PAIR = 128
DH = 64
DEVS = 128
VMEM = pltpu.VMEM
HIGH = lax.Precision.HIGHEST


def dot(a, b, ca, cb, precision=None):
    return lax.dot_general(
        a, b, (((ca,), (cb,)), ((), ())), precision=precision, preferred_element_type=F32
    )


def iota(shape, axis):
    return lax.broadcasted_iota(jnp.int32, shape, axis)


def params(mib):
    return pltpu.CompilerParams(vmem_limit_bytes=mib << 20)


def cost(flops, moved, trans=0):
    return pl.CostEstimate(flops=flops, bytes_accessed=moved, transcendentals=trans)


CHUNK = 256
WIDE = 512


def pair_lanes(columns, pair):
    shape = (columns.shape[0], PAIR)
    return jnp.where(
        iota(shape, 1) < DH,
        columns[:, 2 * pair : 2 * pair + 1],
        columns[:, 2 * pair + 1 : 2 * pair + 2],
    )


def project_kernel(lin_scale, tok, wq, wk, wv, decay, cot, q_out, kv_out, run_out, runt_out, msg, held, sems):
    width = tok.shape[1]
    wide = held.shape[3]
    copies = []
    for step in range(width // wide):
        for part, w in enumerate((wq, wk, wv)):
            copy = pltpu.make_async_copy(
                w.at[:, pl.ds(step * wide, wide)], held.at[part, step], sems.at[part, step]
            )
            copy.start()
            copies.append(copy)
    x = tok[...]
    ld = decay[...]
    lower = (iota((SEG, SEG), 0) >= iota((SEG, SEG), 1)).astype(F32)
    runt = dot(lower, ld, 1, 1, HIGH)
    run = dot(ld, lower, 1, 1, HIGH)
    group = ld.shape[0] // run_out.shape[0]
    for step in range(run_out.shape[0]):
        runt_out[step] = runt[:, step * group : (step + 1) * group]
        run_out[step] = run[step * group : (step + 1) * group, :]
    rows = iota((8, PAIR), 0)
    first = iota((DH, PAIR), 1) < DH
    for step in range(width // wide):
        for part in range(3):
            copies[step * 3 + part].wait()
        at = slice(step * wide, (step + 1) * wide)
        q = dot(x, held[0, step], 1, 0).astype(BF)
        k = dot(x, held[1, step], 1, 0).astype(BF)
        v = dot(x, held[2, step], 1, 0).astype(BF)
        q_out[:, at] = q
        kv_out[0, :, at] = k
        kv_out[1, :, at] = v
        here = []
        for part in range(wide // PAIR):
            cols = slice(part * PAIR, (part + 1) * PAIR)
            pair = step * (wide // PAIR) + part
            lanes = pair_lanes(runt, pair)
            total = lanes[SEG - 1 : SEG, :]
            g = cot[:, pair * PAIR : (pair + 1) * PAIR].astype(F32)
            weighted = (v[:, cols].astype(F32) * jnp.exp(total - lanes)).astype(BF)
            scaled = (g * jnp.exp(lanes)).astype(BF)
            states = (
                dot(k[:, cols], weighted, 0, 0),
                dot(q[:, cols], scaled, 0, 0) * lin_scale,
            )
            here.append((pair, total, states))
        for pair, total, states in here:
            high = total.astype(BF).astype(F32)
            mid = (total - high).astype(BF).astype(F32)
            low = total - high - mid
            tail = jnp.where(
                rows == 0, high, jnp.where(rows == 1, mid, jnp.where(rows == 2, low, 0.0))
            )
            tail = jnp.broadcast_to(tail[None], (8, 8, PAIR))
            for part, full in enumerate(states):
                own = jnp.where(first, full[:DH], full[DH:]).reshape(8, 8, PAIR)
                sent = jnp.concatenate([own, tail], axis=1).reshape(PAIR, PAIR)
                msg[part, pair * PAIR : (pair + 1) * PAIR, :] = sent.astype(BF)


def project(tokens, wq, wk, wv, log_decay, cot, lin_scale):
    rows, width = tokens.shape
    heads = log_decay.shape[0]
    chunks = width // CHUNK
    wide = WIDE
    vmem = pl.BlockSpec(memory_space=VMEM)
    hbm = pl.BlockSpec(memory_space=pltpu.HBM)
    return pl.pallas_call(
        functools.partial(project_kernel, lin_scale),
        in_specs=[vmem, hbm, hbm, hbm, vmem, vmem],
        out_specs=[vmem] * 5,
        out_shape=[
            jax.ShapeDtypeStruct((rows, width), BF),
            jax.ShapeDtypeStruct((2, rows, width), BF),
            jax.ShapeDtypeStruct((chunks, heads // chunks, rows), F32),
            jax.ShapeDtypeStruct((chunks, rows, heads // chunks), F32),
            jax.ShapeDtypeStruct((2, width, PAIR), BF),
        ],
        scratch_shapes=[
            VMEM((3, width // wide, width, wide), BF),
            pltpu.SemaphoreType.DMA((3, width // wide)),
        ],
        compiler_params=params(58),
        cost_estimate=cost(6 * rows * width * width, 6 * width * width + 12 * rows * width),
        name="project",
    )(tokens, wq, wk, wv, log_decay, cot)


def prior_kernel(tok, wk, wv, after, out, held, sems):
    del after
    copies = [
        pltpu.make_async_copy(w, held.at[part], sems.at[part]) for part, w in enumerate((wk, wv))
    ]
    for copy in copies:
        copy.start()
    for part in range(2):
        copies[part].wait()
        out[part] = dot(tok[...], held[part], 1, 0).astype(BF)


def prior(tokens, wk, wv, after):
    rows, width = tokens.shape
    vmem = pl.BlockSpec(memory_space=VMEM)
    hbm = pl.BlockSpec(memory_space=pltpu.HBM)
    return pl.pallas_call(
        prior_kernel,
        in_specs=[vmem, hbm, hbm, hbm],
        out_specs=vmem,
        out_shape=jax.ShapeDtypeStruct((2, rows, width), BF),
        scratch_shapes=[
            VMEM((2, width, width), BF),
            pltpu.SemaphoreType.DMA((2,)),
        ],
        compiler_params=params(58),
        cost_estimate=cost(4 * rows * width * width, 4 * width * width + 6 * rows * width),
        name="prior",
    )(tokens, wk, wv, after)


def flip_kernel(tok, after, out):
    del after
    out[...] = tok[...].T


def flip(tokens, after):
    rows, width = tokens.shape
    return pl.pallas_call(
        flip_kernel,
        in_specs=[pl.BlockSpec(memory_space=VMEM), pl.BlockSpec(memory_space=pl.ANY)],
        out_specs=pl.BlockSpec(memory_space=VMEM),
        out_shape=jax.ShapeDtypeStruct((width, rows), BF),
        compiler_params=params(16),
        cost_estimate=cost(0, 4 * rows * width),
        name="flip",
    )(tokens, after)


def stack_kernel(*refs):
    out = refs[-1]
    for i in range(out.shape[0]):
        out[i] = refs[i][...]


def stack(parts, after):
    shape = parts[0].shape
    whole = pl.BlockSpec(memory_space=VMEM)
    return pl.pallas_call(
        stack_kernel,
        in_specs=[whole] * len(parts) + [pl.BlockSpec(memory_space=pl.ANY)],
        out_specs=whole,
        out_shape=jax.ShapeDtypeStruct((len(parts), *shape), BF),
        compiler_params=params(16),
        cost_estimate=cost(0, 4 * len(parts) * shape[0] * shape[1]),
        name="stack",
    )(*parts, after)


def scan_kernel(place, got, after, out, xs, decays, states):
    del after
    both = got[...].astype(F32)
    xs[...] = both[:, :8, :]
    total = both[:, 8:9, :] + both[:, 9:10, :] + both[:, 10:11, :]
    decays[...] = jnp.broadcast_to(jnp.exp(total), decays.shape)
    backward = place[0] >= DEVS // 2

    def one(i, state):
        at = jnp.where(backward, DEVS - 1 - i, i)
        states[at] = state
        return decays[at] * state + xs[at]

    lax.fori_loop(0, DEVS, one, jnp.zeros((8, PAIR), F32), unroll=8)
    out[...] = states[...].reshape(DEVS * 8, PAIR).astype(BF)


def scan(place, got, after):
    whole = pl.BlockSpec(memory_space=VMEM)
    return pl.pallas_call(
        scan_kernel,
        in_specs=[
            pl.BlockSpec(memory_space=pltpu.SMEM),
            whole,
            pl.BlockSpec(memory_space=pl.ANY),
        ],
        out_specs=whole,
        out_shape=jax.ShapeDtypeStruct((DEVS * 8, PAIR), BF),
        scratch_shapes=[VMEM((DEVS, 8, PAIR), F32)] * 3,
        compiler_params=params(24),
        cost_estimate=cost(2 * DEVS * 8 * PAIR, 4 * DEVS * 16 * PAIR),
        name="scan",
    )(place, got, after)


def near_kernel(lin_scale, place, blocks, q_ref, kv, pkv, cot, run, runt, out, dq_out, own, prev, mark):
    mark[...] = jnp.zeros_like(mark)
    soft_scale = 1.0 / math.sqrt(DH)
    n_own = jnp.int32(0)
    n_prev = jnp.int32(0)
    for j in range(blocks.shape[1]):
        n_own += (blocks[0, j] == place[0]).astype(jnp.int32)
        n_prev += (blocks[0, j] == place[0] - 1).astype(jnp.int32)
    is_own = iota((1, 2 * SEG), 1) < SEG
    times = jnp.where(is_own, n_own, n_prev)
    bias = jnp.where(times > 0, 0.0, -1e30)
    times = times.astype(F32)
    head_of = iota((SEG, PAIR), 1) // DH
    head_of2 = iota((2 * SEG, PAIR), 1) // DH
    lower = iota((SEG, SEG), 0) >= iota((SEG, SEG), 1)
    zero = jnp.zeros((), BF)
    pairs = q_ref.shape[1] // PAIR
    work = []
    for pair in range(pairs):
        at = slice(pair * PAIR, (pair + 1) * PAIR)
        q = q_ref[:, at]
        g = cot[:, at]
        kk = jnp.concatenate([kv[0, :, at], pkv[0, :, at]], axis=0)
        vv = jnp.concatenate([kv[1, :, at], pkv[1, :, at]], axis=0)
        for i in range(2):
            mine = head_of == i
            work.append(
                (
                    dot(jnp.where(mine, q, zero), kk, 1, 1),
                    dot(jnp.where(mine, g, zero), vv, 1, 1),
                )
            )
    mats = []
    for head in range(2 * pairs):
        scores, pgrad = work[head]
        col = runt[0, :, head : head + 1]
        row = run[0, head : head + 1, :]
        dec = jnp.where(lower, jnp.exp(jnp.minimum(col - row, 0.0)), 0.0) * lin_scale
        logits = scores * soft_scale + bias
        peak = jnp.max(logits, axis=1, keepdims=True)
        terms = jnp.exp(logits - peak) * times
        probs = terms * (1.0 / jnp.sum(terms, axis=1, keepdims=True))
        inner = jnp.sum(probs * pgrad, axis=1, keepdims=True)
        dlog = probs * (pgrad - inner) * soft_scale
        a = jnp.concatenate([probs[:, :SEG] + scores[:, :SEG] * dec, probs[:, SEG:]], axis=1)
        b = jnp.concatenate([dlog[:, :SEG] + pgrad[:, :SEG] * dec, dlog[:, SEG:]], axis=1)
        mats.append((a.astype(BF), b.astype(BF)))
    for pair in range(pairs):
        at = slice(pair * PAIR, (pair + 1) * PAIR)
        q = q_ref[:, at]
        g = cot[:, at]
        kk = jnp.concatenate([kv[0, :, at], pkv[0, :, at]], axis=0)
        vv = jnp.concatenate([kv[1, :, at], pkv[1, :, at]], axis=0)
        qt = q.T
        gt = g.T
        res = []
        for i in range(2):
            a, b = mats[2 * pair + i]
            half = slice(i * DH, (i + 1) * DH)
            res.append((dot(a, vv, 1, 0), dot(b, kk, 1, 0), dot(qt[half], b, 1, 0), dot(gt[half], a, 1, 0)))
        out[:, at] = jnp.where(head_of == 0, res[0][0], res[1][0])
        dq_out[:, at] = jnp.where(head_of == 0, res[0][1], res[1][1])
        for part in range(2):
            sums = jnp.concatenate([res[0][2 + part], res[1][2 + part]], axis=0).T
            own[part, :, at] = sums[:SEG]
            prev[part, :, at] = sums[SEG:].astype(BF)


def near(place, blocks, q, kv, pkv, cot, run, runt, lin_scale):
    rows, width = q.shape
    heads = run.shape[1]
    smem = pl.BlockSpec(memory_space=pltpu.SMEM)
    col = pl.BlockSpec((rows, CHUNK), lambda i: (0, i))
    two = pl.BlockSpec((2, rows, CHUNK), lambda i: (0, 0, i))
    return pl.pallas_call(
        functools.partial(near_kernel, lin_scale),
        grid=(width // CHUNK,),
        in_specs=[
            smem,
            smem,
            col,
            two,
            two,
            col,
            pl.BlockSpec((1, heads, rows), lambda i: (i, 0, 0)),
            pl.BlockSpec((1, rows, heads), lambda i: (i, 0, 0)),
        ],
        out_specs=[col, col, two, two, pl.BlockSpec((8, PAIR), lambda i: (0, 0))],
        out_shape=[
            jax.ShapeDtypeStruct((rows, width), F32),
            jax.ShapeDtypeStruct((rows, width), F32),
            jax.ShapeDtypeStruct((2, rows, width), F32),
            jax.ShapeDtypeStruct((2, rows, width), BF),
            jax.ShapeDtypeStruct((8, PAIR), F32),
        ],
        compiler_params=params(58),
        cost_estimate=cost(4000 * 1000 * 1000, 16 * 1000 * 1000, 1000 * 1000),
        name="near",
    )(place, blocks, q, kv, pkv, cot, run, runt)


def join_kernel(lin_scale, near_out, dq_in, own, nxt, q, kv, cot, runt, states, *rest):
    layer, delta = rest[-2:]
    head_of = iota((SEG, PAIR), 1) // DH
    diag = iota((PAIR, PAIR), 0) // DH == iota((PAIR, PAIR), 1) // DH
    zero = jnp.zeros((), BF)
    pairs = q.shape[1] // PAIR
    work = []
    for pair in range(pairs):
        at = slice(pair * PAIR, (pair + 1) * PAIR)
        before, after = (
            jnp.where(diag, jnp.concatenate([states[part, pair]] * 2, axis=0), zero)
            for part in range(2)
        )
        work.append(
            (
                dot(q[:, at], before, 1, 0),
                dot(cot[:, at], before, 1, 1),
                dot(kv[1, :, at], after, 1, 1),
                dot(kv[0, :, at], after, 1, 0),
            )
        )
    for pair in range(pairs):
        at = slice(pair * PAIR, (pair + 1) * PAIR)
        run = jnp.where(
            head_of == 0,
            runt[pair // 2, :, 2 * (pair % 2) : 2 * (pair % 2) + 1],
            runt[pair // 2, :, 2 * (pair % 2) + 1 : 2 * (pair % 2) + 2],
        )
        growth = jnp.exp(run) * lin_scale
        fading = jnp.exp(run[SEG - 1 : SEG, :] - run)
        from_q, from_g, from_v, from_k = work[pair]
        layer[:, at] = (near_out[:, at] + growth * from_q).astype(BF)
        dq = dq_in[:, at] + growth * from_g
        dk = own[0, :, at] + fading * from_v + nxt[0, :, at].astype(F32)
        dv = own[1, :, at] + fading * from_k + nxt[1, :, at].astype(F32)
        delta[pair, :, :PAIR] = dq.astype(BF)
        delta[pair, :, PAIR : 2 * PAIR] = dk.astype(BF)
        delta[pair, :, 2 * PAIR :] = dv.astype(BF)


def join(near_out, dq, own, nxt, q, kv, cot, runt, states, after, lin_scale):
    rows, width = q.shape
    pairs = width // PAIR
    wide = 2 * CHUNK
    col = pl.BlockSpec((rows, wide), lambda i: (0, i))
    two = pl.BlockSpec((2, rows, wide), lambda i: (0, 0, i))
    return pl.pallas_call(
        functools.partial(join_kernel, lin_scale),
        grid=(width // wide,),
        in_specs=[
            col,
            col,
            two,
            two,
            col,
            two,
            col,
            pl.BlockSpec((2, rows, runt.shape[2]), lambda i: (i, 0, 0)),
            pl.BlockSpec((2, wide // PAIR, DH, PAIR), lambda i: (0, i, 0, 0)),
        ]
        + [pl.BlockSpec(memory_space=pl.ANY)] * len(after),
        out_specs=[col, pl.BlockSpec((wide // PAIR, rows, 3 * PAIR), lambda i: (i, 0, 0))],
        out_shape=[
            jax.ShapeDtypeStruct((rows, width), BF),
            jax.ShapeDtypeStruct((pairs, rows, 3 * PAIR), BF),
        ],
        compiler_params=params(58),
        cost_estimate=cost(8 * rows * PAIR * PAIR * pairs, 24 * rows * width),
        name="join",
    )(near_out, dq, own, nxt, q, kv, cot, runt, states, *after)


def back_kernel(delta, wq, wk, wv, out, total):
    step = pl.program_id(0)

    @pl.when(step == 0)
    def _():
        total[...] = jnp.zeros_like(total)

    acc = total[...]
    for part, w in enumerate((wq, wk, wv)):
        for half in range(2):
            acc += dot(
                delta[half, :, part * PAIR : (part + 1) * PAIR],
                w[:, half * PAIR : (half + 1) * PAIR],
                1,
                1,
            )
    total[...] = acc

    @pl.when(step == pl.num_programs(0) - 1)
    def _():
        out[...] = acc.astype(BF)


def back(delta, wq, wk, wv):
    pairs, rows, _ = delta.shape
    width = wq.shape[0]
    weight = pl.BlockSpec((width, 2 * PAIR), lambda i: (0, i))
    return pl.pallas_call(
        back_kernel,
        grid=(pairs // 2,),
        in_specs=[pl.BlockSpec((2, rows, 3 * PAIR), lambda i: (i, 0, 0)), weight, weight, weight],
        out_specs=pl.BlockSpec((rows, width), lambda i: (0, 0)),
        out_shape=jax.ShapeDtypeStruct((rows, width), BF),
        scratch_shapes=[VMEM((rows, width), F32)],
        compiler_params=params(58),
        cost_estimate=cost(6 * rows * width * width, 6 * width * width + 8 * rows * width),
        name="back",
    )(delta, wq, wk, wv)


def outer_kernel(core, at_x, mine, theirs, delta, after, out):
    del after
    near_x = mine.shape[0]
    left, right = [], []
    for tokt, c in ((mine, core[0]), (theirs, 1 - core[0])):
        for i in range(near_x):
            left.append(tokt[i])
            right.append(delta[c * near_x + lax.rem(at_x[0] + near_x - i, near_x)])
    left = jnp.concatenate(left, axis=1)
    out[...] = dot(left, jnp.concatenate(right, axis=0), 1, 0).astype(BF)


def outer(core, at_x, mine, theirs, delta, after):
    near_count, rows, cols = delta.shape
    width = mine.shape[1]
    smem = pl.BlockSpec(memory_space=pltpu.SMEM)
    tok = pl.BlockSpec((near_count // 2, width // 2, rows), lambda i: (0, i, 0))
    return pl.pallas_call(
        outer_kernel,
        grid=(2,),
        in_specs=[
            smem,
            smem,
            tok,
            tok,
            pl.BlockSpec((near_count, rows, cols), lambda i: (0, 0, 0)),
            pl.BlockSpec(memory_space=pl.ANY),
        ],
        out_specs=pl.BlockSpec((width // 2, cols), lambda i: (i, 0)),
        out_shape=jax.ShapeDtypeStruct((width, cols), BF),
        compiler_params=params(58),
        cost_estimate=cost(
            2 * near_count * rows * cols * width, 2 * near_count * rows * (width + cols)
        ),
        name="outer",
    )(core, at_x, mine, theirs, delta, after)


def place_kernel(side, pieces, *rest):
    del side
    for x in range(pieces.shape[0]):
        for r in range(pieces.shape[1]):
            rows = slice(r * pieces.shape[2], (r + 1) * pieces.shape[2])
            for part, o in enumerate(rest[-3:]):
                o[rows, x * PAIR : (x + 1) * PAIR] = pieces[x, r, :, part * PAIR : (part + 1) * PAIR]


def place_half(side, pieces, grads=()):
    near_count, blocks, rows, cols = pieces.shape
    width = blocks * rows
    out = jax.ShapeDtypeStruct((width, width), BF)
    return pl.pallas_call(
        place_kernel,
        grid_spec=pltpu.PrefetchScalarGridSpec(
            num_scalar_prefetch=1,
            grid=(blocks // 4,),
            in_specs=[pl.BlockSpec((near_count, 4, rows, cols), lambda i, side: (0, i, 0, 0))]
            + [pl.BlockSpec(memory_space=pl.ANY)] * len(grads),
            out_specs=[
                pl.BlockSpec((4 * rows, near_count * PAIR), lambda i, side: (i, side[0]))
            ]
            * 3,
        ),
        out_shape=[out] * 3,
        input_output_aliases={2 + i: i for i in range(len(grads))},
        compiler_params=params(24),
        cost_estimate=cost(0, 6 * width * width),
        name="place",
    )(side, pieces, *grads)


def shards(tokens, wq, wk, wv, log_decay, neighbour_blocks, cot):
    rows, width = tokens.shape
    lin_scale = 1.0 / (DH * math.sqrt(rows))
    place = lax.axis_index(AX).astype(jnp.int32).reshape(1)
    core = lax.axis_index("c").astype(jnp.int32).reshape(1)

    at_x = lax.axis_index("x").astype(jnp.int32).reshape(1)
    swap = [(0, 1), (1, 0)]
    prev_tokens = lax.ppermute(tokens, AX, [(i, i + 1) for i in range(DEVS - 1)])
    q, kv, run, runt, msg = project(tokens, wq, wk, wv, log_decay, cot, lin_scale)
    got = lax.all_to_all(msg.reshape(DEVS, 16, PAIR), AX, 0, 0)
    pkv = prior(prev_tokens, wk, wv, runt)
    near_out, dq, own, prev, mark = near(
        place, neighbour_blocks, q, kv, pkv, cot, run, runt, lin_scale
    )
    nxt = lax.ppermute(prev, AX, [(i + 1, i) for i in range(DEVS - 1)])
    states = scan(place, got, mark)
    tokt = flip(tokens, mark)
    around = [lax.ppermute(tokt, "x", [(i, (i + d) % 4) for i in range(4)]) for d in (1, 2, 3)]
    states = lax.all_to_all(states.reshape(DEVS, 8, PAIR), AX, 0, 0)
    states = states.reshape(2, width // PAIR, DH, PAIR)
    layer, delta = join(near_out, dq, own, nxt, q, kv, cot, runt, states, [], lin_scale)

    delta8 = lax.all_to_all(delta, NEAR8, 0, 0)
    mine = stack([tokt, *around], delta)
    theirs = lax.ppermute(mine, "c", swap)
    tokens_grad = back(delta, wq, wk, wv)
    partial = outer(core, at_x, mine, theirs, delta8, tokens_grad)
    parts = lax.all_to_all(partial.reshape(16, width // 16, 3 * PAIR), FAR16, 0, 0)
    grad_norm = 1.0 / math.sqrt(rows * DEVS)
    piece = (jnp.sum(parts.astype(F32), axis=0) * grad_norm).astype(BF)
    plane = lax.all_to_all(jnp.broadcast_to(piece[None], (DEVS // 2, *piece.shape)), PLANE, 0, 0)
    other = lax.ppermute(plane, "c", swap)
    shape = (4, 16, *piece.shape)
    grads = place_half(core, plane.reshape(shape))
    gq, gk, gv = place_half(1 - core, other.reshape(shape), grads)
    return layer, tokens_grad, gq, gk, gv


def solution(mesh):
    chips = Mesh(mesh.devices.reshape(2, 2, 4, 4, 2), AX)
    tok = P(AX, None)
    return jax.shard_map(
        shards,
        mesh=chips,
        in_specs=(tok, P(), P(), P(), P(None, AX), tok, tok),
        out_specs=(tok, tok, P(), P(), P()),
        check_vma=False,
    )
```

```python
import functools
import math

import jax
import jax.numpy as jnp
from jax import lax
from jax.experimental import pallas as pl
from jax.experimental.pallas import tpu as pltpu
from jax.sharding import Mesh
from jax.sharding import PartitionSpec as P

BF = jnp.bfloat16
F32 = jnp.float32
AX = ("yl", "c", "x", "z", "yh")
NEAR8 = ("c", "x")
FAR16 = ("yl", "z", "yh")
PLANE = ("x", "yl", "z", "yh")
SEG = 128
PAIR = 128
DH = 64
DEVS = 128
VMEM = pltpu.VMEM
HIGH = lax.Precision.HIGHEST


def dot(a, b, ca, cb, precision=None):
    return lax.dot_general(
        a, b, (((ca,), (cb,)), ((), ())), precision=precision, preferred_element_type=F32
    )


def iota(shape, axis):
    return lax.broadcasted_iota(jnp.int32, shape, axis)


def params(mib):
    return pltpu.CompilerParams(vmem_limit_bytes=mib << 20)


def cost(flops, moved, trans=0):
    return pl.CostEstimate(flops=flops, bytes_accessed=moved, transcendentals=trans)


CHUNK = 256
WIDE = 512


def pair_lanes(columns, pair):
    shape = (columns.shape[0], PAIR)
    return jnp.where(
        iota(shape, 1) < DH,
        columns[:, 2 * pair : 2 * pair + 1],
        columns[:, 2 * pair + 1 : 2 * pair + 2],
    )


def project_kernel(lin_scale, tok, wq, wk, wv, decay, cot, q_out, kv_out, run_out, runt_out, msg, held, sems):
    width = tok.shape[1]
    wide = held.shape[3]
    copies = []
    for step in range(width // wide):
        for part, w in enumerate((wq, wk, wv)):
            copy = pltpu.make_async_copy(
                w.at[:, pl.ds(step * wide, wide)], held.at[part, step], sems.at[part, step]
            )
            copy.start()
            copies.append(copy)
    x = tok[...]
    ld = decay[...]
    lower = (iota((SEG, SEG), 0) >= iota((SEG, SEG), 1)).astype(F32)
    runt = dot(lower, ld, 1, 1, HIGH)
    run = dot(ld, lower, 1, 1, HIGH)
    group = ld.shape[0] // run_out.shape[0]
    for step in range(run_out.shape[0]):
        runt_out[step] = runt[:, step * group : (step + 1) * group]
        run_out[step] = run[step * group : (step + 1) * group, :]
    rows = iota((8, PAIR), 0)
    first = iota((DH, PAIR), 1) < DH
    for step in range(width // wide):
        for part in range(3):
            copies[step * 3 + part].wait()
        at = slice(step * wide, (step + 1) * wide)
        q = dot(x, held[0, step], 1, 0).astype(BF)
        k = dot(x, held[1, step], 1, 0).astype(BF)
        v = dot(x, held[2, step], 1, 0).astype(BF)
        q_out[:, at] = q
        kv_out[0, :, at] = k
        kv_out[1, :, at] = v
        here = []
        for part in range(wide // PAIR):
            cols = slice(part * PAIR, (part + 1) * PAIR)
            pair = step * (wide // PAIR) + part
            lanes = pair_lanes(runt, pair)
            total = lanes[SEG - 1 : SEG, :]
            g = cot[:, pair * PAIR : (pair + 1) * PAIR].astype(F32)
            weighted = (v[:, cols].astype(F32) * jnp.exp(total - lanes)).astype(BF)
            scaled = (g * jnp.exp(lanes)).astype(BF)
            states = (
                dot(k[:, cols], weighted, 0, 0),
                dot(q[:, cols], scaled, 0, 0) * lin_scale,
            )
            here.append((pair, total, states))
        for pair, total, states in here:
            high = total.astype(BF).astype(F32)
            mid = (total - high).astype(BF).astype(F32)
            low = total - high - mid
            tail = jnp.where(
                rows == 0, high, jnp.where(rows == 1, mid, jnp.where(rows == 2, low, 0.0))
            )
            tail = jnp.broadcast_to(tail[None], (8, 8, PAIR))
            for part, full in enumerate(states):
                own = jnp.where(first, full[:DH], full[DH:]).reshape(8, 8, PAIR)
                sent = jnp.concatenate([own, tail], axis=1).reshape(PAIR, PAIR)
                msg[part, pair * PAIR : (pair + 1) * PAIR, :] = sent.astype(BF)


def project(tokens, wq, wk, wv, log_decay, cot, lin_scale):
    rows, width = tokens.shape
    heads = log_decay.shape[0]
    chunks = width // CHUNK
    wide = WIDE
    vmem = pl.BlockSpec(memory_space=VMEM)
    hbm = pl.BlockSpec(memory_space=pltpu.HBM)
    return pl.pallas_call(
        functools.partial(project_kernel, lin_scale),
        in_specs=[vmem, hbm, hbm, hbm, vmem, vmem],
        out_specs=[vmem] * 5,
        out_shape=[
            jax.ShapeDtypeStruct((rows, width), BF),
            jax.ShapeDtypeStruct((2, rows, width), BF),
            jax.ShapeDtypeStruct((chunks, heads // chunks, rows), F32),
            jax.ShapeDtypeStruct((chunks, rows, heads // chunks), F32),
            jax.ShapeDtypeStruct((2, width, PAIR), BF),
        ],
        scratch_shapes=[
            VMEM((3, width // wide, width, wide), BF),
            pltpu.SemaphoreType.DMA((3, width // wide)),
        ],
        compiler_params=params(58),
        cost_estimate=cost(6 * rows * width * width, 6 * width * width + 12 * rows * width),
        name="project",
    )(tokens, wq, wk, wv, log_decay, cot)


def prior_kernel(tok, wk, wv, after, out, held, sems):
    del after
    copies = [
        pltpu.make_async_copy(w, held.at[part], sems.at[part]) for part, w in enumerate((wk, wv))
    ]
    for copy in copies:
        copy.start()
    for part in range(2):
        copies[part].wait()
        out[part] = dot(tok[...], held[part], 1, 0).astype(BF)


def prior(tokens, wk, wv, after):
    rows, width = tokens.shape
    vmem = pl.BlockSpec(memory_space=VMEM)
    hbm = pl.BlockSpec(memory_space=pltpu.HBM)
    return pl.pallas_call(
        prior_kernel,
        in_specs=[vmem, hbm, hbm, hbm],
        out_specs=vmem,
        out_shape=jax.ShapeDtypeStruct((2, rows, width), BF),
        scratch_shapes=[
            VMEM((2, width, width), BF),
            pltpu.SemaphoreType.DMA((2,)),
        ],
        compiler_params=params(58),
        cost_estimate=cost(4 * rows * width * width, 4 * width * width + 6 * rows * width),
        name="prior",
    )(tokens, wk, wv, after)


def flip_kernel(tok, after, out):
    del after
    out[...] = tok[...].T


def flip(tokens, after):
    rows, width = tokens.shape
    return pl.pallas_call(
        flip_kernel,
        in_specs=[pl.BlockSpec(memory_space=VMEM), pl.BlockSpec(memory_space=pl.ANY)],
        out_specs=pl.BlockSpec(memory_space=VMEM),
        out_shape=jax.ShapeDtypeStruct((width, rows), BF),
        compiler_params=params(16),
        cost_estimate=cost(0, 4 * rows * width),
        name="flip",
    )(tokens, after)


def stack_kernel(*refs):
    out = refs[-1]
    for i in range(out.shape[0]):
        out[i] = refs[i][...]


def stack(parts, after):
    shape = parts[0].shape
    whole = pl.BlockSpec(memory_space=VMEM)
    return pl.pallas_call(
        stack_kernel,
        in_specs=[whole] * len(parts) + [pl.BlockSpec(memory_space=pl.ANY)],
        out_specs=whole,
        out_shape=jax.ShapeDtypeStruct((len(parts), *shape), BF),
        compiler_params=params(16),
        cost_estimate=cost(0, 4 * len(parts) * math.prod(shape)),
        name="stack",
    )(*parts, after)


def scan_kernel(place, got, after, out, xs, decays, states):
    del after
    both = got[...].astype(F32)
    xs[...] = both[:, :8, :]
    total = both[:, 8:9, :] + both[:, 9:10, :] + both[:, 10:11, :]
    decays[...] = jnp.broadcast_to(jnp.exp(total), decays.shape)
    backward = place[0] >= DEVS // 2

    def one(i, state):
        at = jnp.where(backward, DEVS - 1 - i, i)
        states[at] = state
        return decays[at] * state + xs[at]

    lax.fori_loop(0, DEVS, one, jnp.zeros((8, PAIR), F32), unroll=8)
    out[...] = states[...].reshape(DEVS * 8, PAIR).astype(BF)


def scan(place, got, after):
    whole = pl.BlockSpec(memory_space=VMEM)
    return pl.pallas_call(
        scan_kernel,
        in_specs=[
            pl.BlockSpec(memory_space=pltpu.SMEM),
            whole,
            pl.BlockSpec(memory_space=pl.ANY),
        ],
        out_specs=whole,
        out_shape=jax.ShapeDtypeStruct((DEVS * 8, PAIR), BF),
        scratch_shapes=[VMEM((DEVS, 8, PAIR), F32)] * 3,
        compiler_params=params(24),
        cost_estimate=cost(2 * DEVS * 8 * PAIR, 4 * DEVS * 16 * PAIR),
        name="scan",
    )(place, got, after)


def near_kernel(lin_scale, place, blocks, q_ref, kv, pkv, cot, run, runt, out, dq_out, own, prev, mark):
    mark[...] = jnp.zeros_like(mark)
    soft_scale = 1.0 / math.sqrt(DH)
    n_own = jnp.int32(0)
    n_prev = jnp.int32(0)
    for j in range(blocks.shape[1]):
        n_own += (blocks[0, j] == place[0]).astype(jnp.int32)
        n_prev += (blocks[0, j] == place[0] - 1).astype(jnp.int32)
    is_own = iota((1, 2 * SEG), 1) < SEG
    times = jnp.where(is_own, n_own, n_prev)
    bias = jnp.where(times > 0, 0.0, -1e30)
    times = times.astype(F32)
    head_of = iota((SEG, PAIR), 1) // DH
    head_of2 = iota((2 * SEG, PAIR), 1) // DH
    lower = iota((SEG, SEG), 0) >= iota((SEG, SEG), 1)
    zero = jnp.zeros((), BF)
    pairs = q_ref.shape[1] // PAIR
    work = []
    for pair in range(pairs):
        at = slice(pair * PAIR, (pair + 1) * PAIR)
        q = q_ref[:, at]
        g = cot[:, at]
        kk = jnp.concatenate([kv[0, :, at], pkv[0, :, at]], axis=0)
        vv = jnp.concatenate([kv[1, :, at], pkv[1, :, at]], axis=0)
        for i in range(2):
            mine = head_of == i
            work.append(
                (
                    dot(jnp.where(mine, q, zero), kk, 1, 1),
                    dot(jnp.where(mine, g, zero), vv, 1, 1),
                )
            )
    mats = []
    for head in range(2 * pairs):
        scores, pgrad = work[head]
        col = runt[0, :, head : head + 1]
        row = run[0, head : head + 1, :]
        dec = jnp.where(lower, jnp.exp(jnp.minimum(col - row, 0.0)), 0.0) * lin_scale
        logits = scores * soft_scale + bias
        peak = jnp.max(logits, axis=1, keepdims=True)
        terms = jnp.exp(logits - peak) * times
        probs = terms * (1.0 / jnp.sum(terms, axis=1, keepdims=True))
        inner = jnp.sum(probs * pgrad, axis=1, keepdims=True)
        dlog = probs * (pgrad - inner) * soft_scale
        a = jnp.concatenate([probs[:, :SEG] + scores[:, :SEG] * dec, probs[:, SEG:]], axis=1)
        b = jnp.concatenate([dlog[:, :SEG] + pgrad[:, :SEG] * dec, dlog[:, SEG:]], axis=1)
        mats.append((a.astype(BF), b.astype(BF)))
    for pair in range(pairs):
        at = slice(pair * PAIR, (pair + 1) * PAIR)
        q = q_ref[:, at]
        g = cot[:, at]
        kk = jnp.concatenate([kv[0, :, at], pkv[0, :, at]], axis=0)
        vv = jnp.concatenate([kv[1, :, at], pkv[1, :, at]], axis=0)
        qt = q.T
        gt = g.T
        res = []
        for i in range(2):
            a, b = mats[2 * pair + i]
            half = slice(i * DH, (i + 1) * DH)
            res.append((dot(a, vv, 1, 0), dot(b, kk, 1, 0), dot(qt[half], b, 1, 0), dot(gt[half], a, 1, 0)))
        out[:, at] = jnp.where(head_of == 0, res[0][0], res[1][0])
        dq_out[:, at] = jnp.where(head_of == 0, res[0][1], res[1][1])
        for part in range(2):
            sums = jnp.concatenate([res[0][2 + part], res[1][2 + part]], axis=0).T
            own[part, :, at] = sums[:SEG]
            prev[part, :, at] = sums[SEG:].astype(BF)


def near(place, blocks, q, kv, pkv, cot, run, runt, lin_scale):
    rows, width = q.shape
    heads = run.shape[1]
    smem = pl.BlockSpec(memory_space=pltpu.SMEM)
    col = pl.BlockSpec((rows, CHUNK), lambda i: (0, i))
    two = pl.BlockSpec((2, rows, CHUNK), lambda i: (0, 0, i))
    return pl.pallas_call(
        functools.partial(near_kernel, lin_scale),
        grid=(width // CHUNK,),
        in_specs=[
            smem,
            smem,
            col,
            two,
            two,
            col,
            pl.BlockSpec((1, heads, rows), lambda i: (i, 0, 0)),
            pl.BlockSpec((1, rows, heads), lambda i: (i, 0, 0)),
        ],
        out_specs=[col, col, two, two, pl.BlockSpec((8, PAIR), lambda i: (0, 0))],
        out_shape=[
            jax.ShapeDtypeStruct((rows, width), F32),
            jax.ShapeDtypeStruct((rows, width), F32),
            jax.ShapeDtypeStruct((2, rows, width), F32),
            jax.ShapeDtypeStruct((2, rows, width), BF),
            jax.ShapeDtypeStruct((8, PAIR), F32),
        ],
        compiler_params=params(58),
        cost_estimate=cost(4000 * 1000 * 1000, 16 * 1000 * 1000, 1000 * 1000),
        name="near",
    )(place, blocks, q, kv, pkv, cot, run, runt)


def join_kernel(lin_scale, near_out, dq_in, own, nxt, q, kv, cot, runt, states, *rest):
    layer, delta = rest[-2:]
    head_of = iota((SEG, PAIR), 1) // DH
    diag = iota((PAIR, PAIR), 0) // DH == iota((PAIR, PAIR), 1) // DH
    zero = jnp.zeros((), BF)
    pairs = q.shape[1] // PAIR
    work = []
    for pair in range(pairs):
        at = slice(pair * PAIR, (pair + 1) * PAIR)
        before, after = (
            jnp.where(diag, jnp.concatenate([states[part, pair]] * 2, axis=0), zero)
            for part in range(2)
        )
        work.append(
            (
                dot(q[:, at], before, 1, 0),
                dot(cot[:, at], before, 1, 1),
                dot(kv[1, :, at], after, 1, 1),
                dot(kv[0, :, at], after, 1, 0),
            )
        )
    for pair in range(pairs):
        at = slice(pair * PAIR, (pair + 1) * PAIR)
        run = jnp.where(
            head_of == 0,
            runt[pair // 2, :, 2 * (pair % 2) : 2 * (pair % 2) + 1],
            runt[pair // 2, :, 2 * (pair % 2) + 1 : 2 * (pair % 2) + 2],
        )
        growth = jnp.exp(run) * lin_scale
        fading = jnp.exp(run[SEG - 1 : SEG, :] - run)
        from_q, from_g, from_v, from_k = work[pair]
        layer[:, at] = (near_out[:, at] + growth * from_q).astype(BF)
        dq = dq_in[:, at] + growth * from_g
        dk = own[0, :, at] + fading * from_v + nxt[0, :, at].astype(F32)
        dv = own[1, :, at] + fading * from_k + nxt[1, :, at].astype(F32)
        delta[pair, :, :PAIR] = dq.astype(BF)
        delta[pair, :, PAIR : 2 * PAIR] = dk.astype(BF)
        delta[pair, :, 2 * PAIR :] = dv.astype(BF)


def join(near_out, dq, own, nxt, q, kv, cot, runt, states, after, lin_scale):
    rows, width = q.shape
    pairs = width // PAIR
    wide = 2 * CHUNK
    col = pl.BlockSpec((rows, wide), lambda i: (0, i))
    two = pl.BlockSpec((2, rows, wide), lambda i: (0, 0, i))
    return pl.pallas_call(
        functools.partial(join_kernel, lin_scale),
        grid=(width // wide,),
        in_specs=[
            col,
            col,
            two,
            two,
            col,
            two,
            col,
            pl.BlockSpec((2, rows, runt.shape[2]), lambda i: (i, 0, 0)),
            pl.BlockSpec((2, wide // PAIR, DH, PAIR), lambda i: (0, i, 0, 0)),
        ]
        + [pl.BlockSpec(memory_space=pl.ANY)] * len(after),
        out_specs=[col, pl.BlockSpec((wide // PAIR, rows, 3 * PAIR), lambda i: (i, 0, 0))],
        out_shape=[
            jax.ShapeDtypeStruct((rows, width), BF),
            jax.ShapeDtypeStruct((pairs, rows, 3 * PAIR), BF),
        ],
        compiler_params=params(58),
        cost_estimate=cost(8 * rows * PAIR * PAIR * pairs, 24 * rows * width),
        name="join",
    )(near_out, dq, own, nxt, q, kv, cot, runt, states, *after)


def back_kernel(delta, wq, wk, wv, out, total):
    step = pl.program_id(0)

    @pl.when(step == 0)
    def _():
        total[...] = jnp.zeros_like(total)

    acc = total[...]
    for part, w in enumerate((wq, wk, wv)):
        for half in range(2):
            acc += dot(
                delta[half, :, part * PAIR : (part + 1) * PAIR],
                w[:, half * PAIR : (half + 1) * PAIR],
                1,
                1,
            )
    total[...] = acc

    @pl.when(step == pl.num_programs(0) - 1)
    def _():
        out[...] = acc.astype(BF)


def back(delta, wq, wk, wv):
    pairs, rows, _ = delta.shape
    width = wq.shape[0]
    weight = pl.BlockSpec((width, 2 * PAIR), lambda i: (0, i))
    return pl.pallas_call(
        back_kernel,
        grid=(pairs // 2,),
        in_specs=[pl.BlockSpec((2, rows, 3 * PAIR), lambda i: (i, 0, 0)), weight, weight, weight],
        out_specs=pl.BlockSpec((rows, width), lambda i: (0, 0)),
        out_shape=jax.ShapeDtypeStruct((rows, width), BF),
        scratch_shapes=[VMEM((rows, width), F32)],
        compiler_params=params(58),
        cost_estimate=cost(6 * rows * width * width, 6 * width * width + 8 * rows * width),
        name="back",
    )(delta, wq, wk, wv)


def outer_kernel(core, at_x, mine, theirs, delta, after, out):
    del after
    near_x = mine.shape[0]
    left, right = [], []
    for tokt, c in ((mine, core[0]), (theirs, 1 - core[0])):
        for i in range(near_x):
            left.append(tokt[i])
            right.append(delta[c * near_x + lax.rem(at_x[0] + near_x - i, near_x)])
    left = jnp.concatenate(left, axis=1)
    out[...] = dot(left, jnp.concatenate(right, axis=0), 1, 0).astype(BF)


def outer(core, at_x, mine, theirs, delta, after):
    near_count, rows, cols = delta.shape
    width = mine.shape[1]
    smem = pl.BlockSpec(memory_space=pltpu.SMEM)
    tok = pl.BlockSpec((near_count // 2, width // 2, rows), lambda i: (0, i, 0))
    return pl.pallas_call(
        outer_kernel,
        grid=(2,),
        in_specs=[
            smem,
            smem,
            tok,
            tok,
            pl.BlockSpec((near_count, rows, cols), lambda i: (0, 0, 0)),
            pl.BlockSpec(memory_space=pl.ANY),
        ],
        out_specs=pl.BlockSpec((width // 2, cols), lambda i: (i, 0)),
        out_shape=jax.ShapeDtypeStruct((width, cols), BF),
        compiler_params=params(58),
        cost_estimate=cost(
            2 * near_count * rows * cols * width, 2 * near_count * rows * (width + cols)
        ),
        name="outer",
    )(core, at_x, mine, theirs, delta, after)


def device(yl, c, x, z, yh):
    return (((yl * 2 + c) * 4 + x) * 4 + z) * 2 + yh


def gather_groups():
    zero = [
        [device(yl, 0, x, z, yh) for yl in range(2) for z in range(4) for yh in range(2)]
        for x in range(4)
    ]
    one = [
        [device(yl, 1, x, z, yh) for x in range(4) for yl in range(2) for yh in range(2)]
        for z in range(4)
    ]
    return zero + one


def ring(array, by):
    route = []
    for yl in range(2):
        for x in range(4):
            for z in range(4):
                for yh in range(2):
                    route.append((device(yl, 0, x, z, yh), device(yl, 0, (x + by) % 4, z, yh)))
                    route.append((device(yl, 1, x, z, yh), device(yl, 1, x, (z + by) % 4, yh)))
    return lax.ppermute(array, AX, route)


def place_kernel(pieces, side, at_x, at_z, own, other, *refs):
    grads, mark, sems = refs[-5:-2], refs[-2], refs[-1]
    mark[...] = jnp.zeros_like(mark)

    def put(zero, one):
        copies = []

        def start(src, dst):
            copy = pltpu.make_async_copy(src, dst, sems.at[len(copies)])
            copy.start()
            copies.append(copy)

        rows = zero.shape[1]
        for place, by in enumerate(pieces):
            x = lax.rem(at_x[0] + by + 4, 4)
            z = lax.rem(at_z[0] + by + 4, 4)
            for part, grad in enumerate(grads):
                lanes = pl.ds(part * PAIR, PAIR)
                for i in range(8):
                    start(
                        zero.at[place * 8 + i, :, lanes],
                        grad.at[pl.ds(i * rows, rows), pl.ds(pl.multiple_of(x * PAIR, PAIR), PAIR)],
                    )
                    to = pl.multiple_of(((i % 2) * 4 + z) * rows, rows)
                    start(
                        one.at[place * 8 + i, :, lanes],
                        grad.at[pl.ds(to, rows), pl.ds((4 + i // 2) * PAIR, PAIR)],
                    )
        for copy in copies:
            copy.wait()

    @pl.when(side[0] == 0)
    def _():
        put(own, other)

    @pl.when(side[0] == 1)
    def _():
        put(other, own)


def place_tiles(where, pieces, own, other, grads, width):
    hbm = pl.BlockSpec(memory_space=pl.ANY)
    smem = pl.BlockSpec(memory_space=pltpu.SMEM)
    return pl.pallas_call(
        functools.partial(place_kernel, pieces),
        in_specs=[smem] * 3 + [hbm] * (2 + len(grads)),
        out_specs=[hbm] * 3 + [pl.BlockSpec(memory_space=VMEM)],
        out_shape=[jax.ShapeDtypeStruct((width, width), BF)] * 3
        + [jax.ShapeDtypeStruct((8, PAIR), F32)],
        scratch_shapes=[pltpu.SemaphoreType.DMA((6 * own.shape[0],))],
        input_output_aliases={5 + i: i for i in range(len(grads))},
        compiler_params=params(16),
        cost_estimate=cost(0, 8 * own.size),
        name="place",
    )(*where, own, other, *grads)


def halves_kernel(behind, ahead, after, first, second, both):
    del after
    half = first.shape[0]
    first[...] = behind[:half]
    second[...] = ahead[half:]
    both[: 2 * half] = behind[...]
    both[2 * half :] = ahead[...]


def halves(behind, ahead, after):
    pairs, *rest = behind.shape
    whole = pl.BlockSpec(memory_space=VMEM)
    return pl.pallas_call(
        halves_kernel,
        in_specs=[whole, whole, pl.BlockSpec(memory_space=pl.ANY)],
        out_specs=[whole] * 3,
        out_shape=[jax.ShapeDtypeStruct((n, *rest), BF) for n in (pairs // 2, pairs // 2, 2 * pairs)],
        compiler_params=params(16),
        cost_estimate=cost(0, 12 * behind.size),
        name="halves",
    )(behind, ahead, after)


def gather_tiles(piece, where, width):
    swap = [(0, 1), (1, 0)]

    def swapped(array):
        return lax.ppermute(array, "c", swap)

    rows, cols = piece.shape
    here = lax.all_to_all(
        jnp.broadcast_to(piece[None], (16, rows, cols)), AX, 0, 0, axis_index_groups=gather_groups()
    ).reshape(8, 2 * rows, cols)
    behind = ring(here, 1)
    ahead = ring(here, -1)
    *grads, mark = place_tiles(where, (0,), here, swapped(here), (), width)
    half_a, half_b, both = halves(behind, ahead, mark)
    far_a = ring(half_a, 1)
    far_b = ring(half_b, -1)
    *grads, mark = place_tiles(where, (-1, 1), both, swapped(both), grads, width)
    far = stack([far_a, far_b], mark).reshape(here.shape)
    *grads, _ = place_tiles(where, (2,), far, swapped(far), grads, width)
    return grads


def shards(tokens, wq, wk, wv, log_decay, neighbour_blocks, cot):
    rows, width = tokens.shape
    lin_scale = 1.0 / (DH * math.sqrt(rows))
    place = lax.axis_index(AX).astype(jnp.int32).reshape(1)
    core = lax.axis_index("c").astype(jnp.int32).reshape(1)

    at_x = lax.axis_index("x").astype(jnp.int32).reshape(1)
    swap = [(0, 1), (1, 0)]
    prev_tokens = lax.ppermute(tokens, AX, [(i, i + 1) for i in range(DEVS - 1)])
    q, kv, run, runt, msg = project(tokens, wq, wk, wv, log_decay, cot, lin_scale)
    got = lax.all_to_all(msg.reshape(DEVS, 16, PAIR), AX, 0, 0)
    pkv = prior(prev_tokens, wk, wv, runt)
    near_out, dq, own, prev, mark = near(
        place, neighbour_blocks, q, kv, pkv, cot, run, runt, lin_scale
    )
    nxt = lax.ppermute(prev, AX, [(i + 1, i) for i in range(DEVS - 1)])
    states = scan(place, got, mark)
    tokt = flip(tokens, mark)
    around = [lax.ppermute(tokt, "x", [(i, (i + d) % 4) for i in range(4)]) for d in (1, 2, 3)]
    states = lax.all_to_all(states.reshape(DEVS, 8, PAIR), AX, 0, 0)
    states = states.reshape(2, width // PAIR, DH, PAIR)
    layer, delta = join(near_out, dq, own, nxt, q, kv, cot, runt, states, [], lin_scale)

    delta8 = lax.all_to_all(delta, NEAR8, 0, 0)
    mine = stack([tokt, *around], delta)
    theirs = lax.ppermute(mine, "c", swap)
    tokens_grad = back(delta, wq, wk, wv)
    partial = outer(core, at_x, mine, theirs, delta8, tokens_grad)
    parts = lax.all_to_all(partial.reshape(16, width // 16, 3 * PAIR), FAR16, 0, 0)
    grad_norm = 1.0 / math.sqrt(rows * DEVS)
    piece = (jnp.sum(parts.astype(F32), axis=0) * grad_norm).astype(BF)
    at_z = lax.axis_index("z").astype(jnp.int32).reshape(1)
    gq, gk, gv = gather_tiles(piece, (core, at_x, at_z), width)
    return layer, tokens_grad, gq, gk, gv


def solution(mesh):
    chips = Mesh(mesh.devices.reshape(2, 2, 4, 4, 2), AX)
    tok = P(AX, None)
    return jax.shard_map(
        shards,
        mesh=chips,
        in_specs=(tok, P(), P(), P(), P(None, AX), tok, tok),
        out_specs=(tok, tok, P(), P(), P()),
        check_vma=False,
    )
```

```python
import functools
import math

import jax
import jax.numpy as jnp
from jax import lax
from jax.experimental import pallas as pl
from jax.experimental.pallas import tpu as pltpu
from jax.sharding import Mesh
from jax.sharding import PartitionSpec as P

BF = jnp.bfloat16
F32 = jnp.float32
AX = ("yl", "c", "x", "z", "yh")
NEAR8 = ("c", "x")
FAR16 = ("yl", "z", "yh")
PLANE = ("x", "yl", "z", "yh")
SEG = 128
PAIR = 128
DH = 64
DEVS = 128
SPAN = ("x", "z", "yh")
GROUP = ("yl", "c")
PLACES = 32
GROUPS = 4
SLICE = 32
SENT = SLICE + 16
VMEM = pltpu.VMEM
HIGH = lax.Precision.HIGHEST


def dot(a, b, ca, cb, precision=None):
    return lax.dot_general(
        a, b, (((ca,), (cb,)), ((), ())), precision=precision, preferred_element_type=F32
    )


def iota(shape, axis):
    return lax.broadcasted_iota(jnp.int32, shape, axis)


def params(mib):
    return pltpu.CompilerParams(vmem_limit_bytes=mib << 20)


def cost(flops, moved, trans=0):
    return pl.CostEstimate(flops=flops, bytes_accessed=moved, transcendentals=trans)


CHUNK = 256
WIDE = 512


def pair_lanes(columns, pair):
    shape = (columns.shape[0], PAIR)
    return jnp.where(
        iota(shape, 1) < DH,
        columns[:, 2 * pair : 2 * pair + 1],
        columns[:, 2 * pair + 1 : 2 * pair + 2],
    )


def project_kernel(lin_scale, tok, wq, wk, wv, decay, cot, q_out, kv_out, run_out, runt_out, msg, held, sems):
    width = tok.shape[1]
    wide = held.shape[3]
    copies = []
    for step in range(width // wide):
        for part, w in enumerate((wq, wk, wv)):
            copy = pltpu.make_async_copy(
                w.at[:, pl.ds(step * wide, wide)], held.at[part, step], sems.at[part, step]
            )
            copy.start()
            copies.append(copy)
    x = tok[...]
    ld = decay[...]
    lower = (iota((SEG, SEG), 0) >= iota((SEG, SEG), 1)).astype(F32)
    runt = dot(lower, ld, 1, 1, HIGH)
    run = dot(ld, lower, 1, 1, HIGH)
    group = ld.shape[0] // run_out.shape[0]
    for step in range(run_out.shape[0]):
        runt_out[step] = runt[:, step * group : (step + 1) * group]
        run_out[step] = run[step * group : (step + 1) * group, :]
    rows = iota((SENT - SLICE, PAIR), 0)
    first = iota((DH, PAIR), 1) < DH
    for step in range(width // wide):
        for part in range(3):
            copies[step * 3 + part].wait()
        at = slice(step * wide, (step + 1) * wide)
        q = dot(x, held[0, step], 1, 0).astype(BF)
        k = dot(x, held[1, step], 1, 0).astype(BF)
        v = dot(x, held[2, step], 1, 0).astype(BF)
        q_out[:, at] = q
        kv_out[0, :, at] = k
        kv_out[1, :, at] = v
        here = []
        for part in range(wide // PAIR):
            cols = slice(part * PAIR, (part + 1) * PAIR)
            pair = step * (wide // PAIR) + part
            lanes = pair_lanes(runt, pair)
            total = lanes[SEG - 1 : SEG, :]
            g = cot[:, pair * PAIR : (pair + 1) * PAIR].astype(F32)
            weighted = (v[:, cols].astype(F32) * jnp.exp(total - lanes)).astype(BF)
            scaled = (g * jnp.exp(lanes)).astype(BF)
            states = (
                dot(k[:, cols], weighted, 0, 0),
                dot(q[:, cols], scaled, 0, 0) * lin_scale,
            )
            here.append((pair, total, states))
        for pair, total, states in here:
            high = total.astype(BF).astype(F32)
            mid = (total - high).astype(BF).astype(F32)
            low = total - high - mid
            tail = jnp.where(
                rows == 0, high, jnp.where(rows == 1, mid, jnp.where(rows == 2, low, 0.0))
            )
            for part, full in enumerate(states):
                own = jnp.where(first, full[:DH], full[DH:])
                sent = jnp.concatenate([own[:SLICE], tail, own[SLICE:], tail], axis=0)
                msg[part, pair * 2 * SENT : (pair + 1) * 2 * SENT, :] = sent.astype(BF)


def project(tokens, wq, wk, wv, log_decay, cot, lin_scale):
    rows, width = tokens.shape
    heads = log_decay.shape[0]
    chunks = width // CHUNK
    wide = WIDE
    vmem = pl.BlockSpec(memory_space=VMEM)
    hbm = pl.BlockSpec(memory_space=pltpu.HBM)
    return pl.pallas_call(
        functools.partial(project_kernel, lin_scale),
        in_specs=[vmem, hbm, hbm, hbm, vmem, vmem],
        out_specs=[vmem] * 5,
        out_shape=[
            jax.ShapeDtypeStruct((rows, width), BF),
            jax.ShapeDtypeStruct((2, rows, width), BF),
            jax.ShapeDtypeStruct((chunks, heads // chunks, rows), F32),
            jax.ShapeDtypeStruct((chunks, rows, heads // chunks), F32),
            jax.ShapeDtypeStruct((2, width // PAIR * 2 * SENT, PAIR), BF),
        ],
        scratch_shapes=[
            VMEM((3, width // wide, width, wide), BF),
            pltpu.SemaphoreType.DMA((3, width // wide)),
        ],
        compiler_params=params(58),
        cost_estimate=cost(6 * rows * width * width, 6 * width * width + 12 * rows * width),
        name="project",
    )(tokens, wq, wk, wv, log_decay, cot)


def prior_kernel(tok, wk, wv, after, out, held, sems):
    del after
    copies = [
        pltpu.make_async_copy(w, held.at[part], sems.at[part]) for part, w in enumerate((wk, wv))
    ]
    for copy in copies:
        copy.start()
    for part in range(2):
        copies[part].wait()
        out[part] = dot(tok[...], held[part], 1, 0).astype(BF)


def prior(tokens, wk, wv, after):
    rows, width = tokens.shape
    vmem = pl.BlockSpec(memory_space=VMEM)
    hbm = pl.BlockSpec(memory_space=pltpu.HBM)
    return pl.pallas_call(
        prior_kernel,
        in_specs=[vmem, hbm, hbm, hbm],
        out_specs=vmem,
        out_shape=jax.ShapeDtypeStruct((2, rows, width), BF),
        scratch_shapes=[
            VMEM((2, width, width), BF),
            pltpu.SemaphoreType.DMA((2,)),
        ],
        compiler_params=params(58),
        cost_estimate=cost(4 * rows * width * width, 4 * width * width + 6 * rows * width),
        name="prior",
    )(tokens, wk, wv, after)


def flip_kernel(tok, after, out):
    del after
    out[...] = tok[...].T


def flip(tokens, after):
    rows, width = tokens.shape
    return pl.pallas_call(
        flip_kernel,
        in_specs=[pl.BlockSpec(memory_space=VMEM), pl.BlockSpec(memory_space=pl.ANY)],
        out_specs=pl.BlockSpec(memory_space=VMEM),
        out_shape=jax.ShapeDtypeStruct((width, rows), BF),
        compiler_params=params(16),
        cost_estimate=cost(0, 4 * rows * width),
        name="flip",
    )(tokens, after)


def stack_kernel(*refs):
    out = refs[-1]
    for i in range(out.shape[0]):
        out[i] = refs[i][...]


def stack(parts, after):
    shape = parts[0].shape
    whole = pl.BlockSpec(memory_space=VMEM)
    return pl.pallas_call(
        stack_kernel,
        in_specs=[whole] * len(parts) + [pl.BlockSpec(memory_space=pl.ANY)],
        out_specs=whole,
        out_shape=jax.ShapeDtypeStruct((len(parts), *shape), BF),
        compiler_params=params(16),
        cost_estimate=cost(0, 4 * len(parts) * math.prod(shape)),
        name="stack",
    )(*parts, after)


def unpack(got, xs, decays):
    both = got[...].astype(F32)
    xs[...] = both[:, :SLICE, :]
    total = both[:, SLICE : SLICE + 1, :] + both[:, SLICE + 1 : SLICE + 2, :]
    total += both[:, SLICE + 2 : SLICE + 3, :]
    decays[...] = jnp.exp(total)
    return total


def along(backward, i):
    return jnp.where(backward, PLACES - 1 - i, i)


def total_kernel(at_span, got, after, out, xs, decays):
    del after
    total = unpack(got, xs, decays)
    backward = at_span[0] >= PLACES // 2
    state = jnp.zeros((SLICE, PAIR), F32)
    for i in range(PLACES):
        at = along(backward, i)
        state = decays[at] * state + xs[at]
    out[:SLICE] = state
    out[SLICE:] = jnp.broadcast_to(jnp.sum(total, axis=0), (8, PAIR))


def scan_kernel(at_span, at_group, got, one, two, three, out, xs, decays, states):
    unpack(got, xs, decays)
    backward = at_span[0] >= PLACES // 2
    group = at_group[0]
    state = jnp.zeros((SLICE, PAIR), F32)
    for near_by, front, back in ((3, three, one), (2, two, two), (1, one, three)):
        there = jnp.where(backward, group + near_by < GROUPS, group >= near_by)
        that = jnp.where(backward, back[...], front[...])
        joined = jnp.exp(that[SLICE : SLICE + 1]) * state + that[:SLICE]
        state = jnp.where(there, joined, state)
    for i in range(PLACES):
        at = along(backward, i)
        states[at] = state
        state = decays[at] * state + xs[at]
    out[...] = states[...].reshape(PLACES * SLICE, PAIR).astype(BF)


def group_total(at_span, got, after):
    whole = pl.BlockSpec(memory_space=VMEM)
    return pl.pallas_call(
        total_kernel,
        in_specs=[
            pl.BlockSpec(memory_space=pltpu.SMEM),
            whole,
            pl.BlockSpec(memory_space=pl.ANY),
        ],
        out_specs=whole,
        out_shape=jax.ShapeDtypeStruct((SLICE + 8, PAIR), F32),
        scratch_shapes=[VMEM((PLACES, SLICE, PAIR), F32), VMEM((PLACES, 1, PAIR), F32)],
        compiler_params=params(24),
        cost_estimate=cost(2 * PLACES * SLICE * PAIR, 4 * PLACES * SENT * PAIR),
        name="group_total",
    )(at_span, got, after)


def scan(at_span, at_group, got, others):
    whole = pl.BlockSpec(memory_space=VMEM)
    smem = pl.BlockSpec(memory_space=pltpu.SMEM)
    return pl.pallas_call(
        scan_kernel,
        in_specs=[smem, smem] + [whole] * 4,
        out_specs=whole,
        out_shape=jax.ShapeDtypeStruct((PLACES * SLICE, PAIR), BF),
        scratch_shapes=[
            VMEM((PLACES, SLICE, PAIR), F32),
            VMEM((PLACES, 1, PAIR), F32),
            VMEM((PLACES, SLICE, PAIR), F32),
        ],
        compiler_params=params(24),
        cost_estimate=cost(2 * PLACES * SLICE * PAIR, 4 * PLACES * SENT * PAIR),
        name="scan",
    )(at_span, at_group, got, *others)


def near_kernel(lin_scale, place, blocks, q_ref, kv, pkv, cot, run, runt, out, dq_out, own, prev, mark):
    mark[...] = jnp.zeros_like(mark)
    soft_scale = 1.0 / math.sqrt(DH)
    n_own = jnp.int32(0)
    n_prev = jnp.int32(0)
    for j in range(blocks.shape[1]):
        n_own += (blocks[0, j] == place[0]).astype(jnp.int32)
        n_prev += (blocks[0, j] == place[0] - 1).astype(jnp.int32)
    is_own = iota((1, 2 * SEG), 1) < SEG
    times = jnp.where(is_own, n_own, n_prev)
    bias = jnp.where(times > 0, 0.0, -1e30)
    times = times.astype(F32)
    head_of = iota((SEG, PAIR), 1) // DH
    head_of2 = iota((2 * SEG, PAIR), 1) // DH
    lower = iota((SEG, SEG), 0) >= iota((SEG, SEG), 1)
    zero = jnp.zeros((), BF)
    pairs = q_ref.shape[1] // PAIR
    work = []
    for pair in range(pairs):
        at = slice(pair * PAIR, (pair + 1) * PAIR)
        q = q_ref[:, at]
        g = cot[:, at]
        kk = jnp.concatenate([kv[0, :, at], pkv[0, :, at]], axis=0)
        vv = jnp.concatenate([kv[1, :, at], pkv[1, :, at]], axis=0)
        for i in range(2):
            mine = head_of == i
            work.append(
                (
                    dot(jnp.where(mine, q, zero), kk, 1, 1),
                    dot(jnp.where(mine, g, zero), vv, 1, 1),
                )
            )
    mats = []
    for head in range(2 * pairs):
        scores, pgrad = work[head]
        col = runt[0, :, head : head + 1]
        row = run[0, head : head + 1, :]
        dec = jnp.where(lower, jnp.exp(jnp.minimum(col - row, 0.0)), 0.0) * lin_scale
        logits = scores * soft_scale + bias
        peak = jnp.max(logits, axis=1, keepdims=True)
        terms = jnp.exp(logits - peak) * times
        probs = terms * (1.0 / jnp.sum(terms, axis=1, keepdims=True))
        inner = jnp.sum(probs * pgrad, axis=1, keepdims=True)
        dlog = probs * (pgrad - inner) * soft_scale
        a = jnp.concatenate([probs[:, :SEG] + scores[:, :SEG] * dec, probs[:, SEG:]], axis=1)
        b = jnp.concatenate([dlog[:, :SEG] + pgrad[:, :SEG] * dec, dlog[:, SEG:]], axis=1)
        mats.append((a.astype(BF), b.astype(BF)))
    for pair in range(pairs):
        at = slice(pair * PAIR, (pair + 1) * PAIR)
        q = q_ref[:, at]
        g = cot[:, at]
        kk = jnp.concatenate([kv[0, :, at], pkv[0, :, at]], axis=0)
        vv = jnp.concatenate([kv[1, :, at], pkv[1, :, at]], axis=0)
        qt = q.T
        gt = g.T
        res = []
        for i in range(2):
            a, b = mats[2 * pair + i]
            half = slice(i * DH, (i + 1) * DH)
            res.append((dot(a, vv, 1, 0), dot(b, kk, 1, 0), dot(qt[half], b, 1, 0), dot(gt[half], a, 1, 0)))
        out[:, at] = jnp.where(head_of == 0, res[0][0], res[1][0])
        dq_out[:, at] = jnp.where(head_of == 0, res[0][1], res[1][1])
        for part in range(2):
            sums = jnp.concatenate([res[0][2 + part], res[1][2 + part]], axis=0).T
            own[part, :, at] = sums[:SEG]
            prev[part, :, at] = sums[SEG:].astype(BF)


def near(place, blocks, q, kv, pkv, cot, run, runt, lin_scale):
    rows, width = q.shape
    heads = run.shape[1]
    smem = pl.BlockSpec(memory_space=pltpu.SMEM)
    col = pl.BlockSpec((rows, CHUNK), lambda i: (0, i))
    two = pl.BlockSpec((2, rows, CHUNK), lambda i: (0, 0, i))
    return pl.pallas_call(
        functools.partial(near_kernel, lin_scale),
        grid=(width // CHUNK,),
        in_specs=[
            smem,
            smem,
            col,
            two,
            two,
            col,
            pl.BlockSpec((1, heads, rows), lambda i: (i, 0, 0)),
            pl.BlockSpec((1, rows, heads), lambda i: (i, 0, 0)),
        ],
        out_specs=[col, col, two, two, pl.BlockSpec((8, PAIR), lambda i: (0, 0))],
        out_shape=[
            jax.ShapeDtypeStruct((rows, width), F32),
            jax.ShapeDtypeStruct((rows, width), F32),
            jax.ShapeDtypeStruct((2, rows, width), F32),
            jax.ShapeDtypeStruct((2, rows, width), BF),
            jax.ShapeDtypeStruct((8, PAIR), F32),
        ],
        compiler_params=params(58),
        cost_estimate=cost(4000 * 1000 * 1000, 16 * 1000 * 1000, 1000 * 1000),
        name="near",
    )(place, blocks, q, kv, pkv, cot, run, runt)


def join_kernel(lin_scale, near_out, dq_in, own, nxt, q, kv, cot, runt, states, *rest):
    layer, delta = rest[-2:]
    head_of = iota((SEG, PAIR), 1) // DH
    diag = iota((PAIR, PAIR), 0) // DH == iota((PAIR, PAIR), 1) // DH
    zero = jnp.zeros((), BF)
    pairs = q.shape[1] // PAIR
    work = []
    for pair in range(pairs):
        at = slice(pair * PAIR, (pair + 1) * PAIR)
        before, after = (
            jnp.where(diag, jnp.concatenate([states[part, pair]] * 2, axis=0), zero)
            for part in range(2)
        )
        work.append(
            (
                dot(q[:, at], before, 1, 0),
                dot(cot[:, at], before, 1, 1),
                dot(kv[1, :, at], after, 1, 1),
                dot(kv[0, :, at], after, 1, 0),
            )
        )
    for pair in range(pairs):
        at = slice(pair * PAIR, (pair + 1) * PAIR)
        run = jnp.where(
            head_of == 0,
            runt[pair // 2, :, 2 * (pair % 2) : 2 * (pair % 2) + 1],
            runt[pair // 2, :, 2 * (pair % 2) + 1 : 2 * (pair % 2) + 2],
        )
        growth = jnp.exp(run) * lin_scale
        fading = jnp.exp(run[SEG - 1 : SEG, :] - run)
        from_q, from_g, from_v, from_k = work[pair]
        layer[:, at] = (near_out[:, at] + growth * from_q).astype(BF)
        dq = dq_in[:, at] + growth * from_g
        dk = own[0, :, at] + fading * from_v + nxt[0, :, at].astype(F32)
        dv = own[1, :, at] + fading * from_k + nxt[1, :, at].astype(F32)
        delta[pair, :, :PAIR] = dq.astype(BF)
        delta[pair, :, PAIR : 2 * PAIR] = dk.astype(BF)
        delta[pair, :, 2 * PAIR :] = dv.astype(BF)


def join(near_out, dq, own, nxt, q, kv, cot, runt, states, after, lin_scale):
    rows, width = q.shape
    pairs = width // PAIR
    wide = 2 * CHUNK
    col = pl.BlockSpec((rows, wide), lambda i: (0, i))
    two = pl.BlockSpec((2, rows, wide), lambda i: (0, 0, i))
    return pl.pallas_call(
        functools.partial(join_kernel, lin_scale),
        grid=(width // wide,),
        in_specs=[
            col,
            col,
            two,
            two,
            col,
            two,
            col,
            pl.BlockSpec((2, rows, runt.shape[2]), lambda i: (i, 0, 0)),
            pl.BlockSpec((2, wide // PAIR, DH, PAIR), lambda i: (0, i, 0, 0)),
        ]
        + [pl.BlockSpec(memory_space=pl.ANY)] * len(after),
        out_specs=[col, pl.BlockSpec((wide // PAIR, rows, 3 * PAIR), lambda i: (i, 0, 0))],
        out_shape=[
            jax.ShapeDtypeStruct((rows, width), BF),
            jax.ShapeDtypeStruct((pairs, rows, 3 * PAIR), BF),
        ],
        compiler_params=params(58),
        cost_estimate=cost(8 * rows * PAIR * PAIR * pairs, 24 * rows * width),
        name="join",
    )(near_out, dq, own, nxt, q, kv, cot, runt, states, *after)


def back_kernel(delta, wq, wk, wv, out, total):
    step = pl.program_id(0)

    @pl.when(step == 0)
    def _():
        total[...] = jnp.zeros_like(total)

    acc = total[...]
    for part, w in enumerate((wq, wk, wv)):
        for half in range(2):
            acc += dot(
                delta[half, :, part * PAIR : (part + 1) * PAIR],
                w[:, half * PAIR : (half + 1) * PAIR],
                1,
                1,
            )
    total[...] = acc

    @pl.when(step == pl.num_programs(0) - 1)
    def _():
        out[...] = acc.astype(BF)


def back(delta, wq, wk, wv):
    pairs, rows, _ = delta.shape
    width = wq.shape[0]
    weight = pl.BlockSpec((width, 2 * PAIR), lambda i: (0, i))
    return pl.pallas_call(
        back_kernel,
        grid=(pairs // 2,),
        in_specs=[pl.BlockSpec((2, rows, 3 * PAIR), lambda i: (i, 0, 0)), weight, weight, weight],
        out_specs=pl.BlockSpec((rows, width), lambda i: (0, 0)),
        out_shape=jax.ShapeDtypeStruct((rows, width), BF),
        scratch_shapes=[VMEM((rows, width), F32)],
        compiler_params=params(58),
        cost_estimate=cost(6 * rows * width * width, 6 * width * width + 8 * rows * width),
        name="back",
    )(delta, wq, wk, wv)


def outer_kernel(core, at_x, mine, theirs, delta, after, out):
    del after
    near_x = mine.shape[0]
    left, right = [], []
    for tokt, c in ((mine, core[0]), (theirs, 1 - core[0])):
        for i in range(near_x):
            left.append(tokt[i])
            right.append(delta[c * near_x + lax.rem(at_x[0] + near_x - i, near_x)])
    left = jnp.concatenate(left, axis=1)
    out[...] = dot(left, jnp.concatenate(right, axis=0), 1, 0).astype(BF)


def outer(core, at_x, mine, theirs, delta, after):
    near_count, rows, cols = delta.shape
    width = mine.shape[1]
    smem = pl.BlockSpec(memory_space=pltpu.SMEM)
    tok = pl.BlockSpec((near_count // 2, width // 2, rows), lambda i: (0, i, 0))
    return pl.pallas_call(
        outer_kernel,
        grid=(2,),
        in_specs=[
            smem,
            smem,
            tok,
            tok,
            pl.BlockSpec((near_count, rows, cols), lambda i: (0, 0, 0)),
            pl.BlockSpec(memory_space=pl.ANY),
        ],
        out_specs=pl.BlockSpec((width // 2, cols), lambda i: (i, 0)),
        out_shape=jax.ShapeDtypeStruct((width, cols), BF),
        compiler_params=params(58),
        cost_estimate=cost(
            2 * near_count * rows * cols * width, 2 * near_count * rows * (width + cols)
        ),
        name="outer",
    )(core, at_x, mine, theirs, delta, after)


def device(yl, c, x, z, yh):
    return (((yl * 2 + c) * 4 + x) * 4 + z) * 2 + yh


def gather_groups():
    zero = [
        [device(yl, 0, x, z, yh) for yl in range(2) for z in range(4) for yh in range(2)]
        for x in range(4)
    ]
    one = [
        [device(yl, 1, x, z, yh) for x in range(4) for yl in range(2) for yh in range(2)]
        for z in range(4)
    ]
    return zero + one


def ring(array, by):
    route = []
    for yl in range(2):
        for x in range(4):
            for z in range(4):
                for yh in range(2):
                    route.append((device(yl, 0, x, z, yh), device(yl, 0, (x + by) % 4, z, yh)))
                    route.append((device(yl, 1, x, z, yh), device(yl, 1, x, (z + by) % 4, yh)))
    return lax.ppermute(array, AX, route)


def place_kernel(pieces, side, at_x, at_z, own, other, *refs):
    grads, mark, sems = refs[-5:-2], refs[-2], refs[-1]
    mark[...] = jnp.zeros_like(mark)

    def put(zero, one):
        copies = []

        def start(src, dst):
            copy = pltpu.make_async_copy(src, dst, sems.at[len(copies)])
            copy.start()
            copies.append(copy)

        rows = zero.shape[1]
        for place, by in enumerate(pieces):
            x = lax.rem(at_x[0] + by + 4, 4)
            z = lax.rem(at_z[0] + by + 4, 4)
            for part, grad in enumerate(grads):
                lanes = pl.ds(part * PAIR, PAIR)
                for i in range(8):
                    start(
                        zero.at[place * 8 + i, :, lanes],
                        grad.at[pl.ds(i * rows, rows), pl.ds(pl.multiple_of(x * PAIR, PAIR), PAIR)],
                    )
                    to = pl.multiple_of(((i % 2) * 4 + z) * rows, rows)
                    start(
                        one.at[place * 8 + i, :, lanes],
                        grad.at[pl.ds(to, rows), pl.ds((4 + i // 2) * PAIR, PAIR)],
                    )
        for copy in copies:
            copy.wait()

    @pl.when(side[0] == 0)
    def _():
        put(own, other)

    @pl.when(side[0] == 1)
    def _():
        put(other, own)


def place_tiles(where, pieces, own, other, grads, width):
    hbm = pl.BlockSpec(memory_space=pl.ANY)
    smem = pl.BlockSpec(memory_space=pltpu.SMEM)
    return pl.pallas_call(
        functools.partial(place_kernel, pieces),
        in_specs=[smem] * 3 + [hbm] * (2 + len(grads)),
        out_specs=[hbm] * 3 + [pl.BlockSpec(memory_space=VMEM)],
        out_shape=[jax.ShapeDtypeStruct((width, width), BF)] * 3
        + [jax.ShapeDtypeStruct((8, PAIR), F32)],
        scratch_shapes=[pltpu.SemaphoreType.DMA((6 * own.shape[0],))],
        input_output_aliases={5 + i: i for i in range(len(grads))},
        compiler_params=params(16),
        cost_estimate=cost(0, 8 * own.size),
        name="place",
    )(*where, own, other, *grads)


def halves_kernel(behind, ahead, after, first, second, both):
    del after
    half = first.shape[0]
    first[...] = behind[:half]
    second[...] = ahead[half:]
    both[: 2 * half] = behind[...]
    both[2 * half :] = ahead[...]


def halves(behind, ahead, after):
    pairs, *rest = behind.shape
    whole = pl.BlockSpec(memory_space=VMEM)
    return pl.pallas_call(
        halves_kernel,
        in_specs=[whole, whole, pl.BlockSpec(memory_space=pl.ANY)],
        out_specs=[whole] * 3,
        out_shape=[jax.ShapeDtypeStruct((n, *rest), BF) for n in (pairs // 2, pairs // 2, 2 * pairs)],
        compiler_params=params(16),
        cost_estimate=cost(0, 12 * behind.size),
        name="halves",
    )(behind, ahead, after)


def gather_tiles(piece, where, width):
    swap = [(0, 1), (1, 0)]

    def swapped(array):
        return lax.ppermute(array, "c", swap)

    rows, cols = piece.shape
    here = lax.all_to_all(
        jnp.broadcast_to(piece[None], (16, rows, cols)), AX, 0, 0, axis_index_groups=gather_groups()
    ).reshape(8, 2 * rows, cols)
    behind = ring(here, 1)
    ahead = ring(here, -1)
    *grads, mark = place_tiles(where, (0,), here, swapped(here), (), width)
    half_a, half_b, both = halves(behind, ahead, mark)
    far_a = ring(half_a, 1)
    far_b = ring(half_b, -1)
    *grads, mark = place_tiles(where, (-1, 1), both, swapped(both), grads, width)
    far = stack([far_a, far_b], mark).reshape(here.shape)
    *grads, _ = place_tiles(where, (2,), far, swapped(far), grads, width)
    return grads


def shards(tokens, wq, wk, wv, log_decay, neighbour_blocks, cot):
    rows, width = tokens.shape
    lin_scale = 1.0 / (DH * math.sqrt(rows))
    place = lax.axis_index(AX).astype(jnp.int32).reshape(1)
    core = lax.axis_index("c").astype(jnp.int32).reshape(1)

    at_x = lax.axis_index("x").astype(jnp.int32).reshape(1)
    swap = [(0, 1), (1, 0)]
    prev_tokens = lax.ppermute(tokens, AX, [(i, i + 1) for i in range(DEVS - 1)])
    q, kv, run, runt, msg = project(tokens, wq, wk, wv, log_decay, cot, lin_scale)
    got = lax.all_to_all(msg.reshape(PLACES, SENT, PAIR), SPAN, 0, 0)
    pkv = prior(prev_tokens, wk, wv, runt)
    near_out, dq, own, prev, mark = near(
        place, neighbour_blocks, q, kv, pkv, cot, run, runt, lin_scale
    )
    nxt = lax.ppermute(prev, AX, [(i + 1, i) for i in range(DEVS - 1)])
    at_span = lax.axis_index(SPAN).astype(jnp.int32).reshape(1)
    at_group = lax.axis_index(GROUP).astype(jnp.int32).reshape(1)
    total = group_total(at_span, got, mark)
    others = [
        lax.ppermute(total, GROUP, [(i, (i + d) % GROUPS) for i in range(GROUPS)])
        for d in range(1, GROUPS)
    ]
    states = scan(at_span, at_group, got, others)
    tokt = flip(tokens, mark)
    around = [lax.ppermute(tokt, "x", [(i, (i + d) % 4) for i in range(4)]) for d in (1, 2, 3)]
    states = lax.all_to_all(states.reshape(PLACES, SLICE, PAIR), SPAN, 0, 0)
    states = states.reshape(2, width // PAIR, DH, PAIR)
    layer, delta = join(near_out, dq, own, nxt, q, kv, cot, runt, states, [], lin_scale)

    delta8 = lax.all_to_all(delta, NEAR8, 0, 0)
    mine = stack([tokt, *around], delta)
    theirs = lax.ppermute(mine, "c", swap)
    tokens_grad = back(delta, wq, wk, wv)
    partial = outer(core, at_x, mine, theirs, delta8, tokens_grad)
    parts = lax.all_to_all(partial.reshape(16, width // 16, 3 * PAIR), FAR16, 0, 0)
    grad_norm = 1.0 / math.sqrt(rows * DEVS)
    piece = (jnp.sum(parts.astype(F32), axis=0) * grad_norm).astype(BF)
    at_z = lax.axis_index("z").astype(jnp.int32).reshape(1)
    gq, gk, gv = gather_tiles(piece, (core, at_x, at_z), width)
    return layer, tokens_grad, gq, gk, gv


def solution(mesh):
    chips = Mesh(mesh.devices.reshape(2, 2, 4, 4, 2), AX)
    tok = P(AX, None)
    return jax.shard_map(
        shards,
        mesh=chips,
        in_specs=(tok, P(), P(), P(), P(None, AX), tok, tok),
        out_specs=(tok, tok, P(), P(), P()),
        check_vma=False,
    )
```

```python
import functools
import math

import jax
import jax.numpy as jnp
from jax import lax
from jax.experimental import pallas as pl
from jax.experimental.pallas import tpu as pltpu
from jax.sharding import Mesh
from jax.sharding import PartitionSpec as P

BF = jnp.bfloat16
F32 = jnp.float32
AX = ("yl", "c", "x", "z", "yh")
NEAR8 = ("c", "x")
FAR16 = ("yl", "z", "yh")
PLANE = ("x", "yl", "z", "yh")
SEG = 128
PAIR = 128
DH = 64
DEVS = 128
VMEM = pltpu.VMEM
HIGH = lax.Precision.HIGHEST


def dot(a, b, ca, cb, precision=None):
    return lax.dot_general(
        a, b, (((ca,), (cb,)), ((), ())), precision=precision, preferred_element_type=F32
    )


def iota(shape, axis):
    return lax.broadcasted_iota(jnp.int32, shape, axis)


def params(mib):
    return pltpu.CompilerParams(vmem_limit_bytes=mib << 20)


def cost(flops, moved, trans=0):
    return pl.CostEstimate(flops=flops, bytes_accessed=moved, transcendentals=trans)


CHUNK = 256
WIDE = 512


def pair_lanes(columns, pair):
    shape = (columns.shape[0], PAIR)
    return jnp.where(
        iota(shape, 1) < DH,
        columns[:, 2 * pair : 2 * pair + 1],
        columns[:, 2 * pair + 1 : 2 * pair + 2],
    )


def project_kernel(lin_scale, tok, wq, wk, wv, decay, cot, q_out, kv_out, run_out, runt_out, msg, tok_out, held, sems):
    width = tok.shape[1]
    wide = held.shape[3]
    copies = []
    for step in range(width // wide):
        for part, w in enumerate((wq, wk, wv)):
            copy = pltpu.make_async_copy(
                w.at[:, pl.ds(step * wide, wide)], held.at[part, step], sems.at[part, step]
            )
            copy.start()
            copies.append(copy)
    x = tok[...]
    tok_out[...] = x
    ld = decay[...]
    lower = (iota((SEG, SEG), 0) >= iota((SEG, SEG), 1)).astype(F32)
    runt = dot(lower, ld, 1, 1, HIGH)
    run = dot(ld, lower, 1, 1, HIGH)
    group = ld.shape[0] // run_out.shape[0]
    for step in range(run_out.shape[0]):
        runt_out[step] = runt[:, step * group : (step + 1) * group]
        run_out[step] = run[step * group : (step + 1) * group, :]
    rows = iota((8, PAIR), 0)
    first = iota((DH, PAIR), 1) < DH
    for step in range(width // wide):
        for part in range(3):
            copies[step * 3 + part].wait()
        at = slice(step * wide, (step + 1) * wide)
        q = dot(x, held[0, step], 1, 0).astype(BF)
        k = dot(x, held[1, step], 1, 0).astype(BF)
        v = dot(x, held[2, step], 1, 0).astype(BF)
        q_out[:, at] = q
        kv_out[0, :, at] = k
        kv_out[1, :, at] = v
        here = []
        for part in range(wide // PAIR):
            cols = slice(part * PAIR, (part + 1) * PAIR)
            pair = step * (wide // PAIR) + part
            lanes = pair_lanes(runt, pair)
            total = lanes[SEG - 1 : SEG, :]
            g = cot[:, pair * PAIR : (pair + 1) * PAIR].astype(F32)
            weighted = (v[:, cols].astype(F32) * jnp.exp(total - lanes)).astype(BF)
            scaled = (g * jnp.exp(lanes)).astype(BF)
            states = (
                dot(k[:, cols], weighted, 0, 0),
                dot(q[:, cols], scaled, 0, 0) * lin_scale,
            )
            here.append((pair, total, states))
        for pair, total, states in here:
            high = total.astype(BF).astype(F32)
            mid = (total - high).astype(BF).astype(F32)
            low = total - high - mid
            tail = jnp.where(
                rows == 0, high, jnp.where(rows == 1, mid, jnp.where(rows == 2, low, 0.0))
            )
            tail = jnp.broadcast_to(tail[None], (8, 8, PAIR))
            for part, full in enumerate(states):
                own = jnp.where(first, full[:DH], full[DH:]).reshape(8, 8, PAIR)
                sent = jnp.concatenate([own, tail], axis=1).reshape(PAIR, PAIR)
                msg[part, pair * PAIR : (pair + 1) * PAIR, :] = sent.astype(BF)


def project(tokens, wq, wk, wv, log_decay, cot, lin_scale):
    rows, width = tokens.shape
    heads = log_decay.shape[0]
    chunks = width // CHUNK
    wide = WIDE
    vmem = pl.BlockSpec(memory_space=VMEM)
    hbm = pl.BlockSpec(memory_space=pltpu.HBM)
    return pl.pallas_call(
        functools.partial(project_kernel, lin_scale),
        in_specs=[vmem, hbm, hbm, hbm, vmem, vmem],
        out_specs=[vmem] * 6,
        out_shape=[
            jax.ShapeDtypeStruct((rows, width), BF),
            jax.ShapeDtypeStruct((2, rows, width), BF),
            jax.ShapeDtypeStruct((chunks, heads // chunks, rows), F32),
            jax.ShapeDtypeStruct((chunks, rows, heads // chunks), F32),
            jax.ShapeDtypeStruct((2, width, PAIR), BF),
            jax.ShapeDtypeStruct((rows, width), BF),
        ],
        scratch_shapes=[
            VMEM((3, width // wide, width, wide), BF),
            pltpu.SemaphoreType.DMA((3, width // wide)),
        ],
        compiler_params=params(58),
        cost_estimate=cost(6 * rows * width * width, 6 * width * width + 12 * rows * width),
        name="project",
    )(tokens, wq, wk, wv, log_decay, cot)


def prior_kernel(tok, wk, wv, after, out, held, sems):
    del after
    copies = [
        pltpu.make_async_copy(w, held.at[part], sems.at[part]) for part, w in enumerate((wk, wv))
    ]
    for copy in copies:
        copy.start()
    for part in range(2):
        copies[part].wait()
        out[part] = dot(tok[...], held[part], 1, 0).astype(BF)


def prior(tokens, wk, wv, after):
    rows, width = tokens.shape
    vmem = pl.BlockSpec(memory_space=VMEM)
    hbm = pl.BlockSpec(memory_space=pltpu.HBM)
    return pl.pallas_call(
        prior_kernel,
        in_specs=[vmem, hbm, hbm, hbm],
        out_specs=vmem,
        out_shape=jax.ShapeDtypeStruct((2, rows, width), BF),
        scratch_shapes=[
            VMEM((2, width, width), BF),
            pltpu.SemaphoreType.DMA((2,)),
        ],
        compiler_params=params(58),
        cost_estimate=cost(4 * rows * width * width, 4 * width * width + 6 * rows * width),
        name="prior",
    )(tokens, wk, wv, after)


def flip_kernel(tok, after, out):
    del after
    out[...] = tok[...].T


def flip(tokens, after):
    rows, width = tokens.shape
    return pl.pallas_call(
        flip_kernel,
        in_specs=[pl.BlockSpec(memory_space=VMEM), pl.BlockSpec(memory_space=pl.ANY)],
        out_specs=pl.BlockSpec(memory_space=VMEM),
        out_shape=jax.ShapeDtypeStruct((width, rows), BF),
        compiler_params=params(16),
        cost_estimate=cost(0, 4 * rows * width),
        name="flip",
    )(tokens, after)


def stack_kernel(*refs):
    out = refs[-1]
    for i in range(out.shape[0]):
        out[i] = refs[i][...]


def stack(parts, after):
    shape = parts[0].shape
    whole = pl.BlockSpec(memory_space=VMEM)
    return pl.pallas_call(
        stack_kernel,
        in_specs=[whole] * len(parts) + [pl.BlockSpec(memory_space=pl.ANY)],
        out_specs=whole,
        out_shape=jax.ShapeDtypeStruct((len(parts), *shape), BF),
        compiler_params=params(16),
        cost_estimate=cost(0, 4 * len(parts) * math.prod(shape)),
        name="stack",
    )(*parts, after)


def scan_kernel(place, got, after, out, xs, decays, states):
    del after
    both = got[...].astype(F32)
    xs[...] = both[:, :8, :]
    total = both[:, 8:9, :] + both[:, 9:10, :] + both[:, 10:11, :]
    decays[...] = jnp.broadcast_to(jnp.exp(total), decays.shape)
    backward = place[0] >= DEVS // 2

    def one(i, state):
        at = jnp.where(backward, DEVS - 1 - i, i)
        states[at] = state
        return decays[at] * state + xs[at]

    lax.fori_loop(0, DEVS, one, jnp.zeros((8, PAIR), F32), unroll=8)
    out[...] = states[...].reshape(DEVS * 8, PAIR).astype(BF)


def scan(place, got, after):
    whole = pl.BlockSpec(memory_space=VMEM)
    return pl.pallas_call(
        scan_kernel,
        in_specs=[
            pl.BlockSpec(memory_space=pltpu.SMEM),
            whole,
            pl.BlockSpec(memory_space=pl.ANY),
        ],
        out_specs=whole,
        out_shape=jax.ShapeDtypeStruct((DEVS * 8, PAIR), BF),
        scratch_shapes=[VMEM((DEVS, 8, PAIR), F32)] * 3,
        compiler_params=params(24),
        cost_estimate=cost(2 * DEVS * 8 * PAIR, 4 * DEVS * 16 * PAIR),
        name="scan",
    )(place, got, after)


def near_kernel(lin_scale, place, blocks, q_ref, kv, pkv, cot, run, runt, out, dq_out, own, prev, mark):
    mark[...] = jnp.zeros_like(mark)
    soft_scale = 1.0 / math.sqrt(DH)
    n_own = jnp.int32(0)
    n_prev = jnp.int32(0)
    for j in range(blocks.shape[1]):
        n_own += (blocks[0, j] == place[0]).astype(jnp.int32)
        n_prev += (blocks[0, j] == place[0] - 1).astype(jnp.int32)
    is_own = iota((1, 2 * SEG), 1) < SEG
    times = jnp.where(is_own, n_own, n_prev)
    bias = jnp.where(times > 0, 0.0, -1e30)
    times = times.astype(F32)
    head_of = iota((SEG, PAIR), 1) // DH
    head_of2 = iota((2 * SEG, PAIR), 1) // DH
    lower = iota((SEG, SEG), 0) >= iota((SEG, SEG), 1)
    zero = jnp.zeros((), BF)
    pairs = q_ref.shape[1] // PAIR
    work = []
    for pair in range(pairs):
        at = slice(pair * PAIR, (pair + 1) * PAIR)
        q = q_ref[:, at]
        g = cot[:, at]
        kk = jnp.concatenate([kv[0, :, at], pkv[0, :, at]], axis=0)
        vv = jnp.concatenate([kv[1, :, at], pkv[1, :, at]], axis=0)
        for i in range(2):
            mine = head_of == i
            work.append(
                (
                    dot(jnp.where(mine, q, zero), kk, 1, 1),
                    dot(jnp.where(mine, g, zero), vv, 1, 1),
                )
            )
    mats = []
    for head in range(2 * pairs):
        scores, pgrad = work[head]
        col = runt[0, :, head : head + 1]
        row = run[0, head : head + 1, :]
        dec = jnp.where(lower, jnp.exp(jnp.minimum(col - row, 0.0)), 0.0) * lin_scale
        logits = scores * soft_scale + bias
        peak = jnp.max(logits, axis=1, keepdims=True)
        terms = jnp.exp(logits - peak) * times
        probs = terms * (1.0 / jnp.sum(terms, axis=1, keepdims=True))
        inner = jnp.sum(probs * pgrad, axis=1, keepdims=True)
        dlog = probs * (pgrad - inner) * soft_scale
        a = jnp.concatenate([probs[:, :SEG] + scores[:, :SEG] * dec, probs[:, SEG:]], axis=1)
        b = jnp.concatenate([dlog[:, :SEG] + pgrad[:, :SEG] * dec, dlog[:, SEG:]], axis=1)
        mats.append((a.astype(BF), b.astype(BF)))
    for pair in range(pairs):
        at = slice(pair * PAIR, (pair + 1) * PAIR)
        q = q_ref[:, at]
        g = cot[:, at]
        kk = jnp.concatenate([kv[0, :, at], pkv[0, :, at]], axis=0)
        vv = jnp.concatenate([kv[1, :, at], pkv[1, :, at]], axis=0)
        qt = q.T
        gt = g.T
        res = []
        for i in range(2):
            a, b = mats[2 * pair + i]
            half = slice(i * DH, (i + 1) * DH)
            res.append((dot(a, vv, 1, 0), dot(b, kk, 1, 0), dot(qt[half], b, 1, 0), dot(gt[half], a, 1, 0)))
        out[:, at] = jnp.where(head_of == 0, res[0][0], res[1][0])
        dq_out[:, at] = jnp.where(head_of == 0, res[0][1], res[1][1])
        for part in range(2):
            sums = jnp.concatenate([res[0][2 + part], res[1][2 + part]], axis=0).T
            own[part, :, at] = sums[:SEG]
            prev[part, :, at] = sums[SEG:].astype(BF)


def near(place, blocks, q, kv, pkv, cot, run, runt, lin_scale):
    rows, width = q.shape
    heads = run.shape[1]
    smem = pl.BlockSpec(memory_space=pltpu.SMEM)
    col = pl.BlockSpec((rows, CHUNK), lambda i: (0, i))
    two = pl.BlockSpec((2, rows, CHUNK), lambda i: (0, 0, i))
    return pl.pallas_call(
        functools.partial(near_kernel, lin_scale),
        grid=(width // CHUNK,),
        in_specs=[
            smem,
            smem,
            col,
            two,
            two,
            col,
            pl.BlockSpec((1, heads, rows), lambda i: (i, 0, 0)),
            pl.BlockSpec((1, rows, heads), lambda i: (i, 0, 0)),
        ],
        out_specs=[col, col, two, two, pl.BlockSpec((8, PAIR), lambda i: (0, 0))],
        out_shape=[
            jax.ShapeDtypeStruct((rows, width), F32),
            jax.ShapeDtypeStruct((rows, width), F32),
            jax.ShapeDtypeStruct((2, rows, width), F32),
            jax.ShapeDtypeStruct((2, rows, width), BF),
            jax.ShapeDtypeStruct((8, PAIR), F32),
        ],
        compiler_params=params(58),
        cost_estimate=cost(4000 * 1000 * 1000, 16 * 1000 * 1000, 1000 * 1000),
        name="near",
    )(place, blocks, q, kv, pkv, cot, run, runt)


def join_kernel(lin_scale, near_out, dq_in, own, nxt, q, kv, cot, runt, states, layer, delta):
    head_of = iota((SEG, PAIR), 1) // DH
    diag = iota((PAIR, PAIR), 0) // DH == iota((PAIR, PAIR), 1) // DH
    zero = jnp.zeros((), BF)
    pairs = q.shape[1] // PAIR
    work = []
    for pair in range(pairs):
        at = slice(pair * PAIR, (pair + 1) * PAIR)
        before, after = (
            jnp.where(diag, jnp.concatenate([states[part, pair]] * 2, axis=0), zero)
            for part in range(2)
        )
        work.append(
            (
                dot(q[:, at], before, 1, 0),
                dot(cot[:, at], before, 1, 1),
                dot(kv[1, :, at], after, 1, 1),
                dot(kv[0, :, at], after, 1, 0),
            )
        )
    for pair in range(pairs):
        at = slice(pair * PAIR, (pair + 1) * PAIR)
        run = jnp.where(
            head_of == 0,
            runt[pair // 2, :, 2 * (pair % 2) : 2 * (pair % 2) + 1],
            runt[pair // 2, :, 2 * (pair % 2) + 1 : 2 * (pair % 2) + 2],
        )
        growth = jnp.exp(run) * lin_scale
        fading = jnp.exp(run[SEG - 1 : SEG, :] - run)
        from_q, from_g, from_v, from_k = work[pair]
        layer[:, at] = (near_out[:, at] + growth * from_q).astype(BF)
        dq = dq_in[:, at] + growth * from_g
        dk = own[0, :, at] + fading * from_v + nxt[0, :, at].astype(F32)
        dv = own[1, :, at] + fading * from_k + nxt[1, :, at].astype(F32)
        delta[pair, :, :PAIR] = dq.astype(BF)
        delta[pair, :, PAIR : 2 * PAIR] = dk.astype(BF)
        delta[pair, :, 2 * PAIR :] = dv.astype(BF)


def join(near_out, dq, own, nxt, q, kv, cot, runt, states, lin_scale):
    rows, width = q.shape
    pairs = width // PAIR
    wide = 2 * CHUNK
    col = pl.BlockSpec((rows, wide), lambda i: (0, i))
    two = pl.BlockSpec((2, rows, wide), lambda i: (0, 0, i))
    return pl.pallas_call(
        functools.partial(join_kernel, lin_scale),
        grid=(width // wide,),
        in_specs=[
            col,
            col,
            two,
            two,
            col,
            two,
            col,
            pl.BlockSpec((2, rows, runt.shape[2]), lambda i: (i, 0, 0)),
            pl.BlockSpec((2, wide // PAIR, DH, PAIR), lambda i: (0, i, 0, 0)),
        ],
        out_specs=[col, pl.BlockSpec((wide // PAIR, rows, 3 * PAIR), lambda i: (i, 0, 0))],
        out_shape=[
            jax.ShapeDtypeStruct((rows, width), BF),
            jax.ShapeDtypeStruct((pairs, rows, 3 * PAIR), BF),
        ],
        compiler_params=params(58),
        cost_estimate=cost(8 * rows * PAIR * PAIR * pairs, 24 * rows * width),
        name="join",
    )(near_out, dq, own, nxt, q, kv, cot, runt, states)


def back_kernel(delta, wq, wk, wv, out, mark, total):
    step = pl.program_id(0)
    mark[...] = jnp.zeros_like(mark)

    @pl.when(step == 0)
    def _():
        total[...] = jnp.zeros_like(total)

    acc = total[...]
    for part, w in enumerate((wq, wk, wv)):
        for half in range(2):
            acc += dot(
                delta[half, :, part * PAIR : (part + 1) * PAIR],
                w[:, half * PAIR : (half + 1) * PAIR],
                1,
                1,
            )
    total[...] = acc

    @pl.when(step == pl.num_programs(0) - 1)
    def _():
        out[...] = acc.astype(BF)


def back(delta, wq, wk, wv):
    pairs, rows, _ = delta.shape
    width = wq.shape[0]
    weight = pl.BlockSpec((width, 2 * PAIR), lambda i: (0, i))
    return pl.pallas_call(
        back_kernel,
        grid=(pairs // 2,),
        in_specs=[pl.BlockSpec((2, rows, 3 * PAIR), lambda i: (i, 0, 0)), weight, weight, weight],
        out_specs=[
            pl.BlockSpec((rows, width), lambda i: (0, 0)),
            pl.BlockSpec((8, PAIR), lambda i: (0, 0)),
        ],
        out_shape=[
            jax.ShapeDtypeStruct((rows, width), BF),
            jax.ShapeDtypeStruct((8, PAIR), F32),
        ],
        scratch_shapes=[VMEM((rows, width), F32)],
        compiler_params=params(58),
        cost_estimate=cost(6 * rows * width * width, 6 * width * width + 8 * rows * width),
        name="back",
    )(delta, wq, wk, wv)


def outer_kernel(core, at_x, mine, theirs, delta, after, out):
    del after
    near_x = mine.shape[0]
    left, right = [], []
    for tokt, c in ((mine, core[0]), (theirs, 1 - core[0])):
        for i in range(near_x):
            left.append(tokt[i])
            right.append(delta[c * near_x + lax.rem(at_x[0] + near_x - i, near_x)])
    left = jnp.concatenate(left, axis=1)
    out[...] = dot(left, jnp.concatenate(right, axis=0), 1, 0).astype(BF)


def outer(core, at_x, mine, theirs, delta, after):
    near_count, rows, cols = delta.shape
    width = mine.shape[1]
    smem = pl.BlockSpec(memory_space=pltpu.SMEM)
    tok = pl.BlockSpec((near_count // 2, width // 2, rows), lambda i: (0, i, 0))
    return pl.pallas_call(
        outer_kernel,
        grid=(2,),
        in_specs=[
            smem,
            smem,
            tok,
            tok,
            pl.BlockSpec((near_count, rows, cols), lambda i: (0, 0, 0)),
            pl.BlockSpec(memory_space=pl.ANY),
        ],
        out_specs=pl.BlockSpec((width // 2, cols), lambda i: (i, 0)),
        out_shape=jax.ShapeDtypeStruct((width, cols), BF),
        compiler_params=params(20),
        cost_estimate=cost(
            2 * near_count * rows * cols * width, 2 * near_count * rows * (width + cols)
        ),
        name="outer",
    )(core, at_x, mine, theirs, delta, after)


def device(yl, c, x, z, yh):
    return (((yl * 2 + c) * 4 + x) * 4 + z) * 2 + yh


def gather_groups():
    zero = [
        [device(yl, 0, x, z, yh) for yl in range(2) for z in range(4) for yh in range(2)]
        for x in range(4)
    ]
    one = [
        [device(yl, 1, x, z, yh) for x in range(4) for yl in range(2) for yh in range(2)]
        for z in range(4)
    ]
    return zero + one


def ring(array, by):
    route = []
    for yl in range(2):
        for x in range(4):
            for z in range(4):
                for yh in range(2):
                    route.append((device(yl, 0, x, z, yh), device(yl, 0, (x + by) % 4, z, yh)))
                    route.append((device(yl, 1, x, z, yh), device(yl, 1, x, (z + by) % 4, yh)))
    return lax.ppermute(array, AX, route)


def place_kernel(pieces, count, side, at_x, at_z, *refs):
    grads, mark, sems = refs[-5:-2], refs[-2], refs[-1]
    mark[...] = jnp.zeros_like(mark)

    def put(rank):
        copies = []

        def start(src, dst):
            copy = pltpu.make_async_copy(src, dst, sems.at[len(copies)])
            copy.start()
            copies.append(copy)

        for n in range(count):
            source = refs[n]
            rows = source.shape[1]
            by_row = rank[n]
            for place, by in enumerate(pieces):
                x = lax.rem(at_x[0] + by + 4, 4)
                z = lax.rem(at_z[0] + by + 4, 4)
                for part, grad in enumerate(grads):
                    lanes = pl.ds(part * PAIR, PAIR)
                    for i in range(8):
                        if by_row:
                            to = pl.multiple_of(((i % 2) * 4 + z) * rows, rows)
                            at = (pl.ds(to, rows), pl.ds((4 + i // 2) * PAIR, PAIR))
                        else:
                            to = pl.multiple_of(x * PAIR, PAIR)
                            at = (pl.ds(i * rows, rows), pl.ds(to, PAIR))
                        start(source.at[place * 8 + i, :, lanes], grad.at[at])
        for copy in copies:
            copy.wait()

    @pl.when(side[0] == 0)
    def _():
        put((False, True))

    @pl.when(side[0] == 1)
    def _():
        put((True, False))


def place_tiles(where, pieces, sources, grads, width):
    hbm = pl.BlockSpec(memory_space=pl.ANY)
    smem = pl.BlockSpec(memory_space=pltpu.SMEM)
    first = 3 + len(sources)
    return pl.pallas_call(
        functools.partial(place_kernel, pieces, len(sources)),
        in_specs=[smem] * 3 + [hbm] * (len(sources) + len(grads)),
        out_specs=[hbm] * 3 + [pl.BlockSpec(memory_space=VMEM)],
        out_shape=[jax.ShapeDtypeStruct((width, width), BF)] * 3
        + [jax.ShapeDtypeStruct((8, PAIR), F32)],
        scratch_shapes=[pltpu.SemaphoreType.DMA((24 * len(pieces) * len(sources),))],
        input_output_aliases={first + i: i for i in range(len(grads))},
        compiler_params=params(16),
        cost_estimate=cost(0, 4 * sum(a.size for a in sources)),
        name="place",
    )(*where, *sources, *grads)


def halves_kernel(behind, ahead, after, first, second, both):
    del after
    half = first.shape[0]
    first[...] = behind[:half]
    second[...] = ahead[half:]
    both[: 2 * half] = behind[...]
    both[2 * half :] = ahead[...]


def halves(behind, ahead, after):
    pairs, *rest = behind.shape
    whole = pl.BlockSpec(memory_space=VMEM)
    return pl.pallas_call(
        halves_kernel,
        in_specs=[whole, whole, pl.BlockSpec(memory_space=pl.ANY)],
        out_specs=[whole] * 3,
        out_shape=[jax.ShapeDtypeStruct((n, *rest), BF) for n in (pairs // 2, pairs // 2, 2 * pairs)],
        compiler_params=params(16),
        cost_estimate=cost(0, 12 * behind.size),
        name="halves",
    )(behind, ahead, after)


def gather_tiles(piece, where, width):
    swap = [(0, 1), (1, 0)]

    def swapped(array):
        return lax.ppermute(array, "c", swap)

    rows, cols = piece.shape
    here = lax.all_to_all(
        jnp.broadcast_to(piece[None], (16, rows, cols)), AX, 0, 0, axis_index_groups=gather_groups()
    ).reshape(8, 2 * rows, cols)
    behind = ring(here, 1)
    ahead = ring(here, -1)
    *grads, mark = place_tiles(where, (0,), (here, swapped(here)), (), width)
    half_a, half_b, both = halves(behind, ahead, mark)
    far_a = ring(half_a, 1)
    far_b = ring(half_b, -1)
    *grads, mark = place_tiles(where, (-1, 1), (both, swapped(both)), grads, width)
    far = stack([far_a, far_b], mark).reshape(here.shape)
    far_c = swapped(far)
    *grads, _ = place_tiles(where, (2,), (far,), grads, width)
    core, *rest = where
    *grads, _ = place_tiles((1 - core, *rest), (2,), (far_c,), grads, width)
    return grads


def shards(tokens, wq, wk, wv, log_decay, neighbour_blocks, cot):
    rows, width = tokens.shape
    lin_scale = 1.0 / (DH * math.sqrt(rows))
    place = lax.axis_index(AX).astype(jnp.int32).reshape(1)
    core = lax.axis_index("c").astype(jnp.int32).reshape(1)

    at_x = lax.axis_index("x").astype(jnp.int32).reshape(1)
    swap = [(0, 1), (1, 0)]
    q, kv, run, runt, msg, own_tokens = project(tokens, wq, wk, wv, log_decay, cot, lin_scale)
    prev_tokens = lax.ppermute(own_tokens, AX, [(i, i + 1) for i in range(DEVS - 1)])
    got = lax.all_to_all(msg.reshape(DEVS, 16, PAIR), AX, 0, 0)
    pkv = prior(prev_tokens, wk, wv, runt)
    near_out, dq, own, prev, mark = near(
        place, neighbour_blocks, q, kv, pkv, cot, run, runt, lin_scale
    )
    nxt = lax.ppermute(prev, AX, [(i + 1, i) for i in range(DEVS - 1)])
    states = scan(place, got, mark)
    tokt = flip(tokens, mark)
    around = [lax.ppermute(tokt, "x", [(i, (i + d) % 4) for i in range(4)]) for d in (1, 2, 3)]
    states = lax.all_to_all(states.reshape(DEVS, 8, PAIR), AX, 0, 0)
    states = states.reshape(2, width // PAIR, DH, PAIR)
    layer, delta = join(near_out, dq, own, nxt, q, kv, cot, runt, states, lin_scale)

    delta8 = lax.all_to_all(delta, NEAR8, 0, 0)
    mine = stack([tokt, *around], delta)
    theirs = lax.ppermute(mine, "c", swap)
    tokens_grad, mark = back(delta, wq, wk, wv)
    partial = outer(core, at_x, mine, theirs, delta8, mark)
    parts = lax.all_to_all(partial.reshape(16, width // 16, 3 * PAIR), FAR16, 0, 0)
    grad_norm = 1.0 / math.sqrt(rows * DEVS)
    piece = (jnp.sum(parts.astype(F32), axis=0) * grad_norm).astype(BF)
    at_z = lax.axis_index("z").astype(jnp.int32).reshape(1)
    gq, gk, gv = gather_tiles(piece, (core, at_x, at_z), width)
    return layer, tokens_grad, gq, gk, gv


def solution(mesh):
    chips = Mesh(mesh.devices.reshape(2, 2, 4, 4, 2), AX)
    tok = P(AX, None)
    return jax.shard_map(
        shards,
        mesh=chips,
        in_specs=(tok, P(), P(), P(), P(None, AX), tok, tok),
        out_specs=(tok, tok, P(), P(), P()),
        check_vma=False,
    )
```

```python
import functools
import math

import jax
import jax.numpy as jnp
from jax import lax
from jax.experimental import pallas as pl
from jax.experimental.pallas import tpu as pltpu
from jax.sharding import Mesh
from jax.sharding import PartitionSpec as P

BF = jnp.bfloat16
F32 = jnp.float32
AX = ("yl", "c", "x", "z", "yh")
NEAR8 = ("c", "x")
FAR16 = ("yl", "z", "yh")
PLANE = ("x", "yl", "z", "yh")
SEG = 128
PAIR = 128
DH = 64
DEVS = 128
VMEM = pltpu.VMEM
HIGH = lax.Precision.HIGHEST


def dot(a, b, ca, cb, precision=None):
    return lax.dot_general(
        a, b, (((ca,), (cb,)), ((), ())), precision=precision, preferred_element_type=F32
    )


def iota(shape, axis):
    return lax.broadcasted_iota(jnp.int32, shape, axis)


def params(mib):
    return pltpu.CompilerParams(vmem_limit_bytes=mib << 20)


def cost(flops, moved, trans=0):
    return pl.CostEstimate(flops=flops, bytes_accessed=moved, transcendentals=trans)


CHUNK = 256
WIDE = 512


def pair_lanes(columns, pair):
    shape = (columns.shape[0], PAIR)
    return jnp.where(
        iota(shape, 1) < DH,
        columns[:, 2 * pair : 2 * pair + 1],
        columns[:, 2 * pair + 1 : 2 * pair + 2],
    )


def project_kernel(lin_scale, tok, wq, wk, wv, decay, cot, q_out, kv_out, run_out, runt_out, msg, tok_out, held, sems):
    width = tok.shape[1]
    wide = held.shape[3]
    copies = []
    for step in range(width // wide):
        for part, w in enumerate((wq, wk, wv)):
            copy = pltpu.make_async_copy(
                w.at[:, pl.ds(step * wide, wide)], held.at[part, step], sems.at[part, step]
            )
            copy.start()
            copies.append(copy)
    x = tok[...]
    tok_out[...] = x
    ld = decay[...]
    lower = (iota((SEG, SEG), 0) >= iota((SEG, SEG), 1)).astype(F32)
    runt = dot(lower, ld, 1, 1, HIGH)
    run = dot(ld, lower, 1, 1, HIGH)
    group = ld.shape[0] // run_out.shape[0]
    for step in range(run_out.shape[0]):
        runt_out[step] = runt[:, step * group : (step + 1) * group]
        run_out[step] = run[step * group : (step + 1) * group, :]
    rows = iota((8, PAIR), 0)
    first = iota((DH, PAIR), 1) < DH
    for step in range(width // wide):
        for part in range(3):
            copies[step * 3 + part].wait()
        at = slice(step * wide, (step + 1) * wide)
        q = dot(x, held[0, step], 1, 0).astype(BF)
        k = dot(x, held[1, step], 1, 0).astype(BF)
        v = dot(x, held[2, step], 1, 0).astype(BF)
        q_out[:, at] = q
        kv_out[0, :, at] = k
        kv_out[1, :, at] = v
        here = []
        for part in range(wide // PAIR):
            cols = slice(part * PAIR, (part + 1) * PAIR)
            pair = step * (wide // PAIR) + part
            lanes = pair_lanes(runt, pair)
            total = lanes[SEG - 1 : SEG, :]
            g = cot[:, pair * PAIR : (pair + 1) * PAIR].astype(F32)
            weighted = (v[:, cols].astype(F32) * jnp.exp(total - lanes)).astype(BF)
            scaled = (g * jnp.exp(lanes)).astype(BF)
            states = (
                dot(k[:, cols], weighted, 0, 0),
                dot(q[:, cols], scaled, 0, 0) * lin_scale,
            )
            here.append((pair, total, states))
        for pair, total, states in here:
            high = total.astype(BF).astype(F32)
            mid = (total - high).astype(BF).astype(F32)
            low = total - high - mid
            tail = jnp.where(
                rows == 0, high, jnp.where(rows == 1, mid, jnp.where(rows == 2, low, 0.0))
            )
            tail = jnp.broadcast_to(tail[None], (8, 8, PAIR))
            for part, full in enumerate(states):
                own = jnp.where(first, full[:DH], full[DH:]).reshape(8, 8, PAIR)
                sent = jnp.concatenate([own, tail], axis=1).reshape(PAIR, PAIR)
                msg[part, pair * PAIR : (pair + 1) * PAIR, :] = sent.astype(BF)


def project(tokens, wq, wk, wv, log_decay, cot, lin_scale):
    rows, width = tokens.shape
    heads = log_decay.shape[0]
    chunks = width // CHUNK
    wide = WIDE
    vmem = pl.BlockSpec(memory_space=VMEM)
    hbm = pl.BlockSpec(memory_space=pltpu.HBM)
    return pl.pallas_call(
        functools.partial(project_kernel, lin_scale),
        in_specs=[vmem, hbm, hbm, hbm, vmem, vmem],
        out_specs=[vmem] * 6,
        out_shape=[
            jax.ShapeDtypeStruct((rows, width), BF),
            jax.ShapeDtypeStruct((2, rows, width), BF),
            jax.ShapeDtypeStruct((chunks, heads // chunks, rows), F32),
            jax.ShapeDtypeStruct((chunks, rows, heads // chunks), F32),
            jax.ShapeDtypeStruct((2, width, PAIR), BF),
            jax.ShapeDtypeStruct((rows, width), BF),
        ],
        scratch_shapes=[
            VMEM((3, width // wide, width, wide), BF),
            pltpu.SemaphoreType.DMA((3, width // wide)),
        ],
        compiler_params=params(58),
        cost_estimate=cost(6 * rows * width * width, 6 * width * width + 12 * rows * width),
        name="project",
    )(tokens, wq, wk, wv, log_decay, cot)


def flip_kernel(tag, tok, out, tag_out):
    tag_out[0] = tag[0]
    out[...] = tok[...].T


def flip(tag, tokens):
    rows, width = tokens.shape
    whole = pl.BlockSpec(memory_space=VMEM)
    smem = pl.BlockSpec(memory_space=pltpu.SMEM)
    return pl.pallas_call(
        flip_kernel,
        in_specs=[smem, whole],
        out_specs=[whole, smem],
        out_shape=[
            jax.ShapeDtypeStruct((width, rows), BF),
            jax.ShapeDtypeStruct((1,), jnp.int32),
        ],
        compiler_params=params(16),
        cost_estimate=cost(0, 4 * rows * width),
        name="flip",
    )(tag, tokens)


def stack_kernel(*refs):
    out = refs[-1]
    for i in range(out.shape[0]):
        out[i] = refs[i][...]


def stack(parts, after):
    shape = parts[0].shape
    whole = pl.BlockSpec(memory_space=VMEM)
    return pl.pallas_call(
        stack_kernel,
        in_specs=[whole] * len(parts) + [pl.BlockSpec(memory_space=pl.ANY)],
        out_specs=whole,
        out_shape=jax.ShapeDtypeStruct((len(parts), *shape), BF),
        compiler_params=params(16),
        cost_estimate=cost(0, 4 * len(parts) * math.prod(shape)),
        name="stack",
    )(*parts, after)


def scan_kernel(place, got, out, xs, decays, states):
    both = got[...].astype(F32)
    xs[...] = both[:, :8, :]
    total = both[:, 8:9, :] + both[:, 9:10, :] + both[:, 10:11, :]
    decays[...] = jnp.broadcast_to(jnp.exp(total), decays.shape)
    backward = place[0] >= DEVS // 2

    def one(i, state):
        at = jnp.where(backward, DEVS - 1 - i, i)
        states[at] = state
        return decays[at] * state + xs[at]

    lax.fori_loop(0, DEVS, one, jnp.zeros((8, PAIR), F32), unroll=8)
    out[...] = states[...].reshape(DEVS * 8, PAIR).astype(BF)


def scan(place, got):
    whole = pl.BlockSpec(memory_space=VMEM)
    return pl.pallas_call(
        scan_kernel,
        in_specs=[pl.BlockSpec(memory_space=pltpu.SMEM), whole],
        out_specs=whole,
        out_shape=jax.ShapeDtypeStruct((DEVS * 8, PAIR), BF),
        scratch_shapes=[VMEM((DEVS, 8, PAIR), F32)] * 3,
        compiler_params=params(24),
        cost_estimate=cost(2 * DEVS * 8 * PAIR, 4 * DEVS * 16 * PAIR),
        name="scan",
    )(place, got)


def near_kernel(lin_scale, place, blocks, q_ref, kv, ptok, wk, wv, cot, run, runt, out, dq_out, own, prev, tag_out):
    tag_out[0] = place[0]
    soft_scale = 1.0 / math.sqrt(DH)
    n_own = jnp.int32(0)
    n_prev = jnp.int32(0)
    for j in range(blocks.shape[1]):
        n_own += (blocks[0, j] == place[0]).astype(jnp.int32)
        n_prev += (blocks[0, j] == place[0] - 1).astype(jnp.int32)
    is_own = iota((1, 2 * SEG), 1) < SEG
    times = jnp.where(is_own, n_own, n_prev)
    bias = jnp.where(times > 0, 0.0, -1e30)
    times = times.astype(F32)
    head_of = iota((SEG, PAIR), 1) // DH
    head_of2 = iota((2 * SEG, PAIR), 1) // DH
    lower = iota((SEG, SEG), 0) >= iota((SEG, SEG), 1)
    zero = jnp.zeros((), BF)
    pk = dot(ptok[...], wk[...], 1, 0).astype(BF)
    pv = dot(ptok[...], wv[...], 1, 0).astype(BF)
    pairs = q_ref.shape[1] // PAIR
    work = []
    for pair in range(pairs):
        at = slice(pair * PAIR, (pair + 1) * PAIR)
        q = q_ref[:, at]
        g = cot[:, at]
        kk = jnp.concatenate([kv[0, :, at], pk[:, at]], axis=0)
        vv = jnp.concatenate([kv[1, :, at], pv[:, at]], axis=0)
        for i in range(2):
            mine = head_of == i
            work.append(
                (
                    dot(jnp.where(mine, q, zero), kk, 1, 1),
                    dot(jnp.where(mine, g, zero), vv, 1, 1),
                )
            )
    mats = []
    for head in range(2 * pairs):
        scores, pgrad = work[head]
        col = runt[0, :, head : head + 1]
        row = run[0, head : head + 1, :]
        dec = jnp.where(lower, jnp.exp(jnp.minimum(col - row, 0.0)), 0.0) * lin_scale
        logits = scores * soft_scale + bias
        peak = jnp.max(logits, axis=1, keepdims=True)
        terms = jnp.exp(logits - peak) * times
        probs = terms * (1.0 / jnp.sum(terms, axis=1, keepdims=True))
        inner = jnp.sum(probs * pgrad, axis=1, keepdims=True)
        dlog = probs * (pgrad - inner) * soft_scale
        a = jnp.concatenate([probs[:, :SEG] + scores[:, :SEG] * dec, probs[:, SEG:]], axis=1)
        b = jnp.concatenate([dlog[:, :SEG] + pgrad[:, :SEG] * dec, dlog[:, SEG:]], axis=1)
        mats.append((a.astype(BF), b.astype(BF)))
    for pair in range(pairs):
        at = slice(pair * PAIR, (pair + 1) * PAIR)
        q = q_ref[:, at]
        g = cot[:, at]
        kk = jnp.concatenate([kv[0, :, at], pk[:, at]], axis=0)
        vv = jnp.concatenate([kv[1, :, at], pv[:, at]], axis=0)
        qt = q.T
        gt = g.T
        res = []
        for i in range(2):
            a, b = mats[2 * pair + i]
            half = slice(i * DH, (i + 1) * DH)
            res.append((dot(a, vv, 1, 0), dot(b, kk, 1, 0), dot(qt[half], b, 1, 0), dot(gt[half], a, 1, 0)))
        out[:, at] = jnp.where(head_of == 0, res[0][0], res[1][0])
        dq_out[:, at] = jnp.where(head_of == 0, res[0][1], res[1][1])
        for part in range(2):
            sums = jnp.concatenate([res[0][2 + part], res[1][2 + part]], axis=0).T
            own[part, :, at] = sums[:SEG]
            prev[part, :, at] = sums[SEG:].astype(BF)


def near(place, blocks, q, kv, prev_tokens, wk, wv, cot, run, runt, lin_scale):
    rows, width = q.shape
    heads = run.shape[1]
    smem = pl.BlockSpec(memory_space=pltpu.SMEM)
    col = pl.BlockSpec((rows, CHUNK), lambda i: (0, i))
    two = pl.BlockSpec((2, rows, CHUNK), lambda i: (0, 0, i))
    weight = pl.BlockSpec((width, CHUNK), lambda i: (0, i))
    return pl.pallas_call(
        functools.partial(near_kernel, lin_scale),
        grid=(width // CHUNK,),
        in_specs=[
            smem,
            smem,
            col,
            two,
            pl.BlockSpec((rows, width), lambda i: (0, 0)),
            weight,
            weight,
            col,
            pl.BlockSpec((1, heads, rows), lambda i: (i, 0, 0)),
            pl.BlockSpec((1, rows, heads), lambda i: (i, 0, 0)),
        ],
        out_specs=[col, col, two, two, smem],
        out_shape=[
            jax.ShapeDtypeStruct((rows, width), F32),
            jax.ShapeDtypeStruct((rows, width), F32),
            jax.ShapeDtypeStruct((2, rows, width), F32),
            jax.ShapeDtypeStruct((2, rows, width), BF),
            jax.ShapeDtypeStruct((1,), jnp.int32),
        ],
        compiler_params=params(58),
        cost_estimate=cost(4000 * 1000 * 1000, 16 * 1000 * 1000, 1000 * 1000),
        name="near",
    )(place, blocks, q, kv, prev_tokens, wk, wv, cot, run, runt)


def join_kernel(lin_scale, near_out, dq_in, own, nxt, q, kv, cot, runt, states, layer, delta):
    head_of = iota((SEG, PAIR), 1) // DH
    diag = iota((PAIR, PAIR), 0) // DH == iota((PAIR, PAIR), 1) // DH
    zero = jnp.zeros((), BF)
    pairs = q.shape[1] // PAIR
    work = []
    for pair in range(pairs):
        at = slice(pair * PAIR, (pair + 1) * PAIR)
        before, after = (
            jnp.where(diag, jnp.concatenate([states[part, pair]] * 2, axis=0), zero)
            for part in range(2)
        )
        work.append(
            (
                dot(q[:, at], before, 1, 0),
                dot(cot[:, at], before, 1, 1),
                dot(kv[1, :, at], after, 1, 1),
                dot(kv[0, :, at], after, 1, 0),
            )
        )
    for pair in range(pairs):
        at = slice(pair * PAIR, (pair + 1) * PAIR)
        run = jnp.where(
            head_of == 0,
            runt[pair // 2, :, 2 * (pair % 2) : 2 * (pair % 2) + 1],
            runt[pair // 2, :, 2 * (pair % 2) + 1 : 2 * (pair % 2) + 2],
        )
        growth = jnp.exp(run) * lin_scale
        fading = jnp.exp(run[SEG - 1 : SEG, :] - run)
        from_q, from_g, from_v, from_k = work[pair]
        layer[:, at] = (near_out[:, at] + growth * from_q).astype(BF)
        dq = dq_in[:, at] + growth * from_g
        dk = own[0, :, at] + fading * from_v + nxt[0, :, at].astype(F32)
        dv = own[1, :, at] + fading * from_k + nxt[1, :, at].astype(F32)
        delta[pair, :, :PAIR] = dq.astype(BF)
        delta[pair, :, PAIR : 2 * PAIR] = dk.astype(BF)
        delta[pair, :, 2 * PAIR :] = dv.astype(BF)


def join(near_out, dq, own, nxt, q, kv, cot, runt, states, lin_scale):
    rows, width = q.shape
    pairs = width // PAIR
    wide = 2 * CHUNK
    col = pl.BlockSpec((rows, wide), lambda i: (0, i))
    two = pl.BlockSpec((2, rows, wide), lambda i: (0, 0, i))
    return pl.pallas_call(
        functools.partial(join_kernel, lin_scale),
        grid=(width // wide,),
        in_specs=[
            col,
            col,
            two,
            two,
            col,
            two,
            col,
            pl.BlockSpec((2, rows, runt.shape[2]), lambda i: (i, 0, 0)),
            pl.BlockSpec((2, wide // PAIR, DH, PAIR), lambda i: (0, i, 0, 0)),
        ],
        out_specs=[col, pl.BlockSpec((wide // PAIR, rows, 3 * PAIR), lambda i: (i, 0, 0))],
        out_shape=[
            jax.ShapeDtypeStruct((rows, width), BF),
            jax.ShapeDtypeStruct((pairs, rows, 3 * PAIR), BF),
        ],
        compiler_params=params(58),
        cost_estimate=cost(8 * rows * PAIR * PAIR * pairs, 24 * rows * width),
        name="join",
    )(near_out, dq, own, nxt, q, kv, cot, runt, states)


def back_kernel(tag, delta, wq, wk, wv, out, tag_out, total):
    step = pl.program_id(0)
    tag_out[0] = tag[0]

    @pl.when(step == 0)
    def _():
        total[...] = jnp.zeros_like(total)

    acc = total[...]
    for part, w in enumerate((wq, wk, wv)):
        for half in range(2):
            acc += dot(
                delta[half, :, part * PAIR : (part + 1) * PAIR],
                w[:, half * PAIR : (half + 1) * PAIR],
                1,
                1,
            )
    total[...] = acc

    @pl.when(step == pl.num_programs(0) - 1)
    def _():
        out[...] = acc.astype(BF)


def back(tag, delta, wq, wk, wv):
    pairs, rows, _ = delta.shape
    width = wq.shape[0]
    smem = pl.BlockSpec(memory_space=pltpu.SMEM)
    weight = pl.BlockSpec((width, 2 * PAIR), lambda i: (0, i))
    return pl.pallas_call(
        back_kernel,
        grid=(pairs // 2,),
        in_specs=[smem, pl.BlockSpec((2, rows, 3 * PAIR), lambda i: (i, 0, 0)), weight, weight, weight],
        out_specs=[
            pl.BlockSpec((rows, width), lambda i: (0, 0)),
            smem,
        ],
        out_shape=[
            jax.ShapeDtypeStruct((rows, width), BF),
            jax.ShapeDtypeStruct((1,), jnp.int32),
        ],
        scratch_shapes=[VMEM((rows, width), F32)],
        compiler_params=params(58),
        cost_estimate=cost(6 * rows * width * width, 6 * width * width + 8 * rows * width),
        name="back",
    )(tag, delta, wq, wk, wv)


def outer_kernel(core, at_x, mine, theirs, delta, out):
    near_x = mine.shape[0]
    left, right = [], []
    for tokt, c in ((mine, core[0]), (theirs, 1 - core[0])):
        for i in range(near_x):
            left.append(tokt[i])
            right.append(delta[c * near_x + lax.rem(at_x[0] + near_x - i, near_x)])
    left = jnp.concatenate(left, axis=1)
    out[...] = dot(left, jnp.concatenate(right, axis=0), 1, 0).astype(BF)


def outer(core, at_x, mine, theirs, delta):
    near_count, rows, cols = delta.shape
    width = mine.shape[1]
    smem = pl.BlockSpec(memory_space=pltpu.SMEM)
    tok = pl.BlockSpec((near_count // 2, width // 2, rows), lambda i: (0, i, 0))
    return pl.pallas_call(
        outer_kernel,
        grid=(2,),
        in_specs=[
            smem,
            smem,
            tok,
            tok,
            pl.BlockSpec((near_count, rows, cols), lambda i: (0, 0, 0)),
        ],
        out_specs=pl.BlockSpec((width // 2, cols), lambda i: (i, 0)),
        out_shape=jax.ShapeDtypeStruct((width, cols), BF),
        compiler_params=params(20),
        cost_estimate=cost(
            2 * near_count * rows * cols * width, 2 * near_count * rows * (width + cols)
        ),
        name="outer",
    )(core, at_x, mine, theirs, delta)


def device(yl, c, x, z, yh):
    return (((yl * 2 + c) * 4 + x) * 4 + z) * 2 + yh


def gather_groups():
    zero = [
        [device(yl, 0, x, z, yh) for yl in range(2) for z in range(4) for yh in range(2)]
        for x in range(4)
    ]
    one = [
        [device(yl, 1, x, z, yh) for x in range(4) for yl in range(2) for yh in range(2)]
        for z in range(4)
    ]
    return zero + one


def ring(array, by):
    route = []
    for yl in range(2):
        for x in range(4):
            for z in range(4):
                for yh in range(2):
                    route.append((device(yl, 0, x, z, yh), device(yl, 0, (x + by) % 4, z, yh)))
                    route.append((device(yl, 1, x, z, yh), device(yl, 1, x, (z + by) % 4, yh)))
    return lax.ppermute(array, AX, route)


def place_kernel(pieces, count, side, at_x, at_z, *refs):
    grads, mark, sems = refs[-5:-2], refs[-2], refs[-1]
    mark[...] = jnp.zeros_like(mark)

    def put(rank):
        copies = []

        def start(src, dst):
            copy = pltpu.make_async_copy(src, dst, sems.at[len(copies)])
            copy.start()
            copies.append(copy)

        for n in range(count):
            source = refs[n]
            rows = source.shape[1]
            by_row = rank[n]
            for place, by in enumerate(pieces):
                x = lax.rem(at_x[0] + by + 4, 4)
                z = lax.rem(at_z[0] + by + 4, 4)
                for part, grad in enumerate(grads):
                    lanes = pl.ds(part * PAIR, PAIR)
                    for i in range(8):
                        if by_row:
                            to = pl.multiple_of(((i % 2) * 4 + z) * rows, rows)
                            at = (pl.ds(to, rows), pl.ds((4 + i // 2) * PAIR, PAIR))
                        else:
                            to = pl.multiple_of(x * PAIR, PAIR)
                            at = (pl.ds(i * rows, rows), pl.ds(to, PAIR))
                        start(source.at[place * 8 + i, :, lanes], grad.at[at])
        for copy in copies:
            copy.wait()

    @pl.when(side[0] == 0)
    def _():
        put((False, True))

    @pl.when(side[0] == 1)
    def _():
        put((True, False))


def place_tiles(where, pieces, sources, grads, width):
    hbm = pl.BlockSpec(memory_space=pl.ANY)
    smem = pl.BlockSpec(memory_space=pltpu.SMEM)
    first = 3 + len(sources)
    return pl.pallas_call(
        functools.partial(place_kernel, pieces, len(sources)),
        in_specs=[smem] * 3 + [hbm] * (len(sources) + len(grads)),
        out_specs=[hbm] * 3 + [pl.BlockSpec(memory_space=VMEM)],
        out_shape=[jax.ShapeDtypeStruct((width, width), BF)] * 3
        + [jax.ShapeDtypeStruct((8, PAIR), F32)],
        scratch_shapes=[pltpu.SemaphoreType.DMA((24 * len(pieces) * len(sources),))],
        input_output_aliases={first + i: i for i in range(len(grads))},
        compiler_params=params(16),
        cost_estimate=cost(0, 4 * sum(a.size for a in sources)),
        name="place",
    )(*where, *sources, *grads)


def halves_kernel(behind, ahead, after, first, second, both):
    del after
    half = first.shape[0]
    first[...] = behind[:half]
    second[...] = ahead[half:]
    both[: 2 * half] = behind[...]
    both[2 * half :] = ahead[...]


def halves(behind, ahead, after):
    pairs, *rest = behind.shape
    whole = pl.BlockSpec(memory_space=VMEM)
    return pl.pallas_call(
        halves_kernel,
        in_specs=[whole, whole, pl.BlockSpec(memory_space=pl.ANY)],
        out_specs=[whole] * 3,
        out_shape=[jax.ShapeDtypeStruct((n, *rest), BF) for n in (pairs // 2, pairs // 2, 2 * pairs)],
        compiler_params=params(16),
        cost_estimate=cost(0, 12 * behind.size),
        name="halves",
    )(behind, ahead, after)


def gather_tiles(piece, where, width):
    swap = [(0, 1), (1, 0)]

    def swapped(array):
        return lax.ppermute(array, "c", swap)

    rows, cols = piece.shape
    here = lax.all_to_all(
        jnp.broadcast_to(piece[None], (16, rows, cols)), AX, 0, 0, axis_index_groups=gather_groups()
    ).reshape(8, 2 * rows, cols)
    behind = ring(here, 1)
    ahead = ring(here, -1)
    *grads, mark = place_tiles(where, (0,), (here, swapped(here)), (), width)
    half_a, half_b, both = halves(behind, ahead, mark)
    far_a = ring(half_a, 1)
    far_b = ring(half_b, -1)
    *grads, mark = place_tiles(where, (-1, 1), (both, swapped(both)), grads, width)
    far = stack([far_a, far_b], mark).reshape(here.shape)
    far_c = swapped(far)
    *grads, _ = place_tiles(where, (2,), (far,), grads, width)
    core, *rest = where
    *grads, _ = place_tiles((1 - core, *rest), (2,), (far_c,), grads, width)
    return grads


def shards(tokens, wq, wk, wv, log_decay, neighbour_blocks, cot):
    rows, width = tokens.shape
    lin_scale = 1.0 / (DH * math.sqrt(rows))
    place = lax.axis_index(AX).astype(jnp.int32).reshape(1)
    core = lax.axis_index("c").astype(jnp.int32).reshape(1)

    at_x = lax.axis_index("x").astype(jnp.int32).reshape(1)
    swap = [(0, 1), (1, 0)]
    q, kv, run, runt, msg, own_tokens = project(tokens, wq, wk, wv, log_decay, cot, lin_scale)
    prev_tokens = lax.ppermute(own_tokens, AX, [(i, i + 1) for i in range(DEVS - 1)])
    got = lax.all_to_all(msg.reshape(DEVS, 16, PAIR), AX, 0, 0)
    near_out, dq, own, prev, place = near(
        place, neighbour_blocks, q, kv, prev_tokens, wk, wv, cot, run, runt, lin_scale
    )
    nxt = lax.ppermute(prev, AX, [(i + 1, i) for i in range(DEVS - 1)])
    states = scan(place, got)
    tokt, _ = flip(place, own_tokens)
    around = [lax.ppermute(tokt, "x", [(i, (i + d) % 4) for i in range(4)]) for d in (1, 2, 3)]
    states = lax.all_to_all(states.reshape(DEVS, 8, PAIR), AX, 0, 0)
    states = states.reshape(2, width // PAIR, DH, PAIR)
    layer, delta = join(near_out, dq, own, nxt, q, kv, cot, runt, states, lin_scale)

    delta8 = lax.all_to_all(delta, NEAR8, 0, 0)
    mine = stack([tokt, *around], delta)
    theirs = lax.ppermute(mine, "c", swap)
    tokens_grad, later_core = back(core, delta, wq, wk, wv)
    partial = outer(later_core, at_x, mine, theirs, delta8)
    parts = lax.all_to_all(partial.reshape(16, width // 16, 3 * PAIR), FAR16, 0, 0)
    grad_norm = 1.0 / math.sqrt(rows * DEVS)
    piece = (jnp.sum(parts.astype(F32), axis=0) * grad_norm).astype(BF)
    at_z = lax.axis_index("z").astype(jnp.int32).reshape(1)
    gq, gk, gv = gather_tiles(piece, (core, at_x, at_z), width)
    return layer, tokens_grad, gq, gk, gv


def solution(mesh):
    chips = Mesh(mesh.devices.reshape(2, 2, 4, 4, 2), AX)
    tok = P(AX, None)
    return jax.shard_map(
        shards,
        mesh=chips,
        in_specs=(tok, P(), P(), P(), P(None, AX), tok, tok),
        out_specs=(tok, tok, P(), P(), P()),
        check_vma=False,
    )
```

```python
import functools
import math

import jax
import jax.numpy as jnp
from jax import lax
from jax.experimental import pallas as pl
from jax.experimental.pallas import tpu as pltpu
from jax.sharding import Mesh
from jax.sharding import PartitionSpec as P

BF = jnp.bfloat16
F32 = jnp.float32
AX = ("yl", "c", "x", "z", "yh")
NEAR8 = ("c", "x")
FAR16 = ("yl", "z", "yh")
PLANE = ("x", "yl", "z", "yh")
SEG = 128
PAIR = 128
DH = 64
DEVS = 128
VMEM = pltpu.VMEM
HIGH = lax.Precision.HIGHEST


def dot(a, b, ca, cb, precision=None):
    return lax.dot_general(
        a, b, (((ca,), (cb,)), ((), ())), precision=precision, preferred_element_type=F32
    )


def iota(shape, axis):
    return lax.broadcasted_iota(jnp.int32, shape, axis)


def params(mib):
    return pltpu.CompilerParams(vmem_limit_bytes=mib << 20)


def cost(flops, moved, trans=0):
    return pl.CostEstimate(flops=flops, bytes_accessed=moved, transcendentals=trans)


CHUNK = 256
WIDE = 512


def pair_lanes(columns, pair):
    shape = (columns.shape[0], PAIR)
    return jnp.where(
        iota(shape, 1) < DH,
        columns[:, 2 * pair : 2 * pair + 1],
        columns[:, 2 * pair + 1 : 2 * pair + 2],
    )


def project_kernel(lin_scale, tok, wq, wk, wv, decay, cot, q_out, kv_out, run_out, runt_out, msg, tok_out, held, sems):
    width = tok.shape[1]
    wide = held.shape[3]
    copies = []
    for step in range(width // wide):
        for part, w in enumerate((wq, wk, wv)):
            copy = pltpu.make_async_copy(
                w.at[:, pl.ds(step * wide, wide)], held.at[part, step], sems.at[part, step]
            )
            copy.start()
            copies.append(copy)
    x = tok[...]
    tok_out[...] = x
    ld = decay[...]
    lower = (iota((SEG, SEG), 0) >= iota((SEG, SEG), 1)).astype(F32)
    runt = dot(lower, ld, 1, 1, HIGH)
    run = dot(ld, lower, 1, 1, HIGH)
    group = ld.shape[0] // run_out.shape[0]
    for step in range(run_out.shape[0]):
        runt_out[step] = runt[:, step * group : (step + 1) * group]
        run_out[step] = run[step * group : (step + 1) * group, :]
    rows = iota((8, PAIR), 0)
    first = iota((DH, PAIR), 1) < DH
    for step in range(width // wide):
        for part in range(3):
            copies[step * 3 + part].wait()
        at = slice(step * wide, (step + 1) * wide)
        q = dot(x, held[0, step], 1, 0).astype(BF)
        k = dot(x, held[1, step], 1, 0).astype(BF)
        v = dot(x, held[2, step], 1, 0).astype(BF)
        q_out[:, at] = q
        kv_out[0, :, at] = k
        kv_out[1, :, at] = v
        here = []
        for part in range(wide // PAIR):
            cols = slice(part * PAIR, (part + 1) * PAIR)
            pair = step * (wide // PAIR) + part
            lanes = pair_lanes(runt, pair)
            total = lanes[SEG - 1 : SEG, :]
            g = cot[:, pair * PAIR : (pair + 1) * PAIR].astype(F32)
            weighted = (v[:, cols].astype(F32) * jnp.exp(total - lanes)).astype(BF)
            scaled = (g * jnp.exp(lanes)).astype(BF)
            states = (
                dot(k[:, cols], weighted, 0, 0),
                dot(q[:, cols], scaled, 0, 0) * lin_scale,
            )
            here.append((pair, total, states))
        for pair, total, states in here:
            high = total.astype(BF).astype(F32)
            mid = (total - high).astype(BF).astype(F32)
            low = total - high - mid
            tail = jnp.where(
                rows == 0, high, jnp.where(rows == 1, mid, jnp.where(rows == 2, low, 0.0))
            )
            tail = jnp.broadcast_to(tail[None], (8, 8, PAIR))
            for part, full in enumerate(states):
                own = jnp.where(first, full[:DH], full[DH:]).reshape(8, 8, PAIR)
                sent = jnp.concatenate([own, tail], axis=1).reshape(PAIR, PAIR)
                msg[part, pair * PAIR : (pair + 1) * PAIR, :] = sent.astype(BF)


def project(tokens, wq, wk, wv, log_decay, cot, lin_scale):
    rows, width = tokens.shape
    heads = log_decay.shape[0]
    chunks = width // CHUNK
    wide = WIDE
    vmem = pl.BlockSpec(memory_space=VMEM)
    hbm = pl.BlockSpec(memory_space=pltpu.HBM)
    return pl.pallas_call(
        functools.partial(project_kernel, lin_scale),
        in_specs=[vmem, hbm, hbm, hbm, vmem, vmem],
        out_specs=[vmem] * 6,
        out_shape=[
            jax.ShapeDtypeStruct((rows, width), BF),
            jax.ShapeDtypeStruct((2, rows, width), BF),
            jax.ShapeDtypeStruct((chunks, heads // chunks, rows), F32),
            jax.ShapeDtypeStruct((chunks, rows, heads // chunks), F32),
            jax.ShapeDtypeStruct((2, width, PAIR), BF),
            jax.ShapeDtypeStruct((rows, width), BF),
        ],
        scratch_shapes=[
            VMEM((3, width // wide, width, wide), BF),
            pltpu.SemaphoreType.DMA((3, width // wide)),
        ],
        compiler_params=params(58),
        cost_estimate=cost(6 * rows * width * width, 6 * width * width + 12 * rows * width),
        name="project",
    )(tokens, wq, wk, wv, log_decay, cot)


def flip_kernel(tag, tok, out, tag_out):
    tag_out[0] = tag[0]
    out[...] = tok[...].T


def flip(tag, tokens):
    rows, width = tokens.shape
    whole = pl.BlockSpec(memory_space=VMEM)
    smem = pl.BlockSpec(memory_space=pltpu.SMEM)
    return pl.pallas_call(
        flip_kernel,
        in_specs=[smem, whole],
        out_specs=[whole, smem],
        out_shape=[
            jax.ShapeDtypeStruct((width, rows), BF),
            jax.ShapeDtypeStruct((1,), jnp.int32),
        ],
        compiler_params=params(16),
        cost_estimate=cost(0, 4 * rows * width),
        name="flip",
    )(tag, tokens)


def stack_kernel(*refs):
    out = refs[-1]
    for i in range(out.shape[0]):
        out[i] = refs[i][...]


def stack(parts, after):
    shape = parts[0].shape
    whole = pl.BlockSpec(memory_space=VMEM)
    return pl.pallas_call(
        stack_kernel,
        in_specs=[whole] * len(parts) + [pl.BlockSpec(memory_space=pl.ANY)],
        out_specs=whole,
        out_shape=jax.ShapeDtypeStruct((len(parts), *shape), BF),
        compiler_params=params(16),
        cost_estimate=cost(0, 4 * len(parts) * math.prod(shape)),
        name="stack",
    )(*parts, after)


def scan_kernel(place, got, out, xs, decays, states):
    both = got[...].astype(F32)
    xs[...] = both[:, :8, :]
    total = both[:, 8:9, :] + both[:, 9:10, :] + both[:, 10:11, :]
    decays[...] = jnp.broadcast_to(jnp.exp(total), decays.shape)
    backward = place[0] >= DEVS // 2

    def one(i, state):
        at = jnp.where(backward, DEVS - 1 - i, i)
        states[at] = state
        return decays[at] * state + xs[at]

    lax.fori_loop(0, DEVS, one, jnp.zeros((8, PAIR), F32), unroll=8)
    out[...] = states[...].reshape(DEVS * 8, PAIR).astype(BF)


def scan(place, got):
    whole = pl.BlockSpec(memory_space=VMEM)
    return pl.pallas_call(
        scan_kernel,
        in_specs=[pl.BlockSpec(memory_space=pltpu.SMEM), whole],
        out_specs=whole,
        out_shape=jax.ShapeDtypeStruct((DEVS * 8, PAIR), BF),
        scratch_shapes=[VMEM((DEVS, 8, PAIR), F32)] * 3,
        compiler_params=params(24),
        cost_estimate=cost(2 * DEVS * 8 * PAIR, 4 * DEVS * 16 * PAIR),
        name="scan",
    )(place, got)


def near_kernel(lin_scale, place, blocks, q_ref, kv, ptok, wk, wv, cot, run, runt, out, dq_out, own, prev, tag_out):
    tag_out[0] = place[0]
    soft_scale = 1.0 / math.sqrt(DH)
    n_own = jnp.int32(0)
    n_prev = jnp.int32(0)
    for j in range(blocks.shape[1]):
        n_own += (blocks[0, j] == place[0]).astype(jnp.int32)
        n_prev += (blocks[0, j] == place[0] - 1).astype(jnp.int32)
    is_own = iota((1, 2 * SEG), 1) < SEG
    times = jnp.where(is_own, n_own, n_prev)
    bias = jnp.where(times > 0, 0.0, -1e30)
    times = times.astype(F32)
    head_of = iota((SEG, PAIR), 1) // DH
    head_of2 = iota((2 * SEG, PAIR), 1) // DH
    lower = iota((SEG, SEG), 0) >= iota((SEG, SEG), 1)
    zero = jnp.zeros((), BF)
    pk = dot(ptok[...], wk[...], 1, 0).astype(BF)
    pv = dot(ptok[...], wv[...], 1, 0).astype(BF)
    pairs = q_ref.shape[1] // PAIR
    work = []
    for pair in range(pairs):
        at = slice(pair * PAIR, (pair + 1) * PAIR)
        q = q_ref[:, at]
        g = cot[:, at]
        kk = jnp.concatenate([kv[0, :, at], pk[:, at]], axis=0)
        vv = jnp.concatenate([kv[1, :, at], pv[:, at]], axis=0)
        for i in range(2):
            mine = head_of == i
            work.append(
                (
                    dot(jnp.where(mine, q, zero), kk, 1, 1),
                    dot(jnp.where(mine, g, zero), vv, 1, 1),
                )
            )
    mats = []
    for head in range(2 * pairs):
        scores, pgrad = work[head]
        col = runt[0, :, head : head + 1]
        row = run[0, head : head + 1, :]
        dec = jnp.where(lower, jnp.exp(jnp.minimum(col - row, 0.0)), 0.0) * lin_scale
        logits = scores * soft_scale + bias
        peak = jnp.max(logits, axis=1, keepdims=True)
        terms = jnp.exp(logits - peak) * times
        probs = terms * (1.0 / jnp.sum(terms, axis=1, keepdims=True))
        inner = jnp.sum(probs * pgrad, axis=1, keepdims=True)
        dlog = probs * (pgrad - inner) * soft_scale
        a = jnp.concatenate([probs[:, :SEG] + scores[:, :SEG] * dec, probs[:, SEG:]], axis=1)
        b = jnp.concatenate([dlog[:, :SEG] + pgrad[:, :SEG] * dec, dlog[:, SEG:]], axis=1)
        mats.append((a.astype(BF), b.astype(BF)))
    for pair in range(pairs):
        at = slice(pair * PAIR, (pair + 1) * PAIR)
        q = q_ref[:, at]
        g = cot[:, at]
        kk = jnp.concatenate([kv[0, :, at], pk[:, at]], axis=0)
        vv = jnp.concatenate([kv[1, :, at], pv[:, at]], axis=0)
        qt = q.T
        gt = g.T
        res = []
        for i in range(2):
            a, b = mats[2 * pair + i]
            half = slice(i * DH, (i + 1) * DH)
            res.append((dot(a, vv, 1, 0), dot(b, kk, 1, 0), dot(qt[half], b, 1, 0), dot(gt[half], a, 1, 0)))
        out[:, at] = jnp.where(head_of == 0, res[0][0], res[1][0])
        dq_out[:, at] = jnp.where(head_of == 0, res[0][1], res[1][1])
        for part in range(2):
            sums = jnp.concatenate([res[0][2 + part], res[1][2 + part]], axis=0).T
            own[part, :, at] = sums[:SEG]
            prev[part, :, at] = sums[SEG:].astype(BF)


def near(place, blocks, q, kv, prev_tokens, wk, wv, cot, run, runt, lin_scale):
    rows, width = q.shape
    heads = run.shape[1]
    smem = pl.BlockSpec(memory_space=pltpu.SMEM)
    col = pl.BlockSpec((rows, CHUNK), lambda i: (0, i))
    two = pl.BlockSpec((2, rows, CHUNK), lambda i: (0, 0, i))
    weight = pl.BlockSpec((width, CHUNK), lambda i: (0, i))
    return pl.pallas_call(
        functools.partial(near_kernel, lin_scale),
        grid=(width // CHUNK,),
        in_specs=[
            smem,
            smem,
            col,
            two,
            pl.BlockSpec((rows, width), lambda i: (0, 0)),
            weight,
            weight,
            col,
            pl.BlockSpec((1, heads, rows), lambda i: (i, 0, 0)),
            pl.BlockSpec((1, rows, heads), lambda i: (i, 0, 0)),
        ],
        out_specs=[col, col, two, two, smem],
        out_shape=[
            jax.ShapeDtypeStruct((rows, width), F32),
            jax.ShapeDtypeStruct((rows, width), F32),
            jax.ShapeDtypeStruct((2, rows, width), F32),
            jax.ShapeDtypeStruct((2, rows, width), BF),
            jax.ShapeDtypeStruct((1,), jnp.int32),
        ],
        compiler_params=params(58),
        cost_estimate=cost(4000 * 1000 * 1000, 16 * 1000 * 1000, 1000 * 1000),
        name="near",
    )(place, blocks, q, kv, prev_tokens, wk, wv, cot, run, runt)


def join_kernel(lin_scale, near_out, dq_in, own, nxt, q, kv, cot, runt, states, layer, delta):
    head_of = iota((SEG, PAIR), 1) // DH
    diag = iota((PAIR, PAIR), 0) // DH == iota((PAIR, PAIR), 1) // DH
    zero = jnp.zeros((), BF)
    pairs = q.shape[1] // PAIR
    work = []
    for pair in range(pairs):
        at = slice(pair * PAIR, (pair + 1) * PAIR)
        before, after = (
            jnp.where(diag, jnp.concatenate([states[part, pair]] * 2, axis=0), zero)
            for part in range(2)
        )
        work.append(
            (
                dot(q[:, at], before, 1, 0),
                dot(cot[:, at], before, 1, 1),
                dot(kv[1, :, at], after, 1, 1),
                dot(kv[0, :, at], after, 1, 0),
            )
        )
    for pair in range(pairs):
        at = slice(pair * PAIR, (pair + 1) * PAIR)
        run = jnp.where(
            head_of == 0,
            runt[pair // 2, :, 2 * (pair % 2) : 2 * (pair % 2) + 1],
            runt[pair // 2, :, 2 * (pair % 2) + 1 : 2 * (pair % 2) + 2],
        )
        growth = jnp.exp(run) * lin_scale
        fading = jnp.exp(run[SEG - 1 : SEG, :] - run)
        from_q, from_g, from_v, from_k = work[pair]
        layer[:, at] = (near_out[:, at] + growth * from_q).astype(BF)
        dq = dq_in[:, at] + growth * from_g
        dk = own[0, :, at] + fading * from_v + nxt[0, :, at].astype(F32)
        dv = own[1, :, at] + fading * from_k + nxt[1, :, at].astype(F32)
        delta[pair, :, :PAIR] = dq.astype(BF)
        delta[pair, :, PAIR : 2 * PAIR] = dk.astype(BF)
        delta[pair, :, 2 * PAIR :] = dv.astype(BF)


def join(near_out, dq, own, nxt, q, kv, cot, runt, states, lin_scale):
    rows, width = q.shape
    pairs = width // PAIR
    wide = 2 * CHUNK
    col = pl.BlockSpec((rows, wide), lambda i: (0, i))
    two = pl.BlockSpec((2, rows, wide), lambda i: (0, 0, i))
    return pl.pallas_call(
        functools.partial(join_kernel, lin_scale),
        grid=(width // wide,),
        in_specs=[
            col,
            col,
            two,
            two,
            col,
            two,
            col,
            pl.BlockSpec((2, rows, runt.shape[2]), lambda i: (i, 0, 0)),
            pl.BlockSpec((2, wide // PAIR, DH, PAIR), lambda i: (0, i, 0, 0)),
        ],
        out_specs=[col, pl.BlockSpec((wide // PAIR, rows, 3 * PAIR), lambda i: (i, 0, 0))],
        out_shape=[
            jax.ShapeDtypeStruct((rows, width), BF),
            jax.ShapeDtypeStruct((pairs, rows, 3 * PAIR), BF),
        ],
        compiler_params=params(58),
        cost_estimate=cost(8 * rows * PAIR * PAIR * pairs, 24 * rows * width),
        name="join",
    )(near_out, dq, own, nxt, q, kv, cot, runt, states)


def back_kernel(tag, delta, wq, wk, wv, out, tag_out, total):
    step = pl.program_id(0)
    tag_out[0] = tag[0]

    @pl.when(step == 0)
    def _():
        total[...] = jnp.zeros_like(total)

    acc = total[...]
    for part, w in enumerate((wq, wk, wv)):
        for half in range(2):
            acc += dot(
                delta[half, :, part * PAIR : (part + 1) * PAIR],
                w[:, half * PAIR : (half + 1) * PAIR],
                1,
                1,
            )
    total[...] = acc

    @pl.when(step == pl.num_programs(0) - 1)
    def _():
        out[...] = acc.astype(BF)


def back(tag, delta, wq, wk, wv):
    pairs, rows, _ = delta.shape
    width = wq.shape[0]
    smem = pl.BlockSpec(memory_space=pltpu.SMEM)
    weight = pl.BlockSpec((width, 2 * PAIR), lambda i: (0, i))
    return pl.pallas_call(
        back_kernel,
        grid=(pairs // 2,),
        in_specs=[smem, pl.BlockSpec((2, rows, 3 * PAIR), lambda i: (i, 0, 0)), weight, weight, weight],
        out_specs=[
            pl.BlockSpec((rows, width), lambda i: (0, 0)),
            smem,
        ],
        out_shape=[
            jax.ShapeDtypeStruct((rows, width), BF),
            jax.ShapeDtypeStruct((1,), jnp.int32),
        ],
        scratch_shapes=[VMEM((rows, width), F32)],
        compiler_params=params(58),
        cost_estimate=cost(6 * rows * width * width, 6 * width * width + 8 * rows * width),
        name="back",
    )(tag, delta, wq, wk, wv)


def outer_kernel(core, at_x, mine, theirs, delta, out):
    near_x = mine.shape[0]
    left, right = [], []
    for tokt, c in ((mine, core[0]), (theirs, 1 - core[0])):
        for i in range(near_x):
            left.append(tokt[i])
            right.append(delta[c * near_x + lax.rem(at_x[0] + near_x - i, near_x)])
    left = jnp.concatenate(left, axis=1)
    out[...] = dot(left, jnp.concatenate(right, axis=0), 1, 0).astype(BF)


def outer(core, at_x, mine, theirs, delta):
    near_count, rows, cols = delta.shape
    width = mine.shape[1]
    smem = pl.BlockSpec(memory_space=pltpu.SMEM)
    tok = pl.BlockSpec((near_count // 2, width // 2, rows), lambda i: (0, i, 0))
    return pl.pallas_call(
        outer_kernel,
        grid=(2,),
        in_specs=[
            smem,
            smem,
            tok,
            tok,
            pl.BlockSpec((near_count, rows, cols), lambda i: (0, 0, 0)),
        ],
        out_specs=pl.BlockSpec((width // 2, cols), lambda i: (i, 0)),
        out_shape=jax.ShapeDtypeStruct((width, cols), BF),
        compiler_params=params(20),
        cost_estimate=cost(
            2 * near_count * rows * cols * width, 2 * near_count * rows * (width + cols)
        ),
        name="outer",
    )(core, at_x, mine, theirs, delta)


def device(yl, c, x, z, yh):
    return (((yl * 2 + c) * 4 + x) * 4 + z) * 2 + yh


def gather_groups():
    zero = [
        [device(yl, 0, x, z, yh) for yl in range(2) for z in range(4) for yh in range(2)]
        for x in range(4)
    ]
    one = [
        [device(yl, 1, x, z, yh) for x in range(4) for yl in range(2) for yh in range(2)]
        for z in range(4)
    ]
    return zero + one


def ring(array, by):
    route = []
    for yl in range(2):
        for x in range(4):
            for z in range(4):
                for yh in range(2):
                    route.append((device(yl, 0, x, z, yh), device(yl, 0, (x + by) % 4, z, yh)))
                    route.append((device(yl, 1, x, z, yh), device(yl, 1, x, (z + by) % 4, yh)))
    return lax.ppermute(array, AX, route)


def place_kernel(pieces, count, side, at_x, at_z, *refs):
    grads, mark, sems = refs[-5:-2], refs[-2], refs[-1]
    mark[...] = jnp.zeros_like(mark)

    def put(rank):
        copies = []

        def start(src, dst):
            copy = pltpu.make_async_copy(src, dst, sems.at[len(copies)])
            copy.start()
            copies.append(copy)

        for n in range(count):
            source = refs[n]
            rows = source.shape[1]
            by_row = rank[n]
            for place, by in enumerate(pieces):
                x = lax.rem(at_x[0] + by + 4, 4)
                z = lax.rem(at_z[0] + by + 4, 4)
                for part, grad in enumerate(grads):
                    lanes = pl.ds(part * PAIR, PAIR)
                    for i in range(8):
                        if by_row:
                            to = pl.multiple_of(((i % 2) * 4 + z) * rows, rows)
                            at = (pl.ds(to, rows), pl.ds((4 + i // 2) * PAIR, PAIR))
                        else:
                            to = pl.multiple_of(x * PAIR, PAIR)
                            at = (pl.ds(i * rows, rows), pl.ds(to, PAIR))
                        start(source.at[place * 8 + i, :, lanes], grad.at[at])
        for copy in copies:
            copy.wait()

    @pl.when(side[0] == 0)
    def _():
        put((False, True))

    @pl.when(side[0] == 1)
    def _():
        put((True, False))


def place_tiles(where, pieces, sources, grads, width):
    hbm = pl.BlockSpec(memory_space=pl.ANY)
    smem = pl.BlockSpec(memory_space=pltpu.SMEM)
    first = 3 + len(sources)
    return pl.pallas_call(
        functools.partial(place_kernel, pieces, len(sources)),
        in_specs=[smem] * 3 + [hbm] * (len(sources) + len(grads)),
        out_specs=[hbm] * 3 + [pl.BlockSpec(memory_space=VMEM)],
        out_shape=[jax.ShapeDtypeStruct((width, width), BF)] * 3
        + [jax.ShapeDtypeStruct((8, PAIR), F32)],
        scratch_shapes=[pltpu.SemaphoreType.DMA((24 * len(pieces) * len(sources),))],
        input_output_aliases={first + i: i for i in range(len(grads))},
        compiler_params=params(16),
        cost_estimate=cost(0, 4 * sum(a.size for a in sources)),
        name="place",
    )(*where, *sources, *grads)


def halves_kernel(behind, ahead, after, first, second, both):
    del after
    half = first.shape[0]
    first[...] = behind[:half]
    second[...] = ahead[half:]
    both[: 2 * half] = behind[...]
    both[2 * half :] = ahead[...]


def halves(behind, ahead, after):
    pairs, *rest = behind.shape
    whole = pl.BlockSpec(memory_space=VMEM)
    return pl.pallas_call(
        halves_kernel,
        in_specs=[whole, whole, pl.BlockSpec(memory_space=pl.ANY)],
        out_specs=[whole] * 3,
        out_shape=[jax.ShapeDtypeStruct((n, *rest), BF) for n in (pairs // 2, pairs // 2, 2 * pairs)],
        compiler_params=params(16),
        cost_estimate=cost(0, 12 * behind.size),
        name="halves",
    )(behind, ahead, after)


def gather_tiles(piece, where, width):
    swap = [(0, 1), (1, 0)]

    def swapped(array):
        return lax.ppermute(array, "c", swap)

    rows, cols = piece.shape
    here = lax.all_to_all(
        jnp.broadcast_to(piece[None], (16, rows, cols)), AX, 0, 0, axis_index_groups=gather_groups()
    ).reshape(8, 2 * rows, cols)
    behind = ring(here, 1)
    ahead = ring(here, -1)
    *grads, mark = place_tiles(where, (0,), (here, swapped(here)), (), width)
    half_a, half_b, both = halves(behind, ahead, mark)
    far_a = ring(half_a, 1)
    far_b = ring(half_b, -1)
    *grads, mark = place_tiles(where, (-1, 1), (both, swapped(both)), grads, width)
    far = stack([far_a, far_b], mark).reshape(here.shape)
    far_c = swapped(far)
    *grads, _ = place_tiles(where, (2,), (far,), grads, width)
    core, *rest = where
    *grads, _ = place_tiles((1 - core, *rest), (2,), (far_c,), grads, width)
    return grads


def shards(tokens, wq, wk, wv, log_decay, neighbour_blocks, cot):
    rows, width = tokens.shape
    lin_scale = 1.0 / (DH * math.sqrt(rows))
    place = lax.axis_index(AX).astype(jnp.int32).reshape(1)
    core = lax.axis_index("c").astype(jnp.int32).reshape(1)

    at_x = lax.axis_index("x").astype(jnp.int32).reshape(1)
    swap = [(0, 1), (1, 0)]
    q, kv, run, runt, msg, own_tokens = project(tokens, wq, wk, wv, log_decay, cot, lin_scale)
    prev_tokens = lax.ppermute(own_tokens, AX, [(i, i + 1) for i in range(DEVS - 1)])
    got = lax.all_to_all(msg.reshape(DEVS, 16, PAIR), AX, 0, 0)
    near_out, dq, own, prev, place = near(
        place, neighbour_blocks, q, kv, prev_tokens, wk, wv, cot, run, runt, lin_scale
    )
    nxt = lax.ppermute(prev, AX, [(i + 1, i) for i in range(DEVS - 1)])
    tokt, place = flip(place, own_tokens)
    around = [lax.ppermute(tokt, "x", [(i, (i + d) % 4) for i in range(4)]) for d in (1, 2, 3)]
    states = scan(place, got)
    states = lax.all_to_all(states.reshape(DEVS, 8, PAIR), AX, 0, 0)
    states = states.reshape(2, width // PAIR, DH, PAIR)
    layer, delta = join(near_out, dq, own, nxt, q, kv, cot, runt, states, lin_scale)

    delta8 = lax.all_to_all(delta, NEAR8, 0, 0)
    mine = stack([tokt, *around], delta)
    theirs = lax.ppermute(mine, "c", swap)
    tokens_grad, later_core = back(core, delta, wq, wk, wv)
    partial = outer(later_core, at_x, mine, theirs, delta8)
    parts = lax.all_to_all(partial.reshape(16, width // 16, 3 * PAIR), FAR16, 0, 0)
    grad_norm = 1.0 / math.sqrt(rows * DEVS)
    piece = (jnp.sum(parts.astype(F32), axis=0) * grad_norm).astype(BF)
    at_z = lax.axis_index("z").astype(jnp.int32).reshape(1)
    gq, gk, gv = gather_tiles(piece, (core, at_x, at_z), width)
    return layer, tokens_grad, gq, gk, gv


def solution(mesh):
    chips = Mesh(mesh.devices.reshape(2, 2, 4, 4, 2), AX)
    tok = P(AX, None)
    return jax.shard_map(
        shards,
        mesh=chips,
        in_specs=(tok, P(), P(), P(), P(None, AX), tok, tok),
        out_specs=(tok, tok, P(), P(), P()),
        check_vma=False,
    )
```

```python
import functools
import math

import jax
import jax.numpy as jnp
from jax import lax
from jax.experimental import pallas as pl
from jax.experimental.pallas import tpu as pltpu
from jax.sharding import Mesh
from jax.sharding import PartitionSpec as P

BF = jnp.bfloat16
F32 = jnp.float32
AX = ("yl", "c", "x", "z", "yh")
NEAR8 = ("c", "x")
FAR16 = ("yl", "z", "yh")
PLANE = ("x", "yl", "z", "yh")
SEG = 128
PAIR = 128
DH = 64
DEVS = 128
BACK = (0, 2, 1, 3)
VMEM = pltpu.VMEM
HIGH = lax.Precision.HIGHEST


def dot(a, b, ca, cb, precision=None):
    return lax.dot_general(
        a, b, (((ca,), (cb,)), ((), ())), precision=precision, preferred_element_type=F32
    )


def iota(shape, axis):
    return lax.broadcasted_iota(jnp.int32, shape, axis)


def params(mib):
    return pltpu.CompilerParams(vmem_limit_bytes=mib << 20)


def cost(flops, moved, trans=0):
    return pl.CostEstimate(flops=flops, bytes_accessed=moved, transcendentals=trans)


CHUNK = 256
WIDE = 512


def pair_lanes(columns, pair):
    shape = (columns.shape[0], PAIR)
    return jnp.where(
        iota(shape, 1) < DH,
        columns[:, 2 * pair : 2 * pair + 1],
        columns[:, 2 * pair + 1 : 2 * pair + 2],
    )


def project_kernel(lin_scale, tok, wq, wk, wv, decay, cot, q_out, kv_out, run_out, runt_out, msg, tok_out, held, sems):
    width = tok.shape[1]
    wide = held.shape[3]
    copies = []
    for step in range(width // wide):
        for part, w in enumerate((wq, wk, wv)):
            copy = pltpu.make_async_copy(
                w.at[:, pl.ds(step * wide, wide)], held.at[part, step], sems.at[part, step]
            )
            copy.start()
            copies.append(copy)
    x = tok[...]
    tok_out[...] = x
    ld = decay[...]
    lower = (iota((SEG, SEG), 0) >= iota((SEG, SEG), 1)).astype(F32)
    runt = dot(lower, ld, 1, 1, HIGH)
    run = dot(ld, lower, 1, 1, HIGH)
    group = ld.shape[0] // run_out.shape[0]
    for step in range(run_out.shape[0]):
        runt_out[step] = runt[:, step * group : (step + 1) * group]
        run_out[step] = run[step * group : (step + 1) * group, :]
    rows = iota((8, PAIR), 0)
    first = iota((DH, PAIR), 1) < DH
    for step in range(width // wide):
        for part in range(3):
            copies[step * 3 + part].wait()
        at = slice(step * wide, (step + 1) * wide)
        q = dot(x, held[0, step], 1, 0).astype(BF)
        k = dot(x, held[1, step], 1, 0).astype(BF)
        v = dot(x, held[2, step], 1, 0).astype(BF)
        q_out[:, at] = q
        kv_out[0, :, at] = k
        kv_out[1, :, at] = v
        here = []
        for part in range(wide // PAIR):
            cols = slice(part * PAIR, (part + 1) * PAIR)
            pair = step * (wide // PAIR) + part
            lanes = pair_lanes(runt, pair)
            total = lanes[SEG - 1 : SEG, :]
            g = cot[:, pair * PAIR : (pair + 1) * PAIR].astype(F32)
            weighted = (v[:, cols].astype(F32) * jnp.exp(total - lanes)).astype(BF)
            scaled = (g * jnp.exp(lanes)).astype(BF)
            states = (
                dot(k[:, cols], weighted, 0, 0),
                dot(q[:, cols], scaled, 0, 0) * lin_scale,
            )
            here.append((pair, total, states))
        for pair, total, states in here:
            high = total.astype(BF).astype(F32)
            mid = (total - high).astype(BF).astype(F32)
            low = total - high - mid
            tail = jnp.where(
                rows == 0, high, jnp.where(rows == 1, mid, jnp.where(rows == 2, low, 0.0))
            )
            tail = jnp.broadcast_to(tail[None], (8, 8, PAIR))
            for part, full in enumerate(states):
                own = jnp.where(first, full[:DH], full[DH:]).reshape(8, 8, PAIR)
                sent = jnp.concatenate([own, tail], axis=1).reshape(PAIR, PAIR)
                msg[part, pair * PAIR : (pair + 1) * PAIR, :] = sent.astype(BF)


def project(tokens, wq, wk, wv, log_decay, cot, lin_scale):
    rows, width = tokens.shape
    heads = log_decay.shape[0]
    chunks = width // CHUNK
    wide = WIDE
    vmem = pl.BlockSpec(memory_space=VMEM)
    hbm = pl.BlockSpec(memory_space=pltpu.HBM)
    return pl.pallas_call(
        functools.partial(project_kernel, lin_scale),
        in_specs=[vmem, hbm, hbm, hbm, vmem, vmem],
        out_specs=[vmem] * 6,
        out_shape=[
            jax.ShapeDtypeStruct((rows, width), BF),
            jax.ShapeDtypeStruct((2, rows, width), BF),
            jax.ShapeDtypeStruct((chunks, heads // chunks, rows), F32),
            jax.ShapeDtypeStruct((chunks, rows, heads // chunks), F32),
            jax.ShapeDtypeStruct((2, width, PAIR), BF),
            jax.ShapeDtypeStruct((rows, width), BF),
        ],
        scratch_shapes=[
            VMEM((3, width // wide, width, wide), BF),
            pltpu.SemaphoreType.DMA((3, width // wide)),
        ],
        compiler_params=params(58),
        cost_estimate=cost(6 * rows * width * width, 6 * width * width + 12 * rows * width),
        name="project",
    )(tokens, wq, wk, wv, log_decay, cot)


def flip_kernel(tag, tok, out, tag_out):
    tag_out[0] = tag[0]
    out[...] = tok[...].T


def flip(tag, tokens):
    rows, width = tokens.shape
    whole = pl.BlockSpec(memory_space=VMEM)
    smem = pl.BlockSpec(memory_space=pltpu.SMEM)
    return pl.pallas_call(
        flip_kernel,
        in_specs=[smem, whole],
        out_specs=[whole, smem],
        out_shape=[
            jax.ShapeDtypeStruct((width, rows), BF),
            jax.ShapeDtypeStruct((1,), jnp.int32),
        ],
        compiler_params=params(16),
        cost_estimate=cost(0, 4 * rows * width),
        name="flip",
    )(tag, tokens)


def stack_kernel(*refs):
    out = refs[-1]
    for i in range(out.shape[0]):
        out[i] = refs[i][...]


def stack(parts, after):
    shape = parts[0].shape
    whole = pl.BlockSpec(memory_space=VMEM)
    return pl.pallas_call(
        stack_kernel,
        in_specs=[whole] * len(parts) + [pl.BlockSpec(memory_space=pl.ANY)],
        out_specs=whole,
        out_shape=jax.ShapeDtypeStruct((len(parts), *shape), BF),
        compiler_params=params(16),
        cost_estimate=cost(0, 4 * len(parts) * math.prod(shape)),
        name="stack",
    )(*parts, after)


def scan_kernel(place, got, out, xs, decays, states):
    both = got[...].astype(F32)
    xs[...] = both[:, :8, :]
    total = both[:, 8:9, :] + both[:, 9:10, :] + both[:, 10:11, :]
    decays[...] = jnp.broadcast_to(jnp.exp(total), decays.shape)
    backward = place[0] >= DEVS // 2

    def one(i, state):
        at = jnp.where(backward, DEVS - 1 - i, i)
        states[at] = state
        return decays[at] * state + xs[at]

    lax.fori_loop(0, DEVS, one, jnp.zeros((8, PAIR), F32), unroll=8)
    out[...] = states[...].reshape(DEVS * 8, PAIR).astype(BF)


def scan(place, got):
    whole = pl.BlockSpec(memory_space=VMEM)
    return pl.pallas_call(
        scan_kernel,
        in_specs=[pl.BlockSpec(memory_space=pltpu.SMEM), whole],
        out_specs=whole,
        out_shape=jax.ShapeDtypeStruct((DEVS * 8, PAIR), BF),
        scratch_shapes=[VMEM((DEVS, 8, PAIR), F32)] * 3,
        compiler_params=params(24),
        cost_estimate=cost(2 * DEVS * 8 * PAIR, 4 * DEVS * 16 * PAIR),
        name="scan",
    )(place, got)


def near_kernel(lin_scale, place, blocks, q_ref, kv, ptok, wk, wv, cot, run, runt, out, dq_out, own, prev, tag_out):
    tag_out[0] = place[0]
    soft_scale = 1.0 / math.sqrt(DH)
    n_own = jnp.int32(0)
    n_prev = jnp.int32(0)
    for j in range(blocks.shape[1]):
        n_own += (blocks[0, j] == place[0]).astype(jnp.int32)
        n_prev += (blocks[0, j] == place[0] - 1).astype(jnp.int32)
    is_own = iota((1, 2 * SEG), 1) < SEG
    times = jnp.where(is_own, n_own, n_prev)
    bias = jnp.where(times > 0, 0.0, -1e30)
    times = times.astype(F32)
    head_of = iota((SEG, PAIR), 1) // DH
    head_of2 = iota((2 * SEG, PAIR), 1) // DH
    lower = iota((SEG, SEG), 0) >= iota((SEG, SEG), 1)
    zero = jnp.zeros((), BF)
    pk = dot(ptok[...], wk[...], 1, 0).astype(BF)
    pv = dot(ptok[...], wv[...], 1, 0).astype(BF)
    pairs = q_ref.shape[1] // PAIR
    work = []
    for pair in range(pairs):
        at = slice(pair * PAIR, (pair + 1) * PAIR)
        q = q_ref[:, at]
        g = cot[:, at]
        kk = jnp.concatenate([kv[0, :, at], pk[:, at]], axis=0)
        vv = jnp.concatenate([kv[1, :, at], pv[:, at]], axis=0)
        for i in range(2):
            mine = head_of == i
            work.append(
                (
                    dot(jnp.where(mine, q, zero), kk, 1, 1),
                    dot(jnp.where(mine, g, zero), vv, 1, 1),
                )
            )
    mats = []
    for head in range(2 * pairs):
        scores, pgrad = work[head]
        col = runt[0, :, head : head + 1]
        row = run[0, head : head + 1, :]
        dec = jnp.where(lower, jnp.exp(jnp.minimum(col - row, 0.0)), 0.0) * lin_scale
        logits = scores * soft_scale + bias
        peak = jnp.max(logits, axis=1, keepdims=True)
        terms = jnp.exp(logits - peak) * times
        probs = terms * (1.0 / jnp.sum(terms, axis=1, keepdims=True))
        inner = jnp.sum(probs * pgrad, axis=1, keepdims=True)
        dlog = probs * (pgrad - inner) * soft_scale
        a = jnp.concatenate([probs[:, :SEG] + scores[:, :SEG] * dec, probs[:, SEG:]], axis=1)
        b = jnp.concatenate([dlog[:, :SEG] + pgrad[:, :SEG] * dec, dlog[:, SEG:]], axis=1)
        mats.append((a.astype(BF), b.astype(BF)))
    for pair in range(pairs):
        at = slice(pair * PAIR, (pair + 1) * PAIR)
        q = q_ref[:, at]
        g = cot[:, at]
        kk = jnp.concatenate([kv[0, :, at], pk[:, at]], axis=0)
        vv = jnp.concatenate([kv[1, :, at], pv[:, at]], axis=0)
        qt = q.T
        gt = g.T
        res = []
        for i in range(2):
            a, b = mats[2 * pair + i]
            half = slice(i * DH, (i + 1) * DH)
            res.append((dot(a, vv, 1, 0), dot(b, kk, 1, 0), dot(qt[half], b, 1, 0), dot(gt[half], a, 1, 0)))
        out[:, at] = jnp.where(head_of == 0, res[0][0], res[1][0])
        dq_out[:, at] = jnp.where(head_of == 0, res[0][1], res[1][1])
        for part in range(2):
            sums = jnp.concatenate([res[0][2 + part], res[1][2 + part]], axis=0).T
            own[part, :, at] = sums[:SEG]
            prev[part, :, at] = sums[SEG:].astype(BF)


def near(place, blocks, q, kv, prev_tokens, wk, wv, cot, run, runt, lin_scale):
    rows, width = q.shape
    heads = run.shape[1]
    smem = pl.BlockSpec(memory_space=pltpu.SMEM)
    col = pl.BlockSpec((rows, CHUNK), lambda i: (0, i))
    two = pl.BlockSpec((2, rows, CHUNK), lambda i: (0, 0, i))
    weight = pl.BlockSpec((width, CHUNK), lambda i: (0, i))
    return pl.pallas_call(
        functools.partial(near_kernel, lin_scale),
        grid=(width // CHUNK,),
        in_specs=[
            smem,
            smem,
            col,
            two,
            pl.BlockSpec((rows, width), lambda i: (0, 0)),
            weight,
            weight,
            col,
            pl.BlockSpec((1, heads, rows), lambda i: (i, 0, 0)),
            pl.BlockSpec((1, rows, heads), lambda i: (i, 0, 0)),
        ],
        out_specs=[col, col, two, two, smem],
        out_shape=[
            jax.ShapeDtypeStruct((rows, width), F32),
            jax.ShapeDtypeStruct((rows, width), F32),
            jax.ShapeDtypeStruct((2, rows, width), F32),
            jax.ShapeDtypeStruct((2, rows, width), BF),
            jax.ShapeDtypeStruct((1,), jnp.int32),
        ],
        compiler_params=params(58),
        cost_estimate=cost(4000 * 1000 * 1000, 16 * 1000 * 1000, 1000 * 1000),
        name="near",
    )(place, blocks, q, kv, prev_tokens, wk, wv, cot, run, runt)


def join_kernel(lin_scale, near_out, dq_in, own, nxt, q, kv, cot, runt, states, layer, delta):
    head_of = iota((SEG, PAIR), 1) // DH
    diag = iota((PAIR, PAIR), 0) // DH == iota((PAIR, PAIR), 1) // DH
    zero = jnp.zeros((), BF)
    pairs = q.shape[1] // PAIR
    work = []
    for pair in range(pairs):
        at = slice(pair * PAIR, (pair + 1) * PAIR)
        before, after = (
            jnp.where(diag, jnp.concatenate([states[part, pair]] * 2, axis=0), zero)
            for part in range(2)
        )
        work.append(
            (
                dot(q[:, at], before, 1, 0),
                dot(cot[:, at], before, 1, 1),
                dot(kv[1, :, at], after, 1, 1),
                dot(kv[0, :, at], after, 1, 0),
            )
        )
    for pair in range(pairs):
        at = slice(pair * PAIR, (pair + 1) * PAIR)
        run = jnp.where(
            head_of == 0,
            runt[pair // 2, :, 2 * (pair % 2) : 2 * (pair % 2) + 1],
            runt[pair // 2, :, 2 * (pair % 2) + 1 : 2 * (pair % 2) + 2],
        )
        growth = jnp.exp(run) * lin_scale
        fading = jnp.exp(run[SEG - 1 : SEG, :] - run)
        from_q, from_g, from_v, from_k = work[pair]
        layer[:, at] = (near_out[:, at] + growth * from_q).astype(BF)
        dq = dq_in[:, at] + growth * from_g
        dk = own[0, :, at] + fading * from_v + nxt[0, :, at].astype(F32)
        dv = own[1, :, at] + fading * from_k + nxt[1, :, at].astype(F32)
        delta[pair, :, :PAIR] = dq.astype(BF)
        delta[pair, :, PAIR : 2 * PAIR] = dk.astype(BF)
        delta[pair, :, 2 * PAIR :] = dv.astype(BF)


def join(near_out, dq, own, nxt, q, kv, cot, runt, states, lin_scale):
    rows, width = q.shape
    pairs = width // PAIR
    wide = 2 * CHUNK
    col = pl.BlockSpec((rows, wide), lambda i: (0, i))
    two = pl.BlockSpec((2, rows, wide), lambda i: (0, 0, i))
    return pl.pallas_call(
        functools.partial(join_kernel, lin_scale),
        grid=(width // wide,),
        in_specs=[
            col,
            col,
            two,
            two,
            col,
            two,
            col,
            pl.BlockSpec((2, rows, runt.shape[2]), lambda i: (i, 0, 0)),
            pl.BlockSpec((2, wide // PAIR, DH, PAIR), lambda i: (0, i, 0, 0)),
        ],
        out_specs=[col, pl.BlockSpec((wide // PAIR, rows, 3 * PAIR), lambda i: (i, 0, 0))],
        out_shape=[
            jax.ShapeDtypeStruct((rows, width), BF),
            jax.ShapeDtypeStruct((pairs, rows, 3 * PAIR), BF),
        ],
        compiler_params=params(58),
        cost_estimate=cost(8 * rows * PAIR * PAIR * pairs, 24 * rows * width),
        name="join",
    )(near_out, dq, own, nxt, q, kv, cot, runt, states)


def back_kernel(tag, delta, wq, wk, wv, out, tag_out, total):
    step = pl.program_id(0)
    tag_out[0] = tag[0]

    @pl.when(step == 0)
    def _():
        total[...] = jnp.zeros_like(total)

    acc = total[...]
    for part, w in enumerate((wq, wk, wv)):
        for half in range(2):
            acc += dot(
                delta[half, :, part * PAIR : (part + 1) * PAIR],
                w[:, half * PAIR : (half + 1) * PAIR],
                1,
                1,
            )
    total[...] = acc

    @pl.when(step == pl.num_programs(0) - 1)
    def _():
        out[...] = acc.astype(BF)


def back(tag, delta, wq, wk, wv):
    pairs, rows, _ = delta.shape
    width = wq.shape[0]
    smem = pl.BlockSpec(memory_space=pltpu.SMEM)
    weight = pl.BlockSpec((width, 2 * PAIR), lambda i: (0, i))
    return pl.pallas_call(
        back_kernel,
        grid=(pairs // 2,),
        in_specs=[smem, pl.BlockSpec((2, rows, 3 * PAIR), lambda i: (i, 0, 0)), weight, weight, weight],
        out_specs=[
            pl.BlockSpec((rows, width), lambda i: (0, 0)),
            smem,
        ],
        out_shape=[
            jax.ShapeDtypeStruct((rows, width), BF),
            jax.ShapeDtypeStruct((1,), jnp.int32),
        ],
        scratch_shapes=[VMEM((rows, width), F32)],
        compiler_params=params(58),
        cost_estimate=cost(6 * rows * width * width, 6 * width * width + 8 * rows * width),
        name="back",
    )(tag, delta, wq, wk, wv)


def outer_kernel(core, at_x, mine, theirs, delta, out):
    near_x = mine.shape[0]
    left, right = [], []
    for tokt, c in ((mine, core[0]), (theirs, 1 - core[0])):
        for i in range(near_x):
            left.append(tokt[i])
            right.append(delta[c * near_x + lax.rem(at_x[0] + near_x - BACK[i], near_x)])
    left = jnp.concatenate(left, axis=1)
    out[...] = dot(left, jnp.concatenate(right, axis=0), 1, 0).astype(BF)


def outer(core, at_x, mine, theirs, delta):
    near_count, rows, cols = delta.shape
    width = mine.shape[1]
    smem = pl.BlockSpec(memory_space=pltpu.SMEM)
    tok = pl.BlockSpec((near_count // 2, width // 2, rows), lambda i: (0, i, 0))
    return pl.pallas_call(
        outer_kernel,
        grid=(2,),
        in_specs=[
            smem,
            smem,
            tok,
            tok,
            pl.BlockSpec((near_count, rows, cols), lambda i: (0, 0, 0)),
        ],
        out_specs=pl.BlockSpec((width // 2, cols), lambda i: (i, 0)),
        out_shape=jax.ShapeDtypeStruct((width, cols), BF),
        compiler_params=params(20),
        cost_estimate=cost(
            2 * near_count * rows * cols * width, 2 * near_count * rows * (width + cols)
        ),
        name="outer",
    )(core, at_x, mine, theirs, delta)


def device(yl, c, x, z, yh):
    return (((yl * 2 + c) * 4 + x) * 4 + z) * 2 + yh


def gather_groups():
    zero = [
        [device(yl, 0, x, z, yh) for yl in range(2) for z in range(4) for yh in range(2)]
        for x in range(4)
    ]
    one = [
        [device(yl, 1, x, z, yh) for x in range(4) for yl in range(2) for yh in range(2)]
        for z in range(4)
    ]
    return zero + one


def ring(array, by):
    route = []
    for yl in range(2):
        for x in range(4):
            for z in range(4):
                for yh in range(2):
                    route.append((device(yl, 0, x, z, yh), device(yl, 0, (x + by) % 4, z, yh)))
                    route.append((device(yl, 1, x, z, yh), device(yl, 1, x, (z + by) % 4, yh)))
    return lax.ppermute(array, AX, route)


def place_kernel(pieces, count, side, at_x, at_z, *refs):
    grads, mark, sems = refs[-5:-2], refs[-2], refs[-1]
    mark[...] = jnp.zeros_like(mark)

    def put(rank):
        copies = []

        def start(src, dst):
            copy = pltpu.make_async_copy(src, dst, sems.at[len(copies)])
            copy.start()
            copies.append(copy)

        for n in range(count):
            source = refs[n]
            rows = source.shape[1]
            by_row = rank[n]
            for place, by in enumerate(pieces):
                x = lax.rem(at_x[0] + by + 4, 4)
                z = lax.rem(at_z[0] + by + 4, 4)
                for part, grad in enumerate(grads):
                    lanes = pl.ds(part * PAIR, PAIR)
                    for i in range(8):
                        if by_row:
                            to = pl.multiple_of(((i % 2) * 4 + z) * rows, rows)
                            at = (pl.ds(to, rows), pl.ds((4 + i // 2) * PAIR, PAIR))
                        else:
                            to = pl.multiple_of(x * PAIR, PAIR)
                            at = (pl.ds(i * rows, rows), pl.ds(to, PAIR))
                        start(source.at[place * 8 + i, :, lanes], grad.at[at])
        for copy in copies:
            copy.wait()

    @pl.when(side[0] == 0)
    def _():
        put((False, True))

    @pl.when(side[0] == 1)
    def _():
        put((True, False))


def place_tiles(where, pieces, sources, grads, width):
    hbm = pl.BlockSpec(memory_space=pl.ANY)
    smem = pl.BlockSpec(memory_space=pltpu.SMEM)
    first = 3 + len(sources)
    return pl.pallas_call(
        functools.partial(place_kernel, pieces, len(sources)),
        in_specs=[smem] * 3 + [hbm] * (len(sources) + len(grads)),
        out_specs=[hbm] * 3 + [pl.BlockSpec(memory_space=VMEM)],
        out_shape=[jax.ShapeDtypeStruct((width, width), BF)] * 3
        + [jax.ShapeDtypeStruct((8, PAIR), F32)],
        scratch_shapes=[pltpu.SemaphoreType.DMA((24 * len(pieces) * len(sources),))],
        input_output_aliases={first + i: i for i in range(len(grads))},
        compiler_params=params(16),
        cost_estimate=cost(0, 4 * sum(a.size for a in sources)),
        name="place",
    )(*where, *sources, *grads)


def halves_kernel(behind, ahead, after, first, second, both):
    del after
    half = first.shape[0]
    first[...] = behind[:half]
    second[...] = ahead[half:]
    both[: 2 * half] = behind[...]
    both[2 * half :] = ahead[...]


def halves(behind, ahead, after):
    pairs, *rest = behind.shape
    whole = pl.BlockSpec(memory_space=VMEM)
    return pl.pallas_call(
        halves_kernel,
        in_specs=[whole, whole, pl.BlockSpec(memory_space=pl.ANY)],
        out_specs=[whole] * 3,
        out_shape=[jax.ShapeDtypeStruct((n, *rest), BF) for n in (pairs // 2, pairs // 2, 2 * pairs)],
        compiler_params=params(16),
        cost_estimate=cost(0, 12 * behind.size),
        name="halves",
    )(behind, ahead, after)


def gather_tiles(piece, where, width):
    swap = [(0, 1), (1, 0)]

    def swapped(array):
        return lax.ppermute(array, "c", swap)

    rows, cols = piece.shape
    here = lax.all_to_all(
        jnp.broadcast_to(piece[None], (16, rows, cols)), AX, 0, 0, axis_index_groups=gather_groups()
    ).reshape(8, 2 * rows, cols)
    behind = ring(here, 1)
    ahead = ring(here, -1)
    *grads, mark = place_tiles(where, (0,), (here, swapped(here)), (), width)
    half_a, half_b, both = halves(behind, ahead, mark)
    far_a = ring(half_a, 1)
    far_b = ring(half_b, -1)
    *grads, mark = place_tiles(where, (-1, 1), (both, swapped(both)), grads, width)
    far = stack([far_a, far_b], mark).reshape(here.shape)
    far_c = swapped(far)
    *grads, _ = place_tiles(where, (2,), (far,), grads, width)
    core, *rest = where
    *grads, _ = place_tiles((1 - core, *rest), (2,), (far_c,), grads, width)
    return grads


def shards(tokens, wq, wk, wv, log_decay, neighbour_blocks, cot):
    rows, width = tokens.shape
    lin_scale = 1.0 / (DH * math.sqrt(rows))
    place = lax.axis_index(AX).astype(jnp.int32).reshape(1)
    core = lax.axis_index("c").astype(jnp.int32).reshape(1)

    at_x = lax.axis_index("x").astype(jnp.int32).reshape(1)
    swap = [(0, 1), (1, 0)]
    q, kv, run, runt, msg, own_tokens = project(tokens, wq, wk, wv, log_decay, cot, lin_scale)
    prev_tokens = lax.ppermute(own_tokens, AX, [(i, i + 1) for i in range(DEVS - 1)])
    got = lax.all_to_all(msg.reshape(DEVS, 16, PAIR), AX, 0, 0)
    near_out, dq, own, prev, place = near(
        place, neighbour_blocks, q, kv, prev_tokens, wk, wv, cot, run, runt, lin_scale
    )
    nxt = lax.ppermute(prev, AX, [(i + 1, i) for i in range(DEVS - 1)])
    tokt, place = flip(place, own_tokens)
    around = [lax.ppermute(tokt, "x", [(i, (i + d) % 4) for i in range(4)]) for d in BACK[1:]]
    states = scan(place, got)
    states = lax.all_to_all(states.reshape(DEVS, 8, PAIR), AX, 0, 0)
    states = states.reshape(2, width // PAIR, DH, PAIR)
    layer, delta = join(near_out, dq, own, nxt, q, kv, cot, runt, states, lin_scale)

    delta8 = lax.all_to_all(delta, NEAR8, 0, 0)
    mine = stack([tokt, *around], delta)
    theirs = lax.ppermute(mine, "c", swap)
    tokens_grad, later_core = back(core, delta, wq, wk, wv)
    partial = outer(later_core, at_x, mine, theirs, delta8)
    parts = lax.all_to_all(partial.reshape(16, width // 16, 3 * PAIR), FAR16, 0, 0)
    grad_norm = 1.0 / math.sqrt(rows * DEVS)
    piece = (jnp.sum(parts.astype(F32), axis=0) * grad_norm).astype(BF)
    at_z = lax.axis_index("z").astype(jnp.int32).reshape(1)
    gq, gk, gv = gather_tiles(piece, (core, at_x, at_z), width)
    return layer, tokens_grad, gq, gk, gv


def solution(mesh):
    chips = Mesh(mesh.devices.reshape(2, 2, 4, 4, 2), AX)
    tok = P(AX, None)
    return jax.shard_map(
        shards,
        mesh=chips,
        in_specs=(tok, P(), P(), P(), P(None, AX), tok, tok),
        out_specs=(tok, tok, P(), P(), P()),
        check_vma=False,
    )
```

```python
import functools
import math

import jax
import jax.numpy as jnp
from jax import lax
from jax.experimental import pallas as pl
from jax.experimental.pallas import tpu as pltpu
from jax.sharding import Mesh
from jax.sharding import PartitionSpec as P

BF = jnp.bfloat16
F32 = jnp.float32
AX = ("yl", "c", "x", "z", "yh")
NEAR8 = ("c", "x")
FAR16 = ("yl", "z", "yh")
PLANE = ("x", "yl", "z", "yh")
SEG = 128
PAIR = 128
DH = 64
DEVS = 128
VMEM = pltpu.VMEM
HIGH = lax.Precision.HIGHEST


def dot(a, b, ca, cb, precision=None):
    return lax.dot_general(
        a, b, (((ca,), (cb,)), ((), ())), precision=precision, preferred_element_type=F32
    )


def iota(shape, axis):
    return lax.broadcasted_iota(jnp.int32, shape, axis)


def params(mib):
    return pltpu.CompilerParams(vmem_limit_bytes=mib << 20)


def cost(flops, moved, trans=0):
    return pl.CostEstimate(flops=flops, bytes_accessed=moved, transcendentals=trans)


CHUNK = 256
WIDE = 512


def pair_lanes(columns, pair):
    shape = (columns.shape[0], PAIR)
    return jnp.where(
        iota(shape, 1) < DH,
        columns[:, 2 * pair : 2 * pair + 1],
        columns[:, 2 * pair + 1 : 2 * pair + 2],
    )


def project_kernel(lin_scale, tok, wq, wk, wv, decay, cot, q_out, kv_out, run_out, runt_out, msg, tok_out, held, sems):
    width = tok.shape[1]
    wide = held.shape[3]
    copies = []
    for step in range(width // wide):
        for part, w in enumerate((wq, wk, wv)):
            copy = pltpu.make_async_copy(
                w.at[:, pl.ds(step * wide, wide)], held.at[part, step], sems.at[part, step]
            )
            copy.start()
            copies.append(copy)
    x = tok[...]
    tok_out[...] = x
    ld = decay[...]
    lower = (iota((SEG, SEG), 0) >= iota((SEG, SEG), 1)).astype(F32)
    runt = dot(lower, ld, 1, 1, HIGH)
    run = dot(ld, lower, 1, 1, HIGH)
    group = ld.shape[0] // run_out.shape[0]
    for step in range(run_out.shape[0]):
        runt_out[step] = runt[:, step * group : (step + 1) * group]
        run_out[step] = run[step * group : (step + 1) * group, :]
    rows = iota((8, PAIR), 0)
    first = iota((DH, PAIR), 1) < DH
    for step in range(width // wide):
        for part in range(3):
            copies[step * 3 + part].wait()
        at = slice(step * wide, (step + 1) * wide)
        q = dot(x, held[0, step], 1, 0).astype(BF)
        k = dot(x, held[1, step], 1, 0).astype(BF)
        v = dot(x, held[2, step], 1, 0).astype(BF)
        q_out[:, at] = q
        kv_out[0, :, at] = k
        kv_out[1, :, at] = v
        here = []
        for part in range(wide // PAIR):
            cols = slice(part * PAIR, (part + 1) * PAIR)
            pair = step * (wide // PAIR) + part
            lanes = pair_lanes(runt, pair)
            total = lanes[SEG - 1 : SEG, :]
            g = cot[:, pair * PAIR : (pair + 1) * PAIR].astype(F32)
            weighted = (v[:, cols].astype(F32) * jnp.exp(total - lanes)).astype(BF)
            scaled = (g * jnp.exp(lanes)).astype(BF)
            states = (
                dot(k[:, cols], weighted, 0, 0),
                dot(q[:, cols], scaled, 0, 0) * lin_scale,
            )
            here.append((pair, total, states))
        for pair, total, states in here:
            high = total.astype(BF).astype(F32)
            mid = (total - high).astype(BF).astype(F32)
            low = total - high - mid
            tail = jnp.where(
                rows == 0, high, jnp.where(rows == 1, mid, jnp.where(rows == 2, low, 0.0))
            )
            tail = jnp.broadcast_to(tail[None], (8, 8, PAIR))
            for part, full in enumerate(states):
                own = jnp.where(first, full[:DH], full[DH:]).reshape(8, 8, PAIR)
                sent = jnp.concatenate([own, tail], axis=1).reshape(PAIR, PAIR)
                msg[part, pair * PAIR : (pair + 1) * PAIR, :] = sent.astype(BF)


def project(tokens, wq, wk, wv, log_decay, cot, lin_scale):
    rows, width = tokens.shape
    heads = log_decay.shape[0]
    chunks = width // CHUNK
    wide = WIDE
    vmem = pl.BlockSpec(memory_space=VMEM)
    hbm = pl.BlockSpec(memory_space=pltpu.HBM)
    return pl.pallas_call(
        functools.partial(project_kernel, lin_scale),
        in_specs=[vmem, hbm, hbm, hbm, vmem, vmem],
        out_specs=[vmem] * 6,
        out_shape=[
            jax.ShapeDtypeStruct((rows, width), BF),
            jax.ShapeDtypeStruct((2, rows, width), BF),
            jax.ShapeDtypeStruct((chunks, heads // chunks, rows), F32),
            jax.ShapeDtypeStruct((chunks, rows, heads // chunks), F32),
            jax.ShapeDtypeStruct((2, width, PAIR), BF),
            jax.ShapeDtypeStruct((rows, width), BF),
        ],
        scratch_shapes=[
            VMEM((3, width // wide, width, wide), BF),
            pltpu.SemaphoreType.DMA((3, width // wide)),
        ],
        compiler_params=params(58),
        cost_estimate=cost(6 * rows * width * width, 6 * width * width + 12 * rows * width),
        name="project",
    )(tokens, wq, wk, wv, log_decay, cot)


def flip_kernel(tag, tok, out, tag_out):
    tag_out[0] = tag[0]
    out[...] = tok[...].T


def flip(tag, tokens):
    rows, width = tokens.shape
    whole = pl.BlockSpec(memory_space=VMEM)
    smem = pl.BlockSpec(memory_space=pltpu.SMEM)
    return pl.pallas_call(
        flip_kernel,
        in_specs=[smem, whole],
        out_specs=[whole, smem],
        out_shape=[
            jax.ShapeDtypeStruct((width, rows), BF),
            jax.ShapeDtypeStruct((1,), jnp.int32),
        ],
        compiler_params=params(16),
        cost_estimate=cost(0, 4 * rows * width),
        name="flip",
    )(tag, tokens)


def stack_kernel(*refs):
    out = refs[-1]
    for i in range(out.shape[0]):
        out[i] = refs[i][...]


def stack(parts, after):
    shape = parts[0].shape
    whole = pl.BlockSpec(memory_space=VMEM)
    return pl.pallas_call(
        stack_kernel,
        in_specs=[whole] * len(parts) + [pl.BlockSpec(memory_space=pl.ANY)],
        out_specs=whole,
        out_shape=jax.ShapeDtypeStruct((len(parts), *shape), BF),
        compiler_params=params(16),
        cost_estimate=cost(0, 4 * len(parts) * math.prod(shape)),
        name="stack",
    )(*parts, after)


def scan_kernel(place, got, out, xs, decays, states):
    both = got[...].astype(F32)
    xs[...] = both[:, :8, :]
    total = both[:, 8:9, :] + both[:, 9:10, :] + both[:, 10:11, :]
    decays[...] = jnp.broadcast_to(jnp.exp(total), decays.shape)
    backward = place[0] >= DEVS // 2

    def one(i, state):
        at = jnp.where(backward, DEVS - 1 - i, i)
        states[at] = state
        return decays[at] * state + xs[at]

    lax.fori_loop(0, DEVS, one, jnp.zeros((8, PAIR), F32), unroll=8)
    out[...] = states[...].reshape(DEVS * 8, PAIR).astype(BF)


def scan(place, got):
    whole = pl.BlockSpec(memory_space=VMEM)
    return pl.pallas_call(
        scan_kernel,
        in_specs=[pl.BlockSpec(memory_space=pltpu.SMEM), whole],
        out_specs=whole,
        out_shape=jax.ShapeDtypeStruct((DEVS * 8, PAIR), BF),
        scratch_shapes=[VMEM((DEVS, 8, PAIR), F32)] * 3,
        compiler_params=params(24),
        cost_estimate=cost(2 * DEVS * 8 * PAIR, 4 * DEVS * 16 * PAIR),
        name="scan",
    )(place, got)


def near_kernel(lin_scale, place, blocks, q_ref, kv, ptok, wk, wv, cot, run, runt, out, dq_out, own, prev, tag_out):
    tag_out[0] = place[0]
    soft_scale = 1.0 / math.sqrt(DH)
    n_own = jnp.int32(0)
    n_prev = jnp.int32(0)
    for j in range(blocks.shape[1]):
        n_own += (blocks[0, j] == place[0]).astype(jnp.int32)
        n_prev += (blocks[0, j] == place[0] - 1).astype(jnp.int32)
    is_own = iota((1, 2 * SEG), 1) < SEG
    times = jnp.where(is_own, n_own, n_prev)
    bias = jnp.where(times > 0, 0.0, -1e30)
    times = times.astype(F32)
    head_of = iota((SEG, PAIR), 1) // DH
    head_of2 = iota((2 * SEG, PAIR), 1) // DH
    lower = iota((SEG, SEG), 0) >= iota((SEG, SEG), 1)
    zero = jnp.zeros((), BF)
    pk = dot(ptok[...], wk[...], 1, 0).astype(BF)
    pv = dot(ptok[...], wv[...], 1, 0).astype(BF)
    pairs = q_ref.shape[1] // PAIR
    work = []
    for pair in range(pairs):
        at = slice(pair * PAIR, (pair + 1) * PAIR)
        q = q_ref[:, at]
        g = cot[:, at]
        kk = jnp.concatenate([kv[0, :, at], pk[:, at]], axis=0)
        vv = jnp.concatenate([kv[1, :, at], pv[:, at]], axis=0)
        for i in range(2):
            mine = head_of == i
            work.append(
                (
                    dot(jnp.where(mine, q, zero), kk, 1, 1),
                    dot(jnp.where(mine, g, zero), vv, 1, 1),
                )
            )
    mats = []
    for head in range(2 * pairs):
        scores, pgrad = work[head]
        col = runt[0, :, head : head + 1]
        row = run[0, head : head + 1, :]
        dec = jnp.where(lower, jnp.exp(jnp.minimum(col - row, 0.0)), 0.0) * lin_scale
        logits = scores * soft_scale + bias
        peak = jnp.max(logits, axis=1, keepdims=True)
        terms = jnp.exp(logits - peak) * times
        probs = terms * (1.0 / jnp.sum(terms, axis=1, keepdims=True))
        inner = jnp.sum(probs * pgrad, axis=1, keepdims=True)
        dlog = probs * (pgrad - inner) * soft_scale
        a = jnp.concatenate([probs[:, :SEG] + scores[:, :SEG] * dec, probs[:, SEG:]], axis=1)
        b = jnp.concatenate([dlog[:, :SEG] + pgrad[:, :SEG] * dec, dlog[:, SEG:]], axis=1)
        mats.append((a.astype(BF), b.astype(BF)))
    for pair in range(pairs):
        at = slice(pair * PAIR, (pair + 1) * PAIR)
        q = q_ref[:, at]
        g = cot[:, at]
        kk = jnp.concatenate([kv[0, :, at], pk[:, at]], axis=0)
        vv = jnp.concatenate([kv[1, :, at], pv[:, at]], axis=0)
        qt = q.T
        gt = g.T
        res = []
        for i in range(2):
            a, b = mats[2 * pair + i]
            half = slice(i * DH, (i + 1) * DH)
            res.append((dot(a, vv, 1, 0), dot(b, kk, 1, 0), dot(qt[half], b, 1, 0), dot(gt[half], a, 1, 0)))
        out[:, at] = jnp.where(head_of == 0, res[0][0], res[1][0])
        dq_out[:, at] = jnp.where(head_of == 0, res[0][1], res[1][1])
        for part in range(2):
            sums = jnp.concatenate([res[0][2 + part], res[1][2 + part]], axis=0).T
            own[part, :, at] = sums[:SEG]
            prev[part, :, at] = sums[SEG:].astype(BF)


def near(place, blocks, q, kv, prev_tokens, wk, wv, cot, run, runt, lin_scale):
    rows, width = q.shape
    heads = run.shape[1]
    smem = pl.BlockSpec(memory_space=pltpu.SMEM)
    col = pl.BlockSpec((rows, CHUNK), lambda i: (0, i))
    two = pl.BlockSpec((2, rows, CHUNK), lambda i: (0, 0, i))
    weight = pl.BlockSpec((width, CHUNK), lambda i: (0, i))
    return pl.pallas_call(
        functools.partial(near_kernel, lin_scale),
        grid=(width // CHUNK,),
        in_specs=[
            smem,
            smem,
            col,
            two,
            pl.BlockSpec((rows, width), lambda i: (0, 0)),
            weight,
            weight,
            col,
            pl.BlockSpec((1, heads, rows), lambda i: (i, 0, 0)),
            pl.BlockSpec((1, rows, heads), lambda i: (i, 0, 0)),
        ],
        out_specs=[col, col, two, two, smem],
        out_shape=[
            jax.ShapeDtypeStruct((rows, width), F32),
            jax.ShapeDtypeStruct((rows, width), F32),
            jax.ShapeDtypeStruct((2, rows, width), F32),
            jax.ShapeDtypeStruct((2, rows, width), BF),
            jax.ShapeDtypeStruct((1,), jnp.int32),
        ],
        compiler_params=params(58),
        cost_estimate=cost(4000 * 1000 * 1000, 16 * 1000 * 1000, 1000 * 1000),
        name="near",
    )(place, blocks, q, kv, prev_tokens, wk, wv, cot, run, runt)


def join_kernel(lin_scale, near_out, dq_in, own, nxt, q, kv, cot, runt, states, layer, delta):
    head_of = iota((SEG, PAIR), 1) // DH
    diag = iota((PAIR, PAIR), 0) // DH == iota((PAIR, PAIR), 1) // DH
    zero = jnp.zeros((), BF)
    pairs = q.shape[1] // PAIR
    work = []
    for pair in range(pairs):
        at = slice(pair * PAIR, (pair + 1) * PAIR)
        before, after = (
            jnp.where(diag, jnp.concatenate([states[part, pair]] * 2, axis=0), zero)
            for part in range(2)
        )
        work.append(
            (
                dot(q[:, at], before, 1, 0),
                dot(cot[:, at], before, 1, 1),
                dot(kv[1, :, at], after, 1, 1),
                dot(kv[0, :, at], after, 1, 0),
            )
        )
    for pair in range(pairs):
        at = slice(pair * PAIR, (pair + 1) * PAIR)
        run = jnp.where(
            head_of == 0,
            runt[pair // 2, :, 2 * (pair % 2) : 2 * (pair % 2) + 1],
            runt[pair // 2, :, 2 * (pair % 2) + 1 : 2 * (pair % 2) + 2],
        )
        growth = jnp.exp(run) * lin_scale
        fading = jnp.exp(run[SEG - 1 : SEG, :] - run)
        from_q, from_g, from_v, from_k = work[pair]
        layer[:, at] = (near_out[:, at] + growth * from_q).astype(BF)
        dq = dq_in[:, at] + growth * from_g
        dk = own[0, :, at] + fading * from_v + nxt[0, :, at].astype(F32)
        dv = own[1, :, at] + fading * from_k + nxt[1, :, at].astype(F32)
        delta[pair, :, :PAIR] = dq.astype(BF)
        delta[pair, :, PAIR : 2 * PAIR] = dk.astype(BF)
        delta[pair, :, 2 * PAIR :] = dv.astype(BF)


def join(near_out, dq, own, nxt, q, kv, cot, runt, states, lin_scale):
    rows, width = q.shape
    pairs = width // PAIR
    wide = 2 * CHUNK
    col = pl.BlockSpec((rows, wide), lambda i: (0, i))
    two = pl.BlockSpec((2, rows, wide), lambda i: (0, 0, i))
    return pl.pallas_call(
        functools.partial(join_kernel, lin_scale),
        grid=(width // wide,),
        in_specs=[
            col,
            col,
            two,
            two,
            col,
            two,
            col,
            pl.BlockSpec((2, rows, runt.shape[2]), lambda i: (i, 0, 0)),
            pl.BlockSpec((2, wide // PAIR, DH, PAIR), lambda i: (0, i, 0, 0)),
        ],
        out_specs=[col, pl.BlockSpec((wide // PAIR, rows, 3 * PAIR), lambda i: (i, 0, 0))],
        out_shape=[
            jax.ShapeDtypeStruct((rows, width), BF),
            jax.ShapeDtypeStruct((pairs, rows, 3 * PAIR), BF),
        ],
        compiler_params=params(58),
        cost_estimate=cost(8 * rows * PAIR * PAIR * pairs, 24 * rows * width),
        name="join",
    )(near_out, dq, own, nxt, q, kv, cot, runt, states)


def back_kernel(tag, delta, wq, wk, wv, out, tag_out, total):
    step = pl.program_id(0)
    tag_out[0] = tag[0]

    @pl.when(step == 0)
    def _():
        total[...] = jnp.zeros_like(total)

    acc = total[...]
    for part, w in enumerate((wq, wk, wv)):
        for half in range(2):
            acc += dot(
                delta[half, :, part * PAIR : (part + 1) * PAIR],
                w[:, half * PAIR : (half + 1) * PAIR],
                1,
                1,
            )
    total[...] = acc

    @pl.when(step == pl.num_programs(0) - 1)
    def _():
        out[...] = acc.astype(BF)


def back(tag, delta, wq, wk, wv):
    pairs, rows, _ = delta.shape
    width = wq.shape[0]
    smem = pl.BlockSpec(memory_space=pltpu.SMEM)
    weight = pl.BlockSpec((width, 2 * PAIR), lambda i: (0, i))
    return pl.pallas_call(
        back_kernel,
        grid=(pairs // 2,),
        in_specs=[smem, pl.BlockSpec((2, rows, 3 * PAIR), lambda i: (i, 0, 0)), weight, weight, weight],
        out_specs=[
            pl.BlockSpec((rows, width), lambda i: (0, 0)),
            smem,
        ],
        out_shape=[
            jax.ShapeDtypeStruct((rows, width), BF),
            jax.ShapeDtypeStruct((1,), jnp.int32),
        ],
        scratch_shapes=[VMEM((rows, width), F32)],
        compiler_params=params(58),
        cost_estimate=cost(6 * rows * width * width, 6 * width * width + 8 * rows * width),
        name="back",
    )(tag, delta, wq, wk, wv)


def outer_kernel(core, at_x, mine, theirs, delta, out):
    near_x = mine.shape[0]
    left, right = [], []
    for tokt, c in ((mine, core[0]), (theirs, 1 - core[0])):
        for i in range(near_x):
            left.append(tokt[i])
            right.append(delta[c * near_x + lax.rem(at_x[0] + near_x - i, near_x)])
    left = jnp.concatenate(left, axis=1)
    out[...] = dot(left, jnp.concatenate(right, axis=0), 1, 0).astype(BF)


def outer(core, at_x, mine, theirs, delta):
    near_count, rows, cols = delta.shape
    width = mine.shape[1]
    smem = pl.BlockSpec(memory_space=pltpu.SMEM)
    tok = pl.BlockSpec((near_count // 2, width // 2, rows), lambda i: (0, i, 0))
    return pl.pallas_call(
        outer_kernel,
        grid=(2,),
        in_specs=[
            smem,
            smem,
            tok,
            tok,
            pl.BlockSpec((near_count, rows, cols), lambda i: (0, 0, 0)),
        ],
        out_specs=pl.BlockSpec((width // 2, cols), lambda i: (i, 0)),
        out_shape=jax.ShapeDtypeStruct((width, cols), BF),
        compiler_params=params(20),
        cost_estimate=cost(
            2 * near_count * rows * cols * width, 2 * near_count * rows * (width + cols)
        ),
        name="outer",
    )(core, at_x, mine, theirs, delta)


def device(yl, c, x, z, yh):
    return (((yl * 2 + c) * 4 + x) * 4 + z) * 2 + yh


def gather_groups():
    zero = [
        [device(yl, 0, x, z, yh) for yl in range(2) for z in range(4) for yh in range(2)]
        for x in range(4)
    ]
    one = [
        [device(yl, 1, x, z, yh) for x in range(4) for yl in range(2) for yh in range(2)]
        for z in range(4)
    ]
    return zero + one


def ring(array, by):
    route = []
    for yl in range(2):
        for x in range(4):
            for z in range(4):
                for yh in range(2):
                    route.append((device(yl, 0, x, z, yh), device(yl, 0, (x + by) % 4, z, yh)))
                    route.append((device(yl, 1, x, z, yh), device(yl, 1, x, (z + by) % 4, yh)))
    return lax.ppermute(array, AX, route)


def place_kernel(pieces, count, side, at_x, at_z, *refs):
    grads, mark, sems = refs[-5:-2], refs[-2], refs[-1]
    mark[...] = jnp.zeros_like(mark)

    def put(rank):
        copies = []

        def start(src, dst):
            copy = pltpu.make_async_copy(src, dst, sems.at[len(copies)])
            copy.start()
            copies.append(copy)

        for n in range(count):
            source = refs[n]
            by_row = rank[n]
            for place, by in enumerate(pieces):
                x = lax.rem(at_x[0] + by + 4, 4)
                z = lax.rem(at_z[0] + by + 4, 4)
                for part, grad in enumerate(grads):
                    lanes = pl.ds(part * PAIR, PAIR)
                    if by_row:
                        for i in range(8):
                            start(
                                source.at[place * 8 + i, :, lanes],
                                grad.at[(i % 2) * 4 + z, :, pl.ds((4 + i // 2) * PAIR, PAIR)],
                            )
                    else:
                        start(
                            source.at[pl.ds(place * 8, 8), :, lanes],
                            grad.at[:, :, pl.ds(pl.multiple_of(x * PAIR, PAIR), PAIR)],
                        )
        for copy in copies:
            copy.wait()

    @pl.when(side[0] == 0)
    def _():
        put((False, True))

    @pl.when(side[0] == 1)
    def _():
        put((True, False))


def place_tiles(where, pieces, sources, grads, width):
    hbm = pl.BlockSpec(memory_space=pl.ANY)
    smem = pl.BlockSpec(memory_space=pltpu.SMEM)
    first = 3 + len(sources)
    return pl.pallas_call(
        functools.partial(place_kernel, pieces, len(sources)),
        in_specs=[smem] * 3 + [hbm] * (len(sources) + len(grads)),
        out_specs=[hbm] * 3 + [pl.BlockSpec(memory_space=VMEM)],
        out_shape=[jax.ShapeDtypeStruct((8, width // 8, width), BF)] * 3
        + [jax.ShapeDtypeStruct((8, PAIR), F32)],
        scratch_shapes=[pltpu.SemaphoreType.DMA((24 * len(pieces) * len(sources),))],
        input_output_aliases={first + i: i for i in range(len(grads))},
        compiler_params=params(16),
        cost_estimate=cost(0, 4 * sum(a.size for a in sources)),
        name="place",
    )(*where, *sources, *grads)


def halves_kernel(behind, ahead, after, first, second, both):
    del after
    half = first.shape[0]
    first[...] = behind[:half]
    second[...] = ahead[half:]
    both[: 2 * half] = behind[...]
    both[2 * half :] = ahead[...]


def halves(behind, ahead, after):
    pairs, *rest = behind.shape
    whole = pl.BlockSpec(memory_space=VMEM)
    return pl.pallas_call(
        halves_kernel,
        in_specs=[whole, whole, pl.BlockSpec(memory_space=pl.ANY)],
        out_specs=[whole] * 3,
        out_shape=[jax.ShapeDtypeStruct((n, *rest), BF) for n in (pairs // 2, pairs // 2, 2 * pairs)],
        compiler_params=params(16),
        cost_estimate=cost(0, 12 * behind.size),
        name="halves",
    )(behind, ahead, after)


def gather_tiles(piece, where, width):
    swap = [(0, 1), (1, 0)]

    def swapped(array):
        return lax.ppermute(array, "c", swap)

    rows, cols = piece.shape
    here = lax.all_to_all(
        jnp.broadcast_to(piece[None], (16, rows, cols)), AX, 0, 0, axis_index_groups=gather_groups()
    ).reshape(8, 2 * rows, cols)
    behind = ring(here, 1)
    ahead = ring(here, -1)
    *grads, mark = place_tiles(where, (0,), (here, swapped(here)), (), width)
    half_a, half_b, both = halves(behind, ahead, mark)
    far_a = ring(half_a, 1)
    far_b = ring(half_b, -1)
    *grads, mark = place_tiles(where, (-1, 1), (both, swapped(both)), grads, width)
    far = stack([far_a, far_b], mark).reshape(here.shape)
    far_c = swapped(far)
    *grads, _ = place_tiles(where, (2,), (far,), grads, width)
    core, *rest = where
    *grads, _ = place_tiles((1 - core, *rest), (2,), (far_c,), grads, width)
    return [grad.reshape(width, width) for grad in grads]


def shards(tokens, wq, wk, wv, log_decay, neighbour_blocks, cot):
    rows, width = tokens.shape
    lin_scale = 1.0 / (DH * math.sqrt(rows))
    place = lax.axis_index(AX).astype(jnp.int32).reshape(1)
    core = lax.axis_index("c").astype(jnp.int32).reshape(1)

    at_x = lax.axis_index("x").astype(jnp.int32).reshape(1)
    swap = [(0, 1), (1, 0)]
    q, kv, run, runt, msg, own_tokens = project(tokens, wq, wk, wv, log_decay, cot, lin_scale)
    prev_tokens = lax.ppermute(own_tokens, AX, [(i, i + 1) for i in range(DEVS - 1)])
    got = lax.all_to_all(msg.reshape(DEVS, 16, PAIR), AX, 0, 0)
    near_out, dq, own, prev, place = near(
        place, neighbour_blocks, q, kv, prev_tokens, wk, wv, cot, run, runt, lin_scale
    )
    nxt = lax.ppermute(prev, AX, [(i + 1, i) for i in range(DEVS - 1)])
    states = scan(place, got)
    tokt, _ = flip(place, own_tokens)
    around = [lax.ppermute(tokt, "x", [(i, (i + d) % 4) for i in range(4)]) for d in (1, 2, 3)]
    states = lax.all_to_all(states.reshape(DEVS, 8, PAIR), AX, 0, 0)
    states = states.reshape(2, width // PAIR, DH, PAIR)
    layer, delta = join(near_out, dq, own, nxt, q, kv, cot, runt, states, lin_scale)

    delta8 = lax.all_to_all(delta, NEAR8, 0, 0)
    mine = stack([tokt, *around], delta)
    theirs = lax.ppermute(mine, "c", swap)
    tokens_grad, later_core = back(core, delta, wq, wk, wv)
    partial = outer(later_core, at_x, mine, theirs, delta8)
    parts = lax.all_to_all(partial.reshape(16, width // 16, 3 * PAIR), FAR16, 0, 0)
    grad_norm = 1.0 / math.sqrt(rows * DEVS)
    piece = (jnp.sum(parts.astype(F32), axis=0) * grad_norm).astype(BF)
    at_z = lax.axis_index("z").astype(jnp.int32).reshape(1)
    gq, gk, gv = gather_tiles(piece, (core, at_x, at_z), width)
    return layer, tokens_grad, gq, gk, gv


def solution(mesh):
    chips = Mesh(mesh.devices.reshape(2, 2, 4, 4, 2), AX)
    tok = P(AX, None)
    return jax.shard_map(
        shards,
        mesh=chips,
        in_specs=(tok, P(), P(), P(), P(None, AX), tok, tok),
        out_specs=(tok, tok, P(), P(), P()),
        check_vma=False,
    )
```

```python
import functools
import math

import jax
import jax.numpy as jnp
from jax import lax
from jax.experimental import pallas as pl
from jax.experimental.pallas import tpu as pltpu
from jax.sharding import Mesh
from jax.sharding import PartitionSpec as P

BF = jnp.bfloat16
F32 = jnp.float32
AX = ("yl", "c", "x", "z", "yh")
NEAR8 = ("c", "x")
FAR16 = ("yl", "z", "yh")
PLANE = ("x", "yl", "z", "yh")
SEG = 128
PAIR = 128
DH = 64
DEVS = 128
VMEM = pltpu.VMEM
HIGH = lax.Precision.HIGHEST


def dot(a, b, ca, cb, precision=None):
    return lax.dot_general(
        a, b, (((ca,), (cb,)), ((), ())), precision=precision, preferred_element_type=F32
    )


def iota(shape, axis):
    return lax.broadcasted_iota(jnp.int32, shape, axis)


def params(mib):
    return pltpu.CompilerParams(vmem_limit_bytes=mib << 20)


def cost(flops, moved, trans=0):
    return pl.CostEstimate(flops=flops, bytes_accessed=moved, transcendentals=trans)


CHUNK = 256
WIDE = 512


def pair_lanes(columns, pair):
    shape = (columns.shape[0], PAIR)
    return jnp.where(
        iota(shape, 1) < DH,
        columns[:, 2 * pair : 2 * pair + 1],
        columns[:, 2 * pair + 1 : 2 * pair + 2],
    )


def project_kernel(lin_scale, tok, wq, wk, wv, decay, cot, q_out, kv_out, run_out, runt_out, msg, tok_out, held, sems):
    width = tok.shape[1]
    wide = held.shape[3]
    copies = []
    for step in range(width // wide):
        for part, w in enumerate((wq, wk, wv)):
            copy = pltpu.make_async_copy(
                w.at[:, pl.ds(step * wide, wide)], held.at[part, step], sems.at[part, step]
            )
            copy.start()
            copies.append(copy)
    x = tok[...]
    tok_out[...] = x
    ld = decay[...]
    lower = (iota((SEG, SEG), 0) >= iota((SEG, SEG), 1)).astype(F32)
    runt = dot(lower, ld, 1, 1, HIGH)
    run = dot(ld, lower, 1, 1, HIGH)
    group = ld.shape[0] // run_out.shape[0]
    for step in range(run_out.shape[0]):
        runt_out[step] = runt[:, step * group : (step + 1) * group]
        run_out[step] = run[step * group : (step + 1) * group, :]
    rows = iota((8, PAIR), 0)
    first = iota((DH, PAIR), 1) < DH
    for step in range(width // wide):
        for part in range(3):
            copies[step * 3 + part].wait()
        at = slice(step * wide, (step + 1) * wide)
        q = dot(x, held[0, step], 1, 0).astype(BF)
        k = dot(x, held[1, step], 1, 0).astype(BF)
        v = dot(x, held[2, step], 1, 0).astype(BF)
        q_out[:, at] = q
        kv_out[0, :, at] = k
        kv_out[1, :, at] = v
        here = []
        for part in range(wide // PAIR):
            cols = slice(part * PAIR, (part + 1) * PAIR)
            pair = step * (wide // PAIR) + part
            lanes = pair_lanes(runt, pair)
            total = lanes[SEG - 1 : SEG, :]
            g = cot[:, pair * PAIR : (pair + 1) * PAIR].astype(F32)
            weighted = (v[:, cols].astype(F32) * jnp.exp(total - lanes)).astype(BF)
            scaled = (g * jnp.exp(lanes)).astype(BF)
            states = (
                dot(k[:, cols], weighted, 0, 0),
                dot(q[:, cols], scaled, 0, 0) * lin_scale,
            )
            here.append((pair, total, states))
        for pair, total, states in here:
            high = total.astype(BF).astype(F32)
            mid = (total - high).astype(BF).astype(F32)
            low = total - high - mid
            tail = jnp.where(
                rows == 0, high, jnp.where(rows == 1, mid, jnp.where(rows == 2, low, 0.0))
            )
            tail = jnp.broadcast_to(tail[None], (8, 8, PAIR))
            for part, full in enumerate(states):
                own = jnp.where(first, full[:DH], full[DH:]).reshape(8, 8, PAIR)
                sent = jnp.concatenate([own, tail], axis=1).reshape(PAIR, PAIR)
                msg[part, pair * PAIR : (pair + 1) * PAIR, :] = sent.astype(BF)


def project(tokens, wq, wk, wv, log_decay, cot, lin_scale):
    rows, width = tokens.shape
    heads = log_decay.shape[0]
    chunks = width // CHUNK
    wide = WIDE
    vmem = pl.BlockSpec(memory_space=VMEM)
    hbm = pl.BlockSpec(memory_space=pltpu.HBM)
    return pl.pallas_call(
        functools.partial(project_kernel, lin_scale),
        in_specs=[vmem, hbm, hbm, hbm, vmem, vmem],
        out_specs=[vmem] * 6,
        out_shape=[
            jax.ShapeDtypeStruct((rows, width), BF),
            jax.ShapeDtypeStruct((2, rows, width), BF),
            jax.ShapeDtypeStruct((chunks, heads // chunks, rows), F32),
            jax.ShapeDtypeStruct((chunks, rows, heads // chunks), F32),
            jax.ShapeDtypeStruct((2, width, PAIR), BF),
            jax.ShapeDtypeStruct((rows, width), BF),
        ],
        scratch_shapes=[
            VMEM((3, width // wide, width, wide), BF),
            pltpu.SemaphoreType.DMA((3, width // wide)),
        ],
        compiler_params=params(58),
        cost_estimate=cost(6 * rows * width * width, 6 * width * width + 12 * rows * width),
        name="project",
    )(tokens, wq, wk, wv, log_decay, cot)


def flip_kernel(tag, tok, out, tag_out):
    tag_out[0] = tag[0]
    out[...] = tok[...].T


def flip(tag, tokens):
    rows, width = tokens.shape
    whole = pl.BlockSpec(memory_space=VMEM)
    smem = pl.BlockSpec(memory_space=pltpu.SMEM)
    return pl.pallas_call(
        flip_kernel,
        in_specs=[smem, whole],
        out_specs=[whole, smem],
        out_shape=[
            jax.ShapeDtypeStruct((width, rows), BF),
            jax.ShapeDtypeStruct((1,), jnp.int32),
        ],
        compiler_params=params(16),
        cost_estimate=cost(0, 4 * rows * width),
        name="flip",
    )(tag, tokens)


def stack_kernel(*refs):
    out = refs[-1]
    for i in range(out.shape[0]):
        out[i] = refs[i][...]


def stack(parts, after):
    shape = parts[0].shape
    whole = pl.BlockSpec(memory_space=VMEM)
    return pl.pallas_call(
        stack_kernel,
        in_specs=[whole] * len(parts) + [pl.BlockSpec(memory_space=pl.ANY)],
        out_specs=whole,
        out_shape=jax.ShapeDtypeStruct((len(parts), *shape), BF),
        compiler_params=params(16),
        cost_estimate=cost(0, 4 * len(parts) * math.prod(shape)),
        name="stack",
    )(*parts, after)


def scan_kernel(place, got, out, xs, decays, states):
    both = got[...].astype(F32)
    xs[...] = both[:, :8, :]
    total = both[:, 8:9, :] + both[:, 9:10, :] + both[:, 10:11, :]
    decays[...] = jnp.broadcast_to(jnp.exp(total), decays.shape)
    backward = place[0] >= DEVS // 2

    def one(i, state):
        at = jnp.where(backward, DEVS - 1 - i, i)
        states[at] = state
        return decays[at] * state + xs[at]

    lax.fori_loop(0, DEVS, one, jnp.zeros((8, PAIR), F32), unroll=8)
    out[...] = states[...].reshape(DEVS * 8, PAIR).astype(BF)


def scan(place, got):
    whole = pl.BlockSpec(memory_space=VMEM)
    return pl.pallas_call(
        scan_kernel,
        in_specs=[pl.BlockSpec(memory_space=pltpu.SMEM), whole],
        out_specs=whole,
        out_shape=jax.ShapeDtypeStruct((DEVS * 8, PAIR), BF),
        scratch_shapes=[VMEM((DEVS, 8, PAIR), F32)] * 3,
        compiler_params=params(24),
        cost_estimate=cost(2 * DEVS * 8 * PAIR, 4 * DEVS * 16 * PAIR),
        name="scan",
    )(place, got)


def near_kernel(lin_scale, place, blocks, q_ref, kv, ptok, wk, wv, cot, run, runt, out, dq_out, own, prev, tag_out):
    tag_out[0] = place[0]
    soft_scale = 1.0 / math.sqrt(DH)
    n_own = jnp.int32(0)
    n_prev = jnp.int32(0)
    for j in range(blocks.shape[1]):
        n_own += (blocks[0, j] == place[0]).astype(jnp.int32)
        n_prev += (blocks[0, j] == place[0] - 1).astype(jnp.int32)
    is_own = iota((1, 2 * SEG), 1) < SEG
    times = jnp.where(is_own, n_own, n_prev)
    bias = jnp.where(times > 0, 0.0, -1e30)
    times = times.astype(F32)
    head_of = iota((SEG, PAIR), 1) // DH
    head_of2 = iota((2 * SEG, PAIR), 1) // DH
    lower = iota((SEG, SEG), 0) >= iota((SEG, SEG), 1)
    zero = jnp.zeros((), BF)
    pk = dot(ptok[...], wk[...], 1, 0).astype(BF)
    pv = dot(ptok[...], wv[...], 1, 0).astype(BF)
    pairs = q_ref.shape[1] // PAIR
    work = []
    for pair in range(pairs):
        at = slice(pair * PAIR, (pair + 1) * PAIR)
        q = q_ref[:, at]
        g = cot[:, at]
        kk = jnp.concatenate([kv[0, :, at], pk[:, at]], axis=0)
        vv = jnp.concatenate([kv[1, :, at], pv[:, at]], axis=0)
        for i in range(2):
            mine = head_of == i
            work.append(
                (
                    dot(jnp.where(mine, q, zero), kk, 1, 1),
                    dot(jnp.where(mine, g, zero), vv, 1, 1),
                )
            )
    mats = []
    for head in range(2 * pairs):
        scores, pgrad = work[head]
        col = runt[0, :, head : head + 1]
        row = run[0, head : head + 1, :]
        dec = jnp.where(lower, jnp.exp(jnp.minimum(col - row, 0.0)), 0.0) * lin_scale
        logits = scores * soft_scale + bias
        peak = jnp.max(logits, axis=1, keepdims=True)
        terms = jnp.exp(logits - peak) * times
        probs = terms * (1.0 / jnp.sum(terms, axis=1, keepdims=True))
        inner = jnp.sum(probs * pgrad, axis=1, keepdims=True)
        dlog = probs * (pgrad - inner) * soft_scale
        a = jnp.concatenate([probs[:, :SEG] + scores[:, :SEG] * dec, probs[:, SEG:]], axis=1)
        b = jnp.concatenate([dlog[:, :SEG] + pgrad[:, :SEG] * dec, dlog[:, SEG:]], axis=1)
        mats.append((a.astype(BF), b.astype(BF)))
    for pair in range(pairs):
        at = slice(pair * PAIR, (pair + 1) * PAIR)
        q = q_ref[:, at]
        g = cot[:, at]
        kk = jnp.concatenate([kv[0, :, at], pk[:, at]], axis=0)
        vv = jnp.concatenate([kv[1, :, at], pv[:, at]], axis=0)
        qt = q.T
        gt = g.T
        res = []
        for i in range(2):
            a, b = mats[2 * pair + i]
            half = slice(i * DH, (i + 1) * DH)
            res.append((dot(a, vv, 1, 0), dot(b, kk, 1, 0), dot(qt[half], b, 1, 0), dot(gt[half], a, 1, 0)))
        out[:, at] = jnp.where(head_of == 0, res[0][0], res[1][0])
        dq_out[:, at] = jnp.where(head_of == 0, res[0][1], res[1][1])
        for part in range(2):
            sums = jnp.concatenate([res[0][2 + part], res[1][2 + part]], axis=0).T
            own[part, :, at] = sums[:SEG]
            prev[part, :, at] = sums[SEG:].astype(BF)


def near(place, blocks, q, kv, prev_tokens, wk, wv, cot, run, runt, lin_scale):
    rows, width = q.shape
    heads = run.shape[1]
    smem = pl.BlockSpec(memory_space=pltpu.SMEM)
    col = pl.BlockSpec((rows, CHUNK), lambda i: (0, i))
    two = pl.BlockSpec((2, rows, CHUNK), lambda i: (0, 0, i))
    weight = pl.BlockSpec((width, CHUNK), lambda i: (0, i))
    return pl.pallas_call(
        functools.partial(near_kernel, lin_scale),
        grid=(width // CHUNK,),
        in_specs=[
            smem,
            smem,
            col,
            two,
            pl.BlockSpec((rows, width), lambda i: (0, 0)),
            weight,
            weight,
            col,
            pl.BlockSpec((1, heads, rows), lambda i: (i, 0, 0)),
            pl.BlockSpec((1, rows, heads), lambda i: (i, 0, 0)),
        ],
        out_specs=[col, col, two, two, smem],
        out_shape=[
            jax.ShapeDtypeStruct((rows, width), F32),
            jax.ShapeDtypeStruct((rows, width), F32),
            jax.ShapeDtypeStruct((2, rows, width), F32),
            jax.ShapeDtypeStruct((2, rows, width), BF),
            jax.ShapeDtypeStruct((1,), jnp.int32),
        ],
        compiler_params=params(58),
        cost_estimate=cost(4000 * 1000 * 1000, 16 * 1000 * 1000, 1000 * 1000),
        name="near",
    )(place, blocks, q, kv, prev_tokens, wk, wv, cot, run, runt)


def join_kernel(lin_scale, near_out, dq_in, own, nxt, q, kv, cot, runt, states, layer, delta):
    head_of = iota((SEG, PAIR), 1) // DH
    diag = iota((PAIR, PAIR), 0) // DH == iota((PAIR, PAIR), 1) // DH
    zero = jnp.zeros((), BF)
    pairs = q.shape[1] // PAIR
    work = []
    for pair in range(pairs):
        at = slice(pair * PAIR, (pair + 1) * PAIR)
        before, after = (
            jnp.where(diag, jnp.concatenate([states[part, pair]] * 2, axis=0), zero)
            for part in range(2)
        )
        work.append(
            (
                dot(q[:, at], before, 1, 0),
                dot(cot[:, at], before, 1, 1),
                dot(kv[1, :, at], after, 1, 1),
                dot(kv[0, :, at], after, 1, 0),
            )
        )
    for pair in range(pairs):
        at = slice(pair * PAIR, (pair + 1) * PAIR)
        run = jnp.where(
            head_of == 0,
            runt[pair // 2, :, 2 * (pair % 2) : 2 * (pair % 2) + 1],
            runt[pair // 2, :, 2 * (pair % 2) + 1 : 2 * (pair % 2) + 2],
        )
        growth = jnp.exp(run) * lin_scale
        fading = jnp.exp(run[SEG - 1 : SEG, :] - run)
        from_q, from_g, from_v, from_k = work[pair]
        layer[:, at] = (near_out[:, at] + growth * from_q).astype(BF)
        dq = dq_in[:, at] + growth * from_g
        dk = own[0, :, at] + fading * from_v + nxt[0, :, at].astype(F32)
        dv = own[1, :, at] + fading * from_k + nxt[1, :, at].astype(F32)
        delta[pair, :, :PAIR] = dq.astype(BF)
        delta[pair, :, PAIR : 2 * PAIR] = dk.astype(BF)
        delta[pair, :, 2 * PAIR :] = dv.astype(BF)


def join(near_out, dq, own, nxt, q, kv, cot, runt, states, lin_scale):
    rows, width = q.shape
    pairs = width // PAIR
    wide = 2 * CHUNK
    col = pl.BlockSpec((rows, wide), lambda i: (0, i))
    two = pl.BlockSpec((2, rows, wide), lambda i: (0, 0, i))
    return pl.pallas_call(
        functools.partial(join_kernel, lin_scale),
        grid=(width // wide,),
        in_specs=[
            col,
            col,
            two,
            two,
            col,
            two,
            col,
            pl.BlockSpec((2, rows, runt.shape[2]), lambda i: (i, 0, 0)),
            pl.BlockSpec((2, wide // PAIR, DH, PAIR), lambda i: (0, i, 0, 0)),
        ],
        out_specs=[col, pl.BlockSpec((wide // PAIR, rows, 3 * PAIR), lambda i: (i, 0, 0))],
        out_shape=[
            jax.ShapeDtypeStruct((rows, width), BF),
            jax.ShapeDtypeStruct((pairs, rows, 3 * PAIR), BF),
        ],
        compiler_params=params(58),
        cost_estimate=cost(8 * rows * PAIR * PAIR * pairs, 24 * rows * width),
        name="join",
    )(near_out, dq, own, nxt, q, kv, cot, runt, states)


def back_kernel(tag, delta, wq, wk, wv, out, tag_out, total):
    step = pl.program_id(0)
    tag_out[0] = tag[0]

    @pl.when(step == 0)
    def _():
        total[...] = jnp.zeros_like(total)

    acc = total[...]
    for part, w in enumerate((wq, wk, wv)):
        for half in range(2):
            acc += dot(
                delta[half, :, part * PAIR : (part + 1) * PAIR],
                w[:, half * PAIR : (half + 1) * PAIR],
                1,
                1,
            )
    total[...] = acc

    @pl.when(step == pl.num_programs(0) - 1)
    def _():
        out[...] = acc.astype(BF)


def back(tag, delta, wq, wk, wv):
    pairs, rows, _ = delta.shape
    width = wq.shape[0]
    smem = pl.BlockSpec(memory_space=pltpu.SMEM)
    weight = pl.BlockSpec((width, 2 * PAIR), lambda i: (0, i))
    return pl.pallas_call(
        back_kernel,
        grid=(pairs // 2,),
        in_specs=[smem, pl.BlockSpec((2, rows, 3 * PAIR), lambda i: (i, 0, 0)), weight, weight, weight],
        out_specs=[
            pl.BlockSpec((rows, width), lambda i: (0, 0)),
            smem,
        ],
        out_shape=[
            jax.ShapeDtypeStruct((rows, width), BF),
            jax.ShapeDtypeStruct((1,), jnp.int32),
        ],
        scratch_shapes=[VMEM((rows, width), F32)],
        compiler_params=params(58),
        cost_estimate=cost(6 * rows * width * width, 6 * width * width + 8 * rows * width),
        name="back",
    )(tag, delta, wq, wk, wv)


def outer_kernel(core, at_x, mine, theirs, delta, out):
    near_x = mine.shape[0]
    left, right = [], []
    for tokt, c in ((mine, core[0]), (theirs, 1 - core[0])):
        for i in range(near_x):
            left.append(tokt[i])
            right.append(delta[c * near_x + lax.rem(at_x[0] + near_x - i, near_x)])
    left = jnp.concatenate(left, axis=1)
    out[...] = dot(left, jnp.concatenate(right, axis=0), 1, 0).astype(BF)


def outer(core, at_x, mine, theirs, delta):
    near_count, rows, cols = delta.shape
    width = mine.shape[1]
    smem = pl.BlockSpec(memory_space=pltpu.SMEM)
    tok = pl.BlockSpec((near_count // 2, width, rows), lambda i: (0, i, 0))
    return pl.pallas_call(
        outer_kernel,
        grid=(1,),
        in_specs=[
            smem,
            smem,
            tok,
            tok,
            pl.BlockSpec((near_count, rows, cols), lambda i: (0, 0, 0)),
        ],
        out_specs=pl.BlockSpec((width, cols), lambda i: (i, 0)),
        out_shape=jax.ShapeDtypeStruct((width, cols), BF),
        compiler_params=params(20),
        cost_estimate=cost(
            2 * near_count * rows * cols * width, 2 * near_count * rows * (width + cols)
        ),
        name="outer",
    )(core, at_x, mine, theirs, delta)


def device(yl, c, x, z, yh):
    return (((yl * 2 + c) * 4 + x) * 4 + z) * 2 + yh


def gather_groups():
    zero = [
        [device(yl, 0, x, z, yh) for yl in range(2) for z in range(4) for yh in range(2)]
        for x in range(4)
    ]
    one = [
        [device(yl, 1, x, z, yh) for x in range(4) for yl in range(2) for yh in range(2)]
        for z in range(4)
    ]
    return zero + one


def ring(array, by):
    route = []
    for yl in range(2):
        for x in range(4):
            for z in range(4):
                for yh in range(2):
                    route.append((device(yl, 0, x, z, yh), device(yl, 0, (x + by) % 4, z, yh)))
                    route.append((device(yl, 1, x, z, yh), device(yl, 1, x, (z + by) % 4, yh)))
    return lax.ppermute(array, AX, route)


def place_kernel(pieces, count, side, at_x, at_z, *refs):
    grads, mark, sems = refs[-5:-2], refs[-2], refs[-1]
    mark[...] = jnp.zeros_like(mark)

    def put(rank):
        copies = []

        def start(src, dst):
            copy = pltpu.make_async_copy(src, dst, sems.at[len(copies)])
            copy.start()
            copies.append(copy)

        for n in range(count):
            source = refs[n]
            by_row = rank[n]
            for place, by in enumerate(pieces):
                x = lax.rem(at_x[0] + by + 4, 4)
                z = lax.rem(at_z[0] + by + 4, 4)
                for part, grad in enumerate(grads):
                    lanes = pl.ds(part * PAIR, PAIR)
                    if by_row:
                        for i in range(8):
                            start(
                                source.at[place * 8 + i, :, lanes],
                                grad.at[(i % 2) * 4 + z, :, pl.ds((4 + i // 2) * PAIR, PAIR)],
                            )
                    else:
                        start(
                            source.at[pl.ds(place * 8, 8), :, lanes],
                            grad.at[:, :, pl.ds(pl.multiple_of(x * PAIR, PAIR), PAIR)],
                        )
        for copy in copies:
            copy.wait()

    @pl.when(side[0] == 0)
    def _():
        put((False, True))

    @pl.when(side[0] == 1)
    def _():
        put((True, False))


def place_tiles(where, pieces, sources, grads, width):
    hbm = pl.BlockSpec(memory_space=pl.ANY)
    smem = pl.BlockSpec(memory_space=pltpu.SMEM)
    first = 3 + len(sources)
    return pl.pallas_call(
        functools.partial(place_kernel, pieces, len(sources)),
        in_specs=[smem] * 3 + [hbm] * (len(sources) + len(grads)),
        out_specs=[hbm] * 3 + [pl.BlockSpec(memory_space=VMEM)],
        out_shape=[jax.ShapeDtypeStruct((8, width // 8, width), BF)] * 3
        + [jax.ShapeDtypeStruct((8, PAIR), F32)],
        scratch_shapes=[pltpu.SemaphoreType.DMA((24 * len(pieces) * len(sources),))],
        input_output_aliases={first + i: i for i in range(len(grads))},
        compiler_params=params(16),
        cost_estimate=cost(0, 4 * sum(a.size for a in sources)),
        name="place",
    )(*where, *sources, *grads)


def halves_kernel(behind, ahead, after, first, second, both):
    del after
    half = first.shape[0]
    first[...] = behind[:half]
    second[...] = ahead[half:]
    both[: 2 * half] = behind[...]
    both[2 * half :] = ahead[...]


def halves(behind, ahead, after):
    pairs, *rest = behind.shape
    whole = pl.BlockSpec(memory_space=VMEM)
    return pl.pallas_call(
        halves_kernel,
        in_specs=[whole, whole, pl.BlockSpec(memory_space=pl.ANY)],
        out_specs=[whole] * 3,
        out_shape=[jax.ShapeDtypeStruct((n, *rest), BF) for n in (pairs // 2, pairs // 2, 2 * pairs)],
        compiler_params=params(16),
        cost_estimate=cost(0, 12 * behind.size),
        name="halves",
    )(behind, ahead, after)


def gather_tiles(piece, where, width):
    swap = [(0, 1), (1, 0)]

    def swapped(array):
        return lax.ppermute(array, "c", swap)

    rows, cols = piece.shape
    here = lax.all_to_all(
        jnp.broadcast_to(piece[None], (16, rows, cols)), AX, 0, 0, axis_index_groups=gather_groups()
    ).reshape(8, 2 * rows, cols)
    behind = ring(here, 1)
    ahead = ring(here, -1)
    *grads, mark = place_tiles(where, (0,), (here, swapped(here)), (), width)
    half_a, half_b, both = halves(behind, ahead, mark)
    far_a = ring(half_a, 1)
    far_b = ring(half_b, -1)
    *grads, mark = place_tiles(where, (-1, 1), (both, swapped(both)), grads, width)
    far = stack([far_a, far_b], mark).reshape(here.shape)
    far_c = swapped(far)
    *grads, _ = place_tiles(where, (2,), (far,), grads, width)
    core, *rest = where
    *grads, _ = place_tiles((1 - core, *rest), (2,), (far_c,), grads, width)
    return [grad.reshape(width, width) for grad in grads]


def shards(tokens, wq, wk, wv, log_decay, neighbour_blocks, cot):
    rows, width = tokens.shape
    lin_scale = 1.0 / (DH * math.sqrt(rows))
    place = lax.axis_index(AX).astype(jnp.int32).reshape(1)
    core = lax.axis_index("c").astype(jnp.int32).reshape(1)

    at_x = lax.axis_index("x").astype(jnp.int32).reshape(1)
    swap = [(0, 1), (1, 0)]
    q, kv, run, runt, msg, own_tokens = project(tokens, wq, wk, wv, log_decay, cot, lin_scale)
    prev_tokens = lax.ppermute(own_tokens, AX, [(i, i + 1) for i in range(DEVS - 1)])
    got = lax.all_to_all(msg.reshape(DEVS, 16, PAIR), AX, 0, 0)
    near_out, dq, own, prev, place = near(
        place, neighbour_blocks, q, kv, prev_tokens, wk, wv, cot, run, runt, lin_scale
    )
    nxt = lax.ppermute(prev, AX, [(i + 1, i) for i in range(DEVS - 1)])
    states = scan(place, got)
    tokt, _ = flip(place, own_tokens)
    around = [lax.ppermute(tokt, "x", [(i, (i + d) % 4) for i in range(4)]) for d in (1, 2, 3)]
    states = lax.all_to_all(states.reshape(DEVS, 8, PAIR), AX, 0, 0)
    states = states.reshape(2, width // PAIR, DH, PAIR)
    layer, delta = join(near_out, dq, own, nxt, q, kv, cot, runt, states, lin_scale)

    delta8 = lax.all_to_all(delta, NEAR8, 0, 0)
    mine = stack([tokt, *around], delta)
    theirs = lax.ppermute(mine, "c", swap)
    tokens_grad, later_core = back(core, delta, wq, wk, wv)
    partial = outer(later_core, at_x, mine, theirs, delta8)
    parts = lax.all_to_all(partial.reshape(16, width // 16, 3 * PAIR), FAR16, 0, 0)
    grad_norm = 1.0 / math.sqrt(rows * DEVS)
    piece = (jnp.sum(parts.astype(F32), axis=0) * grad_norm).astype(BF)
    at_z = lax.axis_index("z").astype(jnp.int32).reshape(1)
    gq, gk, gv = gather_tiles(piece, (core, at_x, at_z), width)
    return layer, tokens_grad, gq, gk, gv


def solution(mesh):
    chips = Mesh(mesh.devices.reshape(2, 2, 4, 4, 2), AX)
    tok = P(AX, None)
    return jax.shard_map(
        shards,
        mesh=chips,
        in_specs=(tok, P(), P(), P(), P(None, AX), tok, tok),
        out_specs=(tok, tok, P(), P(), P()),
        check_vma=False,
    )
```
